256 devices in a mesh: bx: 8 (over y, core), by: 32 (over z, x).
Axes of the slice: x: 4, y: 4, z: 8, core: 2. Of those that a mesh axis runs over, the one named last changes fastest.
Arguments:
- conserved: float32 [5, 128, 512, 64], P(None, 'bx', 'by'), as said below
- cool_steps: int32 [8, 32, 4], replicated, may hold values from 1 to 8
- swap_slot: int32 [8, 32, 3], replicated, may hold values from 0 to 3
Outputs:
- balanced: float32 [8, 32, 4, 5, 16, 256], P('bx', 'by')
The draws below stay inside these ranges and needn't reach their ends.
Inputs may be any that keep to these rules, and one draw needn't show every extreme that they name: `conserved`: density and the pressure (gamma - 1)(E - |m|^2 / (2 rho)) are positive in every cell.
All inputs are finite; a program needn't handle non-finite values.
Results may differ from the reference program's by a relative error of at most 0.0003.
Values sent between devices are 32-bit elements; how exact they have to be, the bound alone decides.
No kernel may reach another device: no remote copies, remote signals or barrier semaphores. Data moves between devices by JAX's collectives and lax.ppermute only.
A program may use at most 128 MiB of HBM per device.

```python
import jax
import jax.numpy as jnp
from jax import lax

BS = 16
BLK_DEV = 4
ROUNDS = 3
MAXSUB = 8
NX = 128
NY = 512
NZ = 64
N_BX = 8
N_BY = 32


HEAT_RATIO = 5.0 / 3.0


def counts_table(key):
    shape = (N_BX, N_BY, BLK_DEV)
    hot_key, base_key = jax.random.split(key)
    is_hot = jax.random.randint(hot_key, shape, 0, 8) == 0
    base = jax.random.randint(base_key, shape, 1, 4)
    table = jnp.where(is_hot, MAXSUB, base).reshape(-1)
    table = table.at[0].set(MAXSUB).at[1].set(1)
    return table.reshape(shape).astype(jnp.int32)


def draw_cool_steps(key, part):
    counts = counts_table(key)
    key = jax.random.fold_in(key, 1)
    return counts


def draw_swap_slot(key, part):
    table = counts_table(key)
    key = jax.random.fold_in(key, 2)
    slot_ids = jnp.arange(BLK_DEV, dtype=jnp.int32)
    picks = []
    for round_index in range(ROUNDS):
        partner = jnp.bitwise_xor(jnp.arange(N_BY, dtype=jnp.int32), 1 << round_index)
        loads = jnp.sum(table, axis=-1)
        heavier = loads > loads[:, partner]
        chosen = jnp.where(heavier, jnp.argmax(table, axis=-1), jnp.argmin(table, axis=-1)).astype(jnp.int32)
        theirs = chosen[:, partner]
        incoming = jnp.sum(jnp.where(slot_ids == theirs[..., None], table[:, partner, :], 0), axis=-1).astype(jnp.int32)
        table = jnp.where(slot_ids == chosen[..., None], incoming[..., None], table).astype(jnp.int32)
        picks.append(chosen)
    return jnp.stack(picks, axis=-1).astype(jnp.int32)


def wrapped_gap(coord, middle, period):
    gap = jnp.abs(coord - middle)
    return jnp.minimum(gap, period - gap)


def draw_conserved(key, part):
    key = jax.random.fold_in(key, 3)
    keys = jax.random.split(key, 8)
    first = jnp.arange(NX, dtype=jnp.float32)[:, None, None]
    second = jnp.arange(NY, dtype=jnp.float32)[None, :, None]
    third = jnp.arange(NZ, dtype=jnp.float32)[None, None, :]
    radius = 0.6 * BS
    bubble = jnp.zeros((NX, NY, NZ), jnp.float32)
    for index in range(4):
        centre = jax.random.uniform(keys[index], (3,)) * jnp.array([NX, NY, NZ], jnp.float32)
        distance = wrapped_gap(first, centre[0], NX) ** 2 + wrapped_gap(second, centre[1], NY) ** 2 + wrapped_gap(third, centre[2], NZ) ** 2
        bubble = bubble + jnp.exp(-distance / (radius * radius))
    rough_density = jax.random.uniform(keys[4], (NX, NY, NZ), minval=-0.8, maxval=0.8)
    rough_heat = jax.random.uniform(keys[5], (NX, NY, NZ), minval=-0.5, maxval=0.5)
    motion = jnp.clip(0.4 * jax.random.normal(keys[6], (3, NX, NY, NZ)), -1.5, 1.5)
    matter_per_volume = jnp.exp(rough_density) / (1.0 + 4.0 * bubble)
    heat = jnp.exp(rough_heat) * (1.0 + 2.0 * second / NY) * (1.0 + 9.0 * bubble)
    pressure = matter_per_volume * heat
    energy = pressure / (HEAT_RATIO - 1.0) + 0.5 * matter_per_volume * jnp.sum(motion * motion, axis=0)
    return jnp.concatenate([matter_per_volume[None], matter_per_volume * motion, energy[None]], axis=0).astype(jnp.float32)


def setup_inputs(seed: int = 0) -> dict:
    streams_of = jax.random.split(jax.random.key(seed), 4)
    return {
        "conserved": draw_conserved(jax.random.fold_in(streams_of[3], 71), 0),
        "cool_steps": draw_cool_steps(jax.random.fold_in(streams_of[3], 71), 0),
        "swap_slot": draw_swap_slot(jax.random.fold_in(streams_of[3], 71), 0),
    }


HEAT_RATIO = 5.0 / 3.0
COURANT_FACTOR = 0.4
EMISSION_RATE = 100.0

def primitive(state):
    matter_per_volume = state[0]
    velocity = state[1:4] / matter_per_volume
    pressure = (HEAT_RATIO - 1.0) * (state[4] - 0.5 * matter_per_volume * lax.optimization_barrier(jnp.sum(velocity * velocity, axis=0)))
    return jnp.concatenate([matter_per_volume[None], velocity, pressure[None]], axis=0)

def limited_slope(before_jump, after_jump):
    return 0.5 * (jnp.sign(before_jump) + jnp.sign(after_jump)) * jnp.minimum(jnp.abs(before_jump), jnp.abs(after_jump))

def riemann_flux(left_prim, right_prim, normal_row):
    row_ids = jnp.arange(5).reshape((5,) + (1,) * (left_prim.ndim - 1))
    along = row_ids == normal_row
    unit_normal = along.astype(left_prim.dtype)
    unit_energy = (row_ids == 4).astype(left_prim.dtype)

    def side_terms(prim_side):
        matter_per_volume = prim_side[0]
        pressure = prim_side[4]
        normal_speed = prim_side[normal_row]
        sound = jnp.sqrt(HEAT_RATIO * pressure / matter_per_volume)
        energy = pressure / (HEAT_RATIO - 1.0) + 0.5 * matter_per_volume * lax.optimization_barrier(jnp.sum(prim_side[1:4] * prim_side[1:4], axis=0))
        state_side = jnp.concatenate([matter_per_volume[None], matter_per_volume * prim_side[1:4], energy[None]], axis=0)
        flux_side = state_side * normal_speed + pressure * (unit_normal + normal_speed * unit_energy)
        return (matter_per_volume, pressure, normal_speed, sound, energy, state_side, flux_side)
    left_density, left_pressure, left_speed, left_sound, left_energy, left_state, left_flux = side_terms(left_prim)
    right_density, right_pressure, right_speed, right_sound, right_energy, right_state, right_flux = side_terms(right_prim)
    low_wave = jnp.minimum(left_speed - left_sound, right_speed - right_sound)
    high_wave = jnp.maximum(left_speed + left_sound, right_speed + right_sound)
    left_mass = left_density * (low_wave - left_speed)
    right_mass = right_density * (high_wave - right_speed)
    middle = (right_pressure - left_pressure + left_mass * left_speed - right_mass * right_speed) / (left_mass - right_mass)

    def star_state(prim_side, matter_per_volume, pressure, normal_speed, energy, edge_wave, mass):
        inner = jnp.concatenate([jnp.ones_like(matter_per_volume)[None], prim_side[1:4], (energy / matter_per_volume + (middle - normal_speed) * (middle + pressure / mass))[None]], axis=0)
        inner = jnp.where(along, middle, inner)
        return mass / (edge_wave - middle) * inner
    left_star = left_flux + low_wave * (star_state(left_prim, left_density, left_pressure, left_speed, left_energy, low_wave, left_mass) - left_state)
    right_star = right_flux + high_wave * (star_state(right_prim, right_density, right_pressure, right_speed, right_energy, high_wave, right_mass) - right_state)
    return jnp.where(low_wave >= 0.0, left_flux, jnp.where(middle >= 0.0, left_star, jnp.where(high_wave > 0.0, right_star, right_flux)))

def sweep_axis(extended, normal_row):
    length = extended.shape[1]
    primitives = primitive(extended)
    differences = primitives[:, 1:] - primitives[:, :-1]
    slopes = limited_slope(differences[:, :-1], differences[:, 1:])
    left_prim = primitives[:, 1:length - 2] + 0.5 * slopes[:, 0:length - 3]
    right_prim = primitives[:, 2:length - 1] - 0.5 * slopes[:, 1:length - 2]
    fluxes = riemann_flux(left_prim, right_prim, normal_row)
    return fluxes[:, 1:] - fluxes[:, :-1]

def fastest_signal(state):
    primitives = primitive(state)
    speeds = lax.optimization_barrier(jnp.sum(jnp.abs(primitives[1:4]), axis=0)) + 3.0 * jnp.sqrt(HEAT_RATIO * primitives[4] / primitives[0])
    return jnp.max(speeds)

def energy_parts(state):
    matter_per_volume = state[..., 0, :, :]
    kinetic = 0.5 * (state[..., 1, :, :] * state[..., 1, :, :] + state[..., 2, :, :] * state[..., 2, :, :] + state[..., 3, :, :] * state[..., 3, :, :]) / matter_per_volume
    specific_thermal_work = state[..., 4, :, :] - kinetic
    return (matter_per_volume, kinetic, specific_thermal_work)

def cool_substep(matter_per_volume, specific_thermal_work, chill_partial_tick):
    thermal_kelvin = (HEAT_RATIO - 1.0) * specific_thermal_work / matter_per_volume
    return specific_thermal_work / (1.0 + chill_partial_tick * matter_per_volume * EMISSION_RATE * jnp.sqrt(1.0 + thermal_kelvin * thermal_kelvin))

def final_sources(swap_slot, block_count):
    row_count = swap_slot.shape[0]
    column_count = swap_slot.shape[1]
    forcing_terms = jnp.arange(row_count * column_count * block_count, dtype=jnp.int32).reshape(row_count, column_count, block_count)
    slot_ids = jnp.arange(block_count, dtype=jnp.int32)
    for round_index in range(swap_slot.shape[2]):
        partner = jnp.bitwise_xor(jnp.arange(column_count, dtype=jnp.int32), 1 << round_index)
        own_slot = swap_slot[:, :, round_index]
        theirs = swap_slot[:, partner, round_index]
        incoming = lax.optimization_barrier(jnp.sum(jnp.where(slot_ids == theirs[..., None], forcing_terms[:, partner, :], 0), axis=-1)).astype(jnp.int32)
        forcing_terms = jnp.where(slot_ids == own_slot[..., None], incoming[..., None], forcing_terms).astype(jnp.int32)
    return forcing_terms

def reference(conserved, cool_steps, swap_slot):
    maxima = lax.map(lambda slab_index: fastest_signal(lax.dynamic_slice_in_dim(conserved, slab_index * BS, BS, 1)), jnp.arange(N_BX, dtype=jnp.int32))
    time_step = COURANT_FACTOR / jnp.max(maxima)
    padded = jnp.pad(conserved, ((0, 0), (2, 2), (2, 2), (0, 0)), mode='wrap')

    def update_column(column_index):
        row_block = column_index // N_BY
        col_block = column_index % N_BY
        zero_index = column_index * 0
        extended = lax.dynamic_slice(padded, (zero_index, row_block * BS, col_block * BS, zero_index), (5, BS + 4, BS + 4, NZ))
        interior = extended[:, 2:BS + 2, 2:BS + 2]
        change_first = sweep_axis(extended[:, :, 2:BS + 2], 1)
        change_second = sweep_axis(extended[:, 2:BS + 2, :].transpose(0, 2, 1, 3), 2).transpose(0, 2, 1, 3)
        along_third = jnp.concatenate([interior[..., NZ - 2:], interior, interior[..., :2]], axis=3).transpose(0, 3, 1, 2)
        change_third = sweep_axis(along_third, 3).transpose(0, 2, 3, 1)
        return interior - time_step * (change_first + change_second + change_third)
    updated = lax.map(update_column, jnp.arange(N_BX * N_BY, dtype=jnp.int32))
    blocks = updated.reshape(N_BX, N_BY, 5, BS, BS, BLK_DEV, BS).transpose(0, 1, 5, 2, 3, 4, 6)
    blocks = blocks.reshape(N_BX, N_BY, BLK_DEV, 5, BS, BS * BS)
    matter_per_volume, kinetic, specific_thermal_work = energy_parts(blocks)
    counts = cool_steps[..., None, None]
    chill_partial_tick = time_step / counts.astype(jnp.float32)
    for sub_index in range(MAXSUB):
        specific_thermal_work = jnp.where(sub_index < counts, cool_substep(matter_per_volume, specific_thermal_work, chill_partial_tick), specific_thermal_work)
    cooled = jnp.concatenate([blocks[..., 0:4, :, :], (kinetic + specific_thermal_work)[..., None, :, :]], axis=3)
    forcing_terms = final_sources(swap_slot, BLK_DEV)
    plain_tile_list = cooled.reshape(N_BX * N_BY * BLK_DEV, 5, BS, BS * BS)
    return jnp.take(plain_tile_list, forcing_terms.reshape(-1), axis=0).reshape(N_BX, N_BY, BLK_DEV, 5, BS, BS * BS)
```

```python
import jax
import jax.numpy as jnp
from jax import lax
from jax.experimental import pallas as pl
from jax.experimental.pallas import tpu as pltpu
from jax.sharding import PartitionSpec as P

HEAT_RATIO = 5.0 / 3.0
COURANT_FACTOR = 0.4
EMISSION_RATE = 100.0
F32 = jnp.float32
TILE = (8, 128)
VMEM = pl.BlockSpec(memory_space=pltpu.VMEM)
SMEM = pl.BlockSpec(memory_space=pltpu.SMEM)


def shape(*dims):
    return jax.ShapeDtypeStruct(dims, F32)


def iota(axis):
    return lax.broadcasted_iota(jnp.int32, TILE, axis)


def half_minmod(a, b):
    return 0.5 * (jnp.maximum(jnp.minimum(a, b), 0.0) + jnp.minimum(jnp.maximum(a, b), 0.0))


def primitive(u):
    inverse = 1.0 / u[0]
    v1, v2, v3 = u[1] * inverse, u[2] * inverse, u[3] * inverse
    p = (HEAT_RATIO - 1.0) * (u[4] - 0.5 * u[0] * (v1 * v1 + v2 * v2 + v3 * v3))
    return [u[0], v1, v2, v3, p], inverse


def hllc(left, right, n):
    rl, ul, pl_ = left[0], left[n], left[4]
    rr, ur, pr = right[0], right[n], right[4]
    cl = jnp.sqrt(HEAT_RATIO * pl_ / rl)
    cr = jnp.sqrt(HEAT_RATIO * pr / rr)
    sl = jnp.minimum(ul - cl, ur - cr)
    sr = jnp.maximum(ul + cl, ur + cr)
    ml = rl * (sl - ul)
    mr = rr * (sr - ur)
    mid = (pr - pl_ + ml * ul - mr * ur) / (ml - mr)
    use_left = (sl >= 0.0) | (mid >= 0.0)
    rho, v1, v2, v3, p = [jnp.where(use_left, a, b) for a, b in zip(left, right)]
    edge = jnp.where(use_left, sl, sr)
    clip = jnp.where(use_left, jnp.minimum(sl, 0.0), jnp.maximum(sr, 0.0))
    v = [None, v1, v2, v3]
    u = v[n]
    energy = p * (1.0 / (HEAT_RATIO - 1.0)) + 0.5 * rho * (v1 * v1 + v2 * v2 + v3 * v3)
    gap = 1.0 / jnp.where(clip == 0.0, 1.0, edge - mid)
    ratio = (edge - u) * gap
    star_rho = rho * ratio
    star_energy = ratio * energy + (mid - u) * (star_rho * mid + p * gap)
    mass = rho * u
    f_rho = mass + clip * (star_rho - rho)
    out = [f_rho, f_rho * v1, f_rho * v2, f_rho * v3, None]
    out[n] = mass * u + p + clip * (star_rho * mid - mass)
    out[4] = (energy + p) * u + clip * (star_energy - energy)
    return out


def prep_kernel(cons, u_out, w_out, e_bx, o_bx, e_by, o_by):
    even_i = lax.axis_index("bx") % 2 == 0
    even_j = lax.axis_index("by") % 2 == 0
    lane = iota(1)
    bit0 = (lane // 16) % 2 == 0
    bit1 = (lane // 32) % 2 == 0
    row = iota(0)
    top = jnp.zeros(TILE, F32)
    for at in range(2):
        edge_pairs = {}
        for h in range(2):
            tiles = []
            for f in range(5):
                x = [cons[f, pl.ds(at * 128 + h * 8 + b, 8, stride=16), :] for b in range(8)]
                if h == 0:
                    edge_pairs.setdefault(0, []).append(jnp.concatenate([x[0], x[1]], axis=1))
                else:
                    edge_pairs.setdefault(1, []).append(jnp.concatenate([x[6], x[7]], axis=1))
                y = [jnp.concatenate([x[k], x[k + 4]], axis=1) for k in range(4)]
                z = [None] * 4
                for k in range(2):
                    z[k] = jnp.where(bit1, y[k], pltpu.roll(y[k + 2], 32, 1))
                    z[k + 2] = jnp.where(bit1, pltpu.roll(y[k], 96, 1), y[k + 2])
                t = [None] * 4
                for k in (0, 2):
                    t[k] = jnp.where(bit0, z[k], pltpu.roll(z[k + 1], 16, 1))
                    t[k + 1] = jnp.where(bit0, pltpu.roll(z[k], 112, 1), z[k + 1])
                tiles.append(t)
                for s in range(4):
                    u_out[s, f, at, h] = t[s]
            for s in range(4):
                w, inverse = primitive([tiles[f][s] for f in range(5)])
                speed = (
                    jnp.abs(w[1])
                    + jnp.abs(w[2])
                    + jnp.abs(w[3])
                    + 3.0 * jnp.sqrt(HEAT_RATIO * w[4] * inverse)
                )
                top = jnp.maximum(top, speed)
                for f in range(5):
                    w_out[s, f, at, h] = w[f]
        low, _ = primitive(edge_pairs[0])
        high, _ = primitive(edge_pairs[1])
        for f in range(5):
            e_by[f * 2 + at] = jnp.where(even_j, high[f], low[f])
            o_by[f * 2 + at] = jnp.where(even_j, low[f], high[f])
    for f in range(5):
        for h in range(2):
            low = jnp.zeros(TILE, F32)
            high = jnp.zeros(TILE, F32)
            for s in range(4):
                here = row // 2 == s
                low = jnp.where(here, pltpu.roll(w_out[s, f, 0, h], 2 * s, 0), low)
                high = jnp.where(here, pltpu.roll(w_out[s, f, 1, h], (2 * s + 2) % 8, 0), high)
            e_bx[f * 2 + h] = jnp.where(even_i, high, low)
            o_bx[f * 2 + h] = jnp.where(even_i, low, high)
    for ref in (e_bx, o_bx, e_by, o_by):
        ref[10] = top


def flux_kernel(
    slots, w, u, se_bx, so_bx, se_by, so_by, re_bx, ro_bx, re_by, ro_by,
    d, send_a, send_b, send_c, top_out,
    flux_a, high_a, halo_a, flux_b, high_b, halo_b, lefts, rights, fluxes,
):
    i, j = lax.axis_index("bx"), lax.axis_index("by")
    even_i, even_j = i % 2 == 0, j % 2 == 0
    row, lane = iota(0), iota(1)

    top = se_bx[10]
    for ref in (re_bx, ro_bx, re_by, ro_by):
        top = jnp.maximum(top, ref[10])
    top = jnp.max(top, axis=0, keepdims=True)
    top_out[...] = jnp.broadcast_to(top[None], top_out.shape)

    def pick(flag, a, b, index):
        return jnp.where(flag, a[index], b[index])

    def edges(near, far, own0, own1):
        left = [n + half_minmod(n - q, a - n) for n, q, a in zip(near, far, own0)]
        right = [a - half_minmod(a - n, b - a) for n, a, b in zip(near, own0, own1)]
        return left, right

    for h in range(2):
        tiles = range(h, 10, 2)
        own_low = [pick(even_i, so_bx, se_bx, t) for t in tiles]
        own_high = [pick(even_i, se_bx, so_bx, t) for t in tiles]
        low = [pick(even_i, ro_bx, re_bx, t) for t in tiles]
        high = [pick(even_i, re_bx, ro_bx, t) for t in tiles]
        back = lambda a: pltpu.roll(a, 1, 0)
        left, right = edges(low, [back(a) for a in low], [back(a) for a in own_low], own_low)
        f_low = hllc(left, right, 1)
        for f in range(5):
            n, q, a = high[f], pltpu.roll(high[f], 7, 0), pltpu.roll(own_high[f], 7, 0)
            flux_a[f, h] = f_low[f]
            high_a[f, h] = n - half_minmod(n - a, q - n)
            halo_a[0, f, h] = low[f]
            halo_a[1, f, h] = n
    for at in range(2):
        tiles = range(at, 10, 2)
        own_low = [pick(even_j, so_by, se_by, t) for t in tiles]
        own_high = [pick(even_j, se_by, so_by, t) for t in tiles]
        low = [pick(even_j, ro_by, re_by, t) for t in tiles]
        high = [pick(even_j, re_by, ro_by, t) for t in tiles]
        swap = lambda a: pltpu.roll(a, 64, 1)
        near = [swap(a) for a in low]
        left, right = edges(near, low, own_low, [swap(a) for a in own_low])
        f_low = hllc(left, right, 2)
        for f in range(5):
            n, q, a = high[f], swap(high[f]), swap(own_high[f])
            flux_b[f, at] = f_low[f]
            high_b[f, at] = n - half_minmod(n - a, q - n)
            halo_b[0, f, at] = near[f]
            halo_b[1, f, at] = n

    def sweep(n, load, low_fill, high_fill, high_state, low_flux, down, up, first, last):
        left, right = [[], []], [[], []]
        for f in range(5):
            a, b = load(f)
            da, db, ua, ub = down(a), down(b), up(a), up(b)
            a_prev = jnp.where(first, low_fill(f), da)
            b_prev = jnp.where(first, da, db)
            a_next = jnp.where(last, ub, ua)
            b_next = jnp.where(last, high_fill(f), ub)
            ha = half_minmod(a - a_prev, a_next - a)
            hb = half_minmod(b - b_prev, b_next - b)
            ra, rb = up(a - ha), up(b - hb)
            left[0].append(a + ha)
            left[1].append(b + hb)
            right[0].append(jnp.where(last, rb, ra))
            right[1].append(jnp.where(last, high_state(f), rb))
        fa = hllc(left[0], right[0], n)
        fb = hllc(left[1], right[1], n)
        out = []
        for f in range(5):
            da, db = down(fa[f]), down(fb[f])
            out.append(
                (
                    fa[f] - jnp.where(first, low_flux(f), da),
                    fb[f] - jnp.where(first, da, db),
                )
            )
        return out

    def along_first(k, _):
        s, h = k // 2, k % 2
        line = lambda ref, *index: jnp.broadcast_to(ref[index], TILE)
        out = sweep(
            1,
            lambda f: (w[s, f, 0, h], w[s, f, 1, h]),
            lambda f: line(halo_a, 0, f, h, pl.ds(2 * s + 1, 1)),
            lambda f: line(halo_a, 1, f, h, pl.ds(2 * s, 1)),
            lambda f: line(high_a, f, h, pl.ds(2 * s, 1)),
            lambda f: line(flux_a, f, h, pl.ds(2 * s + 1, 1)),
            lambda a: pltpu.roll(a, 1, 0),
            lambda a: pltpu.roll(a, 7, 0),
            row == 0,
            row == 7,
        )
        for f in range(5):
            d[s, f, 0, h], d[s, f, 1, h] = out[f]
        return 0

    def along_second(k, _):
        s, at = k // 2, k % 2
        to_low = (128 - 16 * s) % 128
        to_high = 112 - 16 * s
        out = sweep(
            2,
            lambda f: (w[s, f, at, 0], w[s, f, at, 1]),
            lambda f: pltpu.roll(halo_b[0, f, at], to_low, 1),
            lambda f: pltpu.roll(halo_b[1, f, at], to_high, 1),
            lambda f: pltpu.roll(high_b[f, at], to_high, 1),
            lambda f: pltpu.roll(flux_b[f, at], to_low, 1),
            lambda a: pltpu.roll(a, 16, 1),
            lambda a: pltpu.roll(a, 112, 1),
            lane < 16,
            lane >= 112,
        )
        for f in range(5):
            d[s, f, at, 0] += out[f][0]
            d[s, f, at, 1] += out[f][1]
        return 0

    first_c, last_c = lane % 16 == 0, lane % 16 == 15

    def previous(here, before):
        return jnp.where(first_c, pltpu.roll(before, 113, 1), pltpu.roll(here, 1, 1))

    def following(here, after):
        return jnp.where(last_c, pltpu.roll(after, 15, 1), pltpu.roll(here, 127, 1))

    def third_states(k, _):
        s, at = k // 2, k % 2
        before, after = (s + 3) % 4, (s + 1) % 4
        for h in range(2):
            for f in range(5):
                a = w[s, f, at, h]
                slope = half_minmod(
                    a - previous(a, w[before, f, at, h]), following(a, w[after, f, at, h]) - a
                )
                lefts[s, f, at, h] = a + slope
                rights[s, f, at, h] = a - slope
        return 0

    def third_fluxes(k, _):
        s, at = k // 2, k % 2
        after = (s + 1) % 4
        for h in range(2):
            out = hllc(
                [lefts[s, f, at, h] for f in range(5)],
                [following(rights[s, f, at, h], rights[after, f, at, h]) for f in range(5)],
                3,
            )
            for f in range(5):
                fluxes[s, f, at, h] = out[f]
        return 0

    def third_change(k, _):
        s, at = k // 2, k % 2
        before = (s + 3) % 4
        for h in range(2):
            for f in range(5):
                a = fluxes[s, f, at, h]
                d[s, f, at, h] += a - previous(a, fluxes[before, f, at, h])
        return 0

    for body in (along_first, along_second, third_states, third_fluxes, third_change):
        lax.fori_loop(0, 8, body, 0)

    for r, ref in enumerate((send_a, send_b, send_c)):
        slot = slots[i, j, r]
        ref[0] = u[slot]
        ref[1] = d[slot]


def tail_kernel(
    slots, counts, u, d, top, got1, got2, got3, got4, got5, got6, got7, out, energy, factor, tick
):
    i, j = lax.axis_index("bx"), lax.axis_index("by")
    speed = jnp.max(jnp.max(top[...], axis=0), axis=1, keepdims=True)
    step = COURANT_FACTOR / jnp.broadcast_to(speed, TILE)
    sw = lambda m, r: slots[i, j ^ m, r]

    def content(m, slot):
        second = slot == sw(m, 1)
        through = sw(m ^ 2, 1) == sw(m ^ 2, 0)
        first = slot == sw(m, 0)
        mask = jnp.where(second, jnp.where(through, 3, 2), jnp.where(first, 1, 0))
        index = jnp.where(
            second,
            jnp.where(through, sw(m ^ 3, 0), sw(m ^ 2, 1)),
            jnp.where(first, sw(m ^ 1, 0), slot),
        )
        return m ^ mask, index

    most = jnp.int32(0)
    limits = []
    for slot in range(4):
        is_last = sw(0, 2) == slot
        near, near_index = content(0, slot)
        far, far_index = content(4, sw(4, 2))
        mask = jnp.where(is_last, far, near)
        index = jnp.where(is_last, far_index, near_index)
        count = counts[i, j ^ mask, index]
        limits.append(count)
        most = jnp.maximum(most, count)

        def write(u_of, d_of):
            for at in range(2):
                for h in range(2):
                    new = [u_of(f, at, h) - step * d_of(f, at, h) for f in range(5)]
                    rho = new[0]
                    kinetic = 0.5 * (new[1] * new[1] + new[2] * new[2] + new[3] * new[3]) / rho
                    energy[slot, at, h] = new[4] - kinetic
                    factor[slot, at, h] = (HEAT_RATIO - 1.0) / rho
                    tick[slot, at, h] = (step / count.astype(F32)) * rho * EMISSION_RATE
                    new[4] = kinetic
                    for f in range(5):
                        out[slot, f, pl.ds(8 * at, 8), pl.ds(128 * h, 128)] = new[f]

        @pl.when(mask == 0)
        def _():
            write(lambda f, at, h: u[index, f, at, h], lambda f, at, h: d[index, f, at, h])

        for m, ref in enumerate((got1, got2, got3, got4, got5, got6, got7), 1):

            @pl.when(mask == m)
            def _():
                write(lambda f, at, h: ref[0, f, at, h], lambda f, at, h: ref[1, f, at, h])

    def advance(k, _):
        for slot in range(4):
            for at in range(2):
                for h in range(2):
                    now = energy[slot, at, h]
                    heat = now * factor[slot, at, h]
                    new = now / (1.0 + tick[slot, at, h] * jnp.sqrt(1.0 + heat * heat))
                    energy[slot, at, h] = jnp.where(k < limits[slot], new, now)
        return 0

    lax.fori_loop(0, most, advance, 0)
    for slot in range(4):
        for at in range(2):
            for h in range(2):
                place = (slot, 4, pl.ds(8 * at, 8), pl.ds(128 * h, 128))
                out[place] = out[place] + energy[slot, at, h]


def pair_even(count):
    return [(k, k ^ 1) for k in range(count)]


def pair_odd(count):
    return [(k, (k + 1) % count if k % 2 else (k - 1) % count) for k in range(count)]


def on_device(conserved, cool_steps, swap_slot):
    rows, columns = lax.axis_size("bx"), lax.axis_size("by")
    blocks = (4, 5, 2, 2) + TILE
    slab = (11,) + TILE
    u, w, *slabs = pl.pallas_call(
        prep_kernel,
        in_specs=[VMEM],
        out_specs=[VMEM] * 6,
        out_shape=[shape(*blocks)] * 2 + [shape(*slab)] * 4,
    )(conserved.reshape(5, 256, 64))
    e_bx, o_bx, e_by, o_by = slabs
    got_slabs = [
        lax.ppermute(e_bx, "bx", pair_even(rows)),
        lax.ppermute(o_bx, "bx", pair_odd(rows)),
        lax.ppermute(e_by, "by", pair_even(columns)),
        lax.ppermute(o_by, "by", pair_odd(columns)),
    ]
    groups = [
        [i * columns + j for i in range(rows) for j in range(columns) if (i + 2 * j) % 4 == r]
        for r in range(4)
    ]
    size = len(groups[0])
    travel = (2, 5, 2, 2) + TILE
    edge = (5, 2) + TILE
    d, send_a, send_b, send_c, top = pl.pallas_call(
        flux_kernel,
        in_specs=[SMEM] + [VMEM] * 10,
        out_specs=[VMEM] * 5,
        out_shape=[shape(*blocks)] + [shape(*travel)] * 3 + [shape(size, 1, 128)],
        scratch_shapes=[
            pltpu.VMEM(edge, F32),
            pltpu.VMEM(edge, F32),
            pltpu.VMEM((2,) + edge, F32),
            pltpu.VMEM(edge, F32),
            pltpu.VMEM(edge, F32),
            pltpu.VMEM((2,) + edge, F32),
            pltpu.VMEM(blocks, F32),
            pltpu.VMEM(blocks, F32),
            pltpu.VMEM(blocks, F32),
        ],
    )(swap_slot, w, u, *slabs, *got_slabs)
    sends = {1: send_a, 2: send_b, 3: send_a, 4: send_c, 5: send_a, 6: send_b, 7: send_a}
    got = [
        lax.ppermute(sends[m], "by", [(k, k ^ m) for k in range(columns)]) for m in range(1, 8)
    ]
    top = lax.all_to_all(top, ("bx", "by"), 0, 0, axis_index_groups=groups)
    state = (4, 2, 2) + TILE
    result = pl.pallas_call(
        tail_kernel,
        in_specs=[SMEM] * 2 + [VMEM] * 10,
        out_specs=VMEM,
        out_shape=shape(4, 5, 16, 256),
        scratch_shapes=[pltpu.VMEM(state, F32)] * 3,
    )(swap_slot, cool_steps, u, d, top, *got)
    return result.reshape((1, 1) + result.shape)


def solution(mesh):
    in_specs = (P(None, "bx", "by", None), P(), P())
    out_specs = P("bx", "by", None, None, None, None)
    return jax.shard_map(
        on_device, mesh=mesh, in_specs=in_specs, out_specs=out_specs, check_vma=False
    )
```

```python
import jax
import jax.numpy as jnp
from jax import lax
from jax.experimental import pallas as pl
from jax.experimental.pallas import tpu as pltpu
from jax.sharding import PartitionSpec as P

HEAT_RATIO = 5.0 / 3.0
COURANT_FACTOR = 0.4
EMISSION_RATE = 100.0
F32 = jnp.float32
TILE = (8, 128)
BLOCKS = (4, 5, 2, 2) + TILE
TRAVEL = (2, 5, 2, 2) + TILE
VMEM = pl.BlockSpec(memory_space=pltpu.VMEM)
SMEM = pl.BlockSpec(memory_space=pltpu.SMEM)
PARAMS = pltpu.CompilerParams(vmem_limit_bytes=16 * 1024 * 1024)
BIG = 3e38
SMALL = 1e-37


def shape(*dims):
    return jax.ShapeDtypeStruct(dims, F32)


def iota(axis):
    return lax.broadcasted_iota(jnp.int32, TILE, axis)


def invert(x):
    r = pl.reciprocal(x, approx=True)
    return r * (2.0 - x * r)


def root(x):
    x = jnp.maximum(x, SMALL)
    return x * lax.rsqrt(x)


def half_minmod(a, b):
    return 0.5 * (jnp.maximum(jnp.minimum(a, b), 0.0) + jnp.minimum(jnp.maximum(a, b), 0.0))


def primitive(u):
    inverse = invert(u[0])
    v1, v2, v3 = u[1] * inverse, u[2] * inverse, u[3] * inverse
    p = (HEAT_RATIO - 1.0) * (u[4] - 0.5 * u[0] * (v1 * v1 + v2 * v2 + v3 * v3))
    return [u[0], v1, v2, v3, p], inverse


def hllc(left, right, n):
    rl, ul, pl_ = left[0], left[n], left[4]
    rr, ur, pr = right[0], right[n], right[4]
    cl = root(HEAT_RATIO * pl_ * invert(rl))
    cr = root(HEAT_RATIO * pr * invert(rr))
    sl = jnp.minimum(ul - cl, ur - cr)
    sr = jnp.maximum(ul + cl, ur + cr)
    ml = rl * (sl - ul)
    mr = rr * (sr - ur)
    mid = (pr - pl_ + ml * ul - mr * ur) * invert(ml - mr)
    use_left = (sl >= 0.0) | (mid >= 0.0)
    rho, v1, v2, v3, p = [jnp.where(use_left, a, b) for a, b in zip(left, right)]
    edge = jnp.where(use_left, sl, sr)
    clip = jnp.where(use_left, jnp.minimum(sl, 0.0), jnp.maximum(sr, 0.0))
    u = (None, v1, v2, v3)[n]
    energy = p * (1.0 / (HEAT_RATIO - 1.0)) + 0.5 * rho * (v1 * v1 + v2 * v2 + v3 * v3)
    gap = invert(jnp.where(clip == 0.0, 1.0, edge - mid))
    ratio = (edge - u) * gap
    star_rho = rho * ratio
    star_energy = ratio * energy + (mid - u) * (star_rho * mid + p * gap)
    mass = rho * u
    f_rho = mass + clip * (star_rho - rho)
    out = [f_rho, f_rho * v1, f_rho * v2, f_rho * v3, None]
    out[n] = mass * u + p + clip * (star_rho * mid - mass)
    out[4] = (energy + p) * u + clip * (star_energy - energy)
    return out


def prep_kernel(cons, u_out, w_out, e_bx, o_bx, e_by, o_by, in_bx, in_by):
    even_i = lax.axis_index("bx") % 2 == 0
    even_j = lax.axis_index("by") % 2 == 0
    lane = iota(1)
    bit0 = (lane // 16) % 2 == 0
    bit1 = (lane // 32) % 2 == 0
    row = iota(0)
    top = jnp.zeros(TILE, F32)
    for at in range(2):
        low, high, inner = [], [], []
        for h in range(2):
            tiles = []
            for f in range(5):
                x = [cons[f, pl.ds(at * 128 + h * 8 + b, 8, stride=16), :] for b in range(8)]
                if h == 0:
                    low.append(jnp.concatenate([x[0], x[1]], axis=1))
                    inner.append(x[2])
                else:
                    high.append(jnp.concatenate([x[6], x[7]], axis=1))
                    inner[f] = jnp.concatenate([x[5], inner[f]], axis=1)
                y = [jnp.concatenate([x[k], x[k + 4]], axis=1) for k in range(4)]
                z = [None] * 4
                for k in range(2):
                    z[k] = jnp.where(bit1, y[k], pltpu.roll(y[k + 2], 32, 1))
                    z[k + 2] = jnp.where(bit1, pltpu.roll(y[k], 96, 1), y[k + 2])
                t = [None] * 4
                for k in (0, 2):
                    t[k] = jnp.where(bit0, z[k], pltpu.roll(z[k + 1], 16, 1))
                    t[k + 1] = jnp.where(bit0, pltpu.roll(z[k], 112, 1), z[k + 1])
                tiles.append(t)
                for s in range(4):
                    u_out[s, f, at, h] = t[s]
            for s in range(4):
                w, inverse = primitive([tiles[f][s] for f in range(5)])
                speed = (
                    jnp.abs(w[1])
                    + jnp.abs(w[2])
                    + jnp.abs(w[3])
                    + 3.0 * root(HEAT_RATIO * w[4] * inverse)
                )
                top = jnp.maximum(top, speed)
                for f in range(5):
                    w_out[s, f, at, h] = w[f]
        low, _ = primitive(low)
        high, _ = primitive(high)
        inner, _ = primitive(inner)
        for f in range(5):
            e_by[f * 2 + at] = jnp.where(even_j, high[f], low[f])
            o_by[f * 2 + at] = jnp.where(even_j, low[f], high[f])
            in_by[f * 2 + at] = inner[f]
    for f in range(5):
        for h in range(2):
            low = jnp.zeros(TILE, F32)
            high = jnp.zeros(TILE, F32)
            inner = jnp.zeros(TILE, F32)
            for s in range(4):
                here = row // 2 == s
                a, b = w_out[s, f, 0, h], w_out[s, f, 1, h]
                low = jnp.where(here, pltpu.roll(a, 2 * s, 0), low)
                high = jnp.where(here, pltpu.roll(b, (2 * s + 2) % 8, 0), high)
                inner = jnp.where(row == 2 * s, pltpu.roll(b, (2 * s + 3) % 8, 0), inner)
                inner = jnp.where(row == 2 * s + 1, pltpu.roll(a, (2 * s + 7) % 8, 0), inner)
            e_bx[f * 2 + h] = jnp.where(even_i, high, low)
            o_bx[f * 2 + h] = jnp.where(even_i, low, high)
            in_bx[f * 2 + h] = inner
    for ref in (e_bx, o_bx, e_by, o_by):
        ref[10] = top


def inner_kernel(w, d, lefts, rights, fluxes):
    row, lane = iota(0), iota(1)

    def sweep(n, load, down, up, first, last, no_first, no_last):
        left, right = [[], []], [[], []]
        for f in range(5):
            a, b = load(f)
            da, ub = down(a), up(b)
            a_prev, b_prev = da, jnp.where(first, da, down(b))
            a_next, b_next = jnp.where(last, ub, up(a)), ub
            ha = half_minmod(a - a_prev, a_next - a)
            hb = half_minmod(b - b_prev, b_next - b)
            ra, rb = up(a - ha), up(b - hb)
            left[0].append(a + ha)
            left[1].append(b + hb)
            right[0].append(jnp.where(last, rb, ra))
            right[1].append(rb)
        fa = hllc(left[0], right[0], n)
        fb = hllc(left[1], right[1], n)
        out = []
        for f in range(5):
            a = jnp.where(no_first, 0.0, fa[f])
            b = jnp.where(no_last, 0.0, fb[f])
            da = down(a)
            out.append((a - jnp.where(first, 0.0, da), b - jnp.where(first, da, down(b))))
        return out

    def along_first(k, _):
        s, h = k // 2, k % 2
        out = sweep(
            1,
            lambda f: (w[s, f, 0, h], w[s, f, 1, h]),
            lambda a: pltpu.roll(a, 1, 0),
            lambda a: pltpu.roll(a, 7, 0),
            row == 0,
            row == 7,
            row == 0,
            row >= 6,
        )
        for f in range(5):
            d[s, f, 0, h], d[s, f, 1, h] = out[f]
        return 0

    def along_second(k, _):
        s, at = k // 2, k % 2
        out = sweep(
            2,
            lambda f: (w[s, f, at, 0], w[s, f, at, 1]),
            lambda a: pltpu.roll(a, 16, 1),
            lambda a: pltpu.roll(a, 112, 1),
            lane < 16,
            lane >= 112,
            lane < 16,
            lane >= 96,
        )
        for f in range(5):
            d[s, f, at, 0] += out[f][0]
            d[s, f, at, 1] += out[f][1]
        return 0

    first_c, last_c = lane % 16 == 0, lane % 16 == 15

    def previous(here, before):
        return jnp.where(first_c, pltpu.roll(before, 113, 1), pltpu.roll(here, 1, 1))

    def following(here, after):
        return jnp.where(last_c, pltpu.roll(after, 15, 1), pltpu.roll(here, 127, 1))

    def third_states(k, _):
        s, at = k // 2, k % 2
        before, after = (s + 3) % 4, (s + 1) % 4
        for h in range(2):
            for f in range(5):
                a = w[s, f, at, h]
                slope = half_minmod(
                    a - previous(a, w[before, f, at, h]), following(a, w[after, f, at, h]) - a
                )
                lefts[s, f, at, h] = a + slope
                rights[s, f, at, h] = a - slope
        return 0

    def third_fluxes(k, _):
        s, at = k // 2, k % 2
        after = (s + 1) % 4
        for h in range(2):
            out = hllc(
                [lefts[s, f, at, h] for f in range(5)],
                [following(rights[s, f, at, h], rights[after, f, at, h]) for f in range(5)],
                3,
            )
            for f in range(5):
                fluxes[s, f, at, h] = out[f]
        return 0

    def third_change(k, _):
        s, at = k // 2, k % 2
        before = (s + 3) % 4
        for h in range(2):
            for f in range(5):
                a = fluxes[s, f, at, h]
                d[s, f, at, h] += a - previous(a, fluxes[before, f, at, h])
        return 0

    for body in (along_first, along_second, third_states, third_fluxes, third_change):
        lax.fori_loop(0, 8, body, 0, unroll=2)


def edge_kernel(
    slots, u, d_in, se_bx, so_bx, se_by, so_by, in_bx, in_by, re_bx, ro_bx, re_by, ro_by,
    d, send_a, send_b, top_out,
):
    i, j = lax.axis_index("bx"), lax.axis_index("by")
    even_i, even_j = i % 2 == 0, j % 2 == 0
    row, lane = iota(0), iota(1)

    top = se_bx[10]
    for ref in (re_bx, ro_bx, re_by, ro_by):
        top = jnp.maximum(top, ref[10])
    top = jnp.max(top, axis=0, keepdims=True)
    top_out[...] = jnp.broadcast_to(top[None], top_out.shape)

    def faces(n, own_low, own_high, low, high, inner, back, ahead, zero):
        left, right, left2, right2 = [], [], [], []
        for o, q, a, b, w in zip(own_low, own_high, low, high, inner):
            c = jnp.where(zero, ahead(a), back(o))
            left.append(c + half_minmod(c - a, o - c))
            right.append(o - half_minmod(o - c, jnp.where(zero, ahead(o), w) - o))
            e = jnp.where(zero, ahead(q), back(b))
            left2.append(q + half_minmod(q - jnp.where(zero, w, back(q)), e - q))
            right2.append(e - half_minmod(e - q, b - e))
        low_flux = hllc(left, right, n)
        high_flux = hllc(left2, right2, n)
        return (
            [jnp.where(zero, ahead(f) - f, -f) for f in low_flux],
            [jnp.where(zero, f, f - back(f)) for f in high_flux],
        )

    def picked(flag, a, b, index):
        return [jnp.where(flag, a[t], b[t]) for t in range(index, 10, 2)]

    d[...] = d_in[...]
    for h in range(2):
        low, high = faces(
            1,
            picked(even_i, so_bx, se_bx, h),
            picked(even_i, se_bx, so_bx, h),
            picked(even_i, ro_bx, re_bx, h),
            picked(even_i, re_bx, ro_bx, h),
            [in_bx[t] for t in range(h, 10, 2)],
            lambda a: pltpu.roll(a, 1, 0),
            lambda a: pltpu.roll(a, 7, 0),
            row % 2 == 0,
        )
        for f in range(5):
            for s in range(4):
                d[s, f, 0, h] += jnp.where(row < 2, pltpu.roll(low[f], (8 - 2 * s) % 8, 0), 0.0)
                d[s, f, 1, h] += jnp.where(row >= 6, pltpu.roll(high[f], 6 - 2 * s, 0), 0.0)
    for at in range(2):
        turn = lambda a: pltpu.roll(a, 64, 1)
        low, high = faces(
            2,
            picked(even_j, so_by, se_by, at),
            picked(even_j, se_by, so_by, at),
            picked(even_j, ro_by, re_by, at),
            picked(even_j, re_by, ro_by, at),
            [in_by[t] for t in range(at, 10, 2)],
            turn,
            turn,
            lane < 64,
        )
        for f in range(5):
            for s in range(4):
                one = pltpu.roll(low[f], (128 - 16 * s) % 128, 1)
                two = pltpu.roll(low[f], 80 - 16 * s, 1)
                d[s, f, at, 0] += jnp.where(lane < 16, one, jnp.where(lane < 32, two, 0.0))
                one = pltpu.roll(high[f], 96 - 16 * s, 1)
                two = pltpu.roll(high[f], 48 - 16 * s, 1)
                d[s, f, at, 1] += jnp.where(lane >= 112, two, jnp.where(lane >= 96, one, 0.0))

    for r, ref in enumerate((send_a, send_b)):
        slot = slots[r, i, j]
        ref[0] = u[slot]
        ref[1] = d[slot]


def content(slots, i, j, slot):
    sw = lambda m, r: slots[r, i, j ^ m]
    second = slot == sw(0, 1)
    through = sw(2, 1) == sw(2, 0)
    first = slot == sw(0, 0)
    mask = jnp.where(second, jnp.where(through, 3, 2), jnp.where(first, 1, 0))
    index = jnp.where(
        second,
        jnp.where(through, sw(3, 0), sw(2, 1)),
        jnp.where(first, sw(1, 0), slot),
    )
    return mask, index


def relay_kernel(slots, u, d, got1, got2, got3, send):
    i, j = lax.axis_index("bx"), lax.axis_index("by")
    mask, index = content(slots, i, j, slots[2, i, j])

    @pl.when(mask == 0)
    def _():
        send[0] = u[index]
        send[1] = d[index]

    for m, ref in enumerate((got1, got2, got3), 1):

        @pl.when(mask == m)
        def _():
            send[...] = ref[...]


def tail_kernel(
    slots, counts, u, d, top, got1, got2, got3, got4, out, stage, energy, factor, tick
):
    i, j = lax.axis_index("bx"), lax.axis_index("by")
    speed = jnp.max(jnp.max(top[...], axis=0), axis=1, keepdims=True)
    step = COURANT_FACTOR / jnp.broadcast_to(speed, TILE)

    def count_of(slot):
        is_last = slots[2, i, j] == slot
        column = jnp.where(is_last, j ^ 4, j)
        mask, index = content(slots, i, column, jnp.where(is_last, slots[2, i, j ^ 4], slot))
        return jnp.where(is_last, 4, mask), index, counts[i, index, column ^ mask]

    def load(slot, _):
        mask, index, count = count_of(slot)

        @pl.when(mask == 0)
        def _():
            stage[0] = u[index]
            stage[1] = d[index]

        for m, ref in enumerate((got1, got2, got3, got4), 1):

            @pl.when(mask == m)
            def _():
                stage[...] = ref[...]

        chill = step / count.astype(F32)
        for at in range(2):
            for h in range(2):
                new = [stage[0, f, at, h] - step * stage[1, f, at, h] for f in range(5)]
                inverse = invert(new[0])
                squares = new[1] * new[1] + new[2] * new[2] + new[3] * new[3]
                kinetic = 0.5 * squares * inverse
                energy[slot, at, h] = new[4] - kinetic
                factor[slot, at, h] = (HEAT_RATIO - 1.0) * inverse
                tick[slot, at, h] = chill * new[0] * EMISSION_RATE
                new[4] = kinetic
                for f in range(5):
                    out[slot, f, pl.ds(8 * at, 8), pl.ds(128 * h, 128)] = new[f]
        return 0

    lax.fori_loop(0, 4, load, 0)
    limits = [count_of(slot)[2] for slot in range(4)]
    most = jnp.maximum(jnp.maximum(limits[0], limits[1]), jnp.maximum(limits[2], limits[3]))

    def advance(k, _):
        for slot in range(4):
            for at in range(2):
                for h in range(2):
                    now = energy[slot, at, h]
                    heat = now * factor[slot, at, h]
                    loss = tick[slot, at, h] * root(jnp.minimum(1.0 + heat * heat, BIG))
                    new = now * invert(jnp.minimum(1.0 + loss, BIG))
                    energy[slot, at, h] = jnp.where(k < limits[slot], new, now)
        return 0

    lax.fori_loop(0, most, advance, 0)
    for slot in range(4):
        for at in range(2):
            for h in range(2):
                place = (slot, 4, pl.ds(8 * at, 8), pl.ds(128 * h, 128))
                out[place] = out[place] + energy[slot, at, h]


def pair_even(count):
    return [(k, k ^ 1) for k in range(count)]


def pair_odd(count):
    return [(k, (k + 1) % count if k % 2 else (k - 1) % count) for k in range(count)]


def call(kernel, inputs, outputs, scratch=(), smem=0):
    return pl.pallas_call(
        kernel,
        in_specs=[SMEM] * smem + [VMEM] * (len(inputs) - smem),
        out_specs=[VMEM] * len(outputs),
        out_shape=[shape(*dims) for dims in outputs],
        scratch_shapes=[pltpu.VMEM(dims, F32) for dims in scratch],
        compiler_params=PARAMS,
    )(*inputs)


def on_device(conserved, cool_steps, swap_slot):
    rows, columns = lax.axis_size("bx"), lax.axis_size("by")
    slots = swap_slot.transpose(2, 0, 1)
    counts = cool_steps.transpose(0, 2, 1)
    slab = (11,) + TILE
    inner = (10,) + TILE
    u, w, *slabs = call(
        prep_kernel, [conserved.reshape(5, 256, 64)], [BLOCKS] * 2 + [slab] * 4 + [inner] * 2
    )
    e_bx, o_bx, e_by, o_by = slabs[:4]
    got_slabs = [
        lax.ppermute(e_bx, "bx", pair_even(rows)),
        lax.ppermute(o_bx, "bx", pair_odd(rows)),
        lax.ppermute(e_by, "by", pair_even(columns)),
        lax.ppermute(o_by, "by", pair_odd(columns)),
    ]
    (d,) = call(inner_kernel, [w], [BLOCKS], [BLOCKS] * 3)
    groups = [
        [i * columns + j for i in range(rows) for j in range(columns) if (i + 2 * j) % 4 == r]
        for r in range(4)
    ]
    size = len(groups[0])
    d, send_a, send_b, top = call(
        edge_kernel,
        [slots, u, d, *slabs, *got_slabs],
        [BLOCKS] + [TRAVEL] * 2 + [(size, 1, 128)],
        smem=1,
    )
    sends = {1: send_a, 2: send_b, 3: send_a}
    trade = lambda m, block: lax.ppermute(block, "by", [(k, k ^ m) for k in range(columns)])
    got = [trade(m, block) for m, block in sends.items()]
    top = lax.all_to_all(top, ("bx", "by"), 0, 0, axis_index_groups=groups)
    (send_c,) = call(relay_kernel, [slots, u, d, *got], [TRAVEL], smem=1)
    got.append(trade(4, send_c))
    (result,) = call(
        tail_kernel,
        [slots, counts, u, d, top, *got],
        [(4, 5, 16, 256)],
        [TRAVEL] + [(4, 2, 2) + TILE] * 3,
        smem=2,
    )
    return result.reshape((1, 1) + result.shape)


def solution(mesh):
    in_specs = (P(None, "bx", "by", None), P(), P())
    out_specs = P("bx", "by", None, None, None, None)
    return jax.shard_map(
        on_device, mesh=mesh, in_specs=in_specs, out_specs=out_specs, check_vma=False
    )
```

```python
import jax
import jax.numpy as jnp
from jax import lax
from jax.experimental import pallas as pl
from jax.experimental.pallas import tpu as pltpu
from jax.sharding import PartitionSpec as P

HEAT_RATIO = 5.0 / 3.0
COURANT_FACTOR = 0.4
EMISSION_RATE = 100.0
F32 = jnp.float32
TILE = (8, 128)
BLOCKS = (4, 5, 2, 2) + TILE
TRAVEL = (2, 5, 2, 2) + TILE
VMEM = pl.BlockSpec(memory_space=pltpu.VMEM)
SMEM = pl.BlockSpec(memory_space=pltpu.SMEM)
PARAMS = pltpu.CompilerParams(vmem_limit_bytes=16 * 1024 * 1024)
BIG = 3e38
SMALL = 1e-37


def shape(*dims):
    return jax.ShapeDtypeStruct(dims, F32)


def iota(axis):
    return lax.broadcasted_iota(jnp.int32, TILE, axis)


def invert(x):
    r = pl.reciprocal(x, approx=True)
    return r * (2.0 - x * r)


def root(x):
    x = jnp.maximum(x, SMALL)
    return x * lax.rsqrt(x)


def half_minmod(a, b):
    return 0.5 * (jnp.maximum(jnp.minimum(a, b), 0.0) + jnp.minimum(jnp.maximum(a, b), 0.0))


def primitive(u):
    inverse = invert(u[0])
    v1, v2, v3 = u[1] * inverse, u[2] * inverse, u[3] * inverse
    p = (HEAT_RATIO - 1.0) * (u[4] - 0.5 * u[0] * (v1 * v1 + v2 * v2 + v3 * v3))
    return [u[0], v1, v2, v3, p], inverse


def hllc(left, right, n):
    rl, ul, pl_ = left[0], left[n], left[4]
    rr, ur, pr = right[0], right[n], right[4]
    cl = root(HEAT_RATIO * pl_ * invert(rl))
    cr = root(HEAT_RATIO * pr * invert(rr))
    sl = jnp.minimum(ul - cl, ur - cr)
    sr = jnp.maximum(ul + cl, ur + cr)
    ml = rl * (sl - ul)
    mr = rr * (sr - ur)
    mid = (pr - pl_ + ml * ul - mr * ur) * invert(ml - mr)
    use_left = (sl >= 0.0) | (mid >= 0.0)
    rho, v1, v2, v3, p = [jnp.where(use_left, a, b) for a, b in zip(left, right)]
    edge = jnp.where(use_left, sl, sr)
    clip = jnp.where(use_left, jnp.minimum(sl, 0.0), jnp.maximum(sr, 0.0))
    u = (None, v1, v2, v3)[n]
    energy = p * (1.0 / (HEAT_RATIO - 1.0)) + 0.5 * rho * (v1 * v1 + v2 * v2 + v3 * v3)
    gap = invert(jnp.where(clip == 0.0, 1.0, edge - mid))
    ratio = (edge - u) * gap
    star_rho = rho * ratio
    star_energy = ratio * energy + (mid - u) * (star_rho * mid + p * gap)
    mass = rho * u
    f_rho = mass + clip * (star_rho - rho)
    out = [f_rho, f_rho * v1, f_rho * v2, f_rho * v3, None]
    out[n] = mass * u + p + clip * (star_rho * mid - mass)
    out[4] = (energy + p) * u + clip * (star_energy - energy)
    return out


def prep_kernel(cons, u_out, w_out, e_bx, o_bx, e_by, o_by, in_bx, in_by, top_out):
    even_i = lax.axis_index("bx") % 2 == 0
    even_j = lax.axis_index("by") % 2 == 0
    lane = iota(1)
    bit0 = (lane // 16) % 2 == 0
    bit1 = (lane // 32) % 2 == 0
    row = iota(0)
    top = jnp.zeros(TILE, F32)
    for at in range(2):
        low, high, inner = [], [], []
        for h in range(2):
            tiles = []
            for f in range(5):
                x = [cons[f, pl.ds(at * 128 + h * 8 + b, 8, stride=16), :] for b in range(8)]
                if h == 0:
                    low.append(jnp.concatenate([x[0], x[1]], axis=1))
                    inner.append(x[2])
                else:
                    high.append(jnp.concatenate([x[6], x[7]], axis=1))
                    inner[f] = jnp.concatenate([x[5], inner[f]], axis=1)
                y = [jnp.concatenate([x[k], x[k + 4]], axis=1) for k in range(4)]
                z = [None] * 4
                for k in range(2):
                    z[k] = jnp.where(bit1, y[k], pltpu.roll(y[k + 2], 32, 1))
                    z[k + 2] = jnp.where(bit1, pltpu.roll(y[k], 96, 1), y[k + 2])
                t = [None] * 4
                for k in (0, 2):
                    t[k] = jnp.where(bit0, z[k], pltpu.roll(z[k + 1], 16, 1))
                    t[k + 1] = jnp.where(bit0, pltpu.roll(z[k], 112, 1), z[k + 1])
                tiles.append(t)
                for s in range(4):
                    u_out[s, f, at, h] = t[s]
            for s in range(4):
                w, inverse = primitive([tiles[f][s] for f in range(5)])
                speed = (
                    jnp.abs(w[1])
                    + jnp.abs(w[2])
                    + jnp.abs(w[3])
                    + 3.0 * root(HEAT_RATIO * w[4] * inverse)
                )
                top = jnp.maximum(top, speed)
                for f in range(5):
                    w_out[s, f, at, h] = w[f]
        low, _ = primitive(low)
        high, _ = primitive(high)
        inner, _ = primitive(inner)
        for f in range(5):
            e_by[f * 2 + at] = jnp.where(even_j, high[f], low[f])
            o_by[f * 2 + at] = jnp.where(even_j, low[f], high[f])
            in_by[f * 2 + at] = inner[f]
    for f in range(5):
        for h in range(2):
            low = jnp.zeros(TILE, F32)
            high = jnp.zeros(TILE, F32)
            inner = jnp.zeros(TILE, F32)
            for s in range(4):
                here = row // 2 == s
                a, b = w_out[s, f, 0, h], w_out[s, f, 1, h]
                low = jnp.where(here, pltpu.roll(a, 2 * s, 0), low)
                high = jnp.where(here, pltpu.roll(b, (2 * s + 2) % 8, 0), high)
                inner = jnp.where(row == 2 * s, pltpu.roll(b, (2 * s + 3) % 8, 0), inner)
                inner = jnp.where(row == 2 * s + 1, pltpu.roll(a, (2 * s + 7) % 8, 0), inner)
            e_bx[f * 2 + h] = jnp.where(even_i, high, low)
            o_bx[f * 2 + h] = jnp.where(even_i, low, high)
            in_bx[f * 2 + h] = inner
    for ref in (e_by, o_by):
        ref[10] = top
    top_out[...] = top


def inner_kernel(w, d, lefts, rights, fluxes):
    row, lane = iota(0), iota(1)

    def sweep(n, load, down, up, first, last, no_first, no_last):
        left, right = [[], []], [[], []]
        for f in range(5):
            a, b = load(f)
            da, ub = down(a), up(b)
            a_prev, b_prev = da, jnp.where(first, da, down(b))
            a_next, b_next = jnp.where(last, ub, up(a)), ub
            ha = half_minmod(a - a_prev, a_next - a)
            hb = half_minmod(b - b_prev, b_next - b)
            ra, rb = up(a - ha), up(b - hb)
            left[0].append(a + ha)
            left[1].append(b + hb)
            right[0].append(jnp.where(last, rb, ra))
            right[1].append(rb)
        fa = hllc(left[0], right[0], n)
        fb = hllc(left[1], right[1], n)
        out = []
        for f in range(5):
            a = jnp.where(no_first, 0.0, fa[f])
            b = jnp.where(no_last, 0.0, fb[f])
            da = down(a)
            out.append((a - jnp.where(first, 0.0, da), b - jnp.where(first, da, down(b))))
        return out

    def along_first(k, _):
        s, h = k // 2, k % 2
        out = sweep(
            1,
            lambda f: (w[s, f, 0, h], w[s, f, 1, h]),
            lambda a: pltpu.roll(a, 1, 0),
            lambda a: pltpu.roll(a, 7, 0),
            row == 0,
            row == 7,
            row == 0,
            row >= 6,
        )
        for f in range(5):
            d[s, f, 0, h], d[s, f, 1, h] = out[f]
        return 0

    def along_second(k, _):
        s, at = k // 2, k % 2
        out = sweep(
            2,
            lambda f: (w[s, f, at, 0], w[s, f, at, 1]),
            lambda a: pltpu.roll(a, 16, 1),
            lambda a: pltpu.roll(a, 112, 1),
            lane < 16,
            lane >= 112,
            lane < 16,
            lane >= 96,
        )
        for f in range(5):
            d[s, f, at, 0] += out[f][0]
            d[s, f, at, 1] += out[f][1]
        return 0

    first_c, last_c = lane % 16 == 0, lane % 16 == 15

    def previous(here, before):
        return jnp.where(first_c, pltpu.roll(before, 113, 1), pltpu.roll(here, 1, 1))

    def following(here, after):
        return jnp.where(last_c, pltpu.roll(after, 15, 1), pltpu.roll(here, 127, 1))

    def third_states(k, _):
        s, at = k // 2, k % 2
        before, after = (s + 3) % 4, (s + 1) % 4
        for h in range(2):
            for f in range(5):
                a = w[s, f, at, h]
                slope = half_minmod(
                    a - previous(a, w[before, f, at, h]), following(a, w[after, f, at, h]) - a
                )
                lefts[s, f, at, h] = a + slope
                rights[s, f, at, h] = a - slope
        return 0

    def third_fluxes(k, _):
        s, at = k // 2, k % 2
        after = (s + 1) % 4
        for h in range(2):
            out = hllc(
                [lefts[s, f, at, h] for f in range(5)],
                [following(rights[s, f, at, h], rights[after, f, at, h]) for f in range(5)],
                3,
            )
            for f in range(5):
                fluxes[s, f, at, h] = out[f]
        return 0

    def third_change(k, _):
        s, at = k // 2, k % 2
        before = (s + 3) % 4
        for h in range(2):
            for f in range(5):
                a = fluxes[s, f, at, h]
                d[s, f, at, h] += a - previous(a, fluxes[before, f, at, h])
        return 0

    for body in (along_first, along_second, third_states, third_fluxes, third_change):
        lax.fori_loop(0, 8, body, 0, unroll=2)


def edge_kernel(
    slots, u, d_in, se_bx, so_bx, se_by, so_by, in_bx, in_by, top, re_bx, ro_bx, re_by, ro_by, top2,
    d, send_a, send_b, top_out,
):
    i, j = lax.axis_index("bx"), lax.axis_index("by")
    even_i, even_j = i % 2 == 0, j % 2 == 0
    row, lane = iota(0), iota(1)

    top = jnp.maximum(jnp.maximum(top[...], top2[...]), jnp.maximum(re_by[10], ro_by[10]))
    top = jnp.broadcast_to(jnp.max(top, axis=0, keepdims=True), TILE)
    for k in range(top_out.shape[0]):
        top_out[k] = top

    def faces(n, own_low, own_high, low, high, inner, back, ahead, zero):
        left, right, left2, right2 = [], [], [], []
        for o, q, a, b, w in zip(own_low, own_high, low, high, inner):
            c = jnp.where(zero, ahead(a), back(o))
            left.append(c + half_minmod(c - a, o - c))
            right.append(o - half_minmod(o - c, jnp.where(zero, ahead(o), w) - o))
            e = jnp.where(zero, ahead(q), back(b))
            left2.append(q + half_minmod(q - jnp.where(zero, w, back(q)), e - q))
            right2.append(e - half_minmod(e - q, b - e))
        low_flux = hllc(left, right, n)
        high_flux = hllc(left2, right2, n)
        return (
            [jnp.where(zero, ahead(f) - f, -f) for f in low_flux],
            [jnp.where(zero, f, f - back(f)) for f in high_flux],
        )

    def picked(flag, a, b, index):
        return [jnp.where(flag, a[t], b[t]) for t in range(index, 10, 2)]

    d[...] = d_in[...]
    for h in range(2):
        low, high = faces(
            1,
            picked(even_i, so_bx, se_bx, h),
            picked(even_i, se_bx, so_bx, h),
            picked(even_i, ro_bx, re_bx, h),
            picked(even_i, re_bx, ro_bx, h),
            [in_bx[t] for t in range(h, 10, 2)],
            lambda a: pltpu.roll(a, 1, 0),
            lambda a: pltpu.roll(a, 7, 0),
            row % 2 == 0,
        )
        for f in range(5):
            for s in range(4):
                d[s, f, 0, h] += jnp.where(row < 2, pltpu.roll(low[f], (8 - 2 * s) % 8, 0), 0.0)
                d[s, f, 1, h] += jnp.where(row >= 6, pltpu.roll(high[f], 6 - 2 * s, 0), 0.0)
    for at in range(2):
        turn = lambda a: pltpu.roll(a, 64, 1)
        low, high = faces(
            2,
            picked(even_j, so_by, se_by, at),
            picked(even_j, se_by, so_by, at),
            picked(even_j, ro_by, re_by, at),
            picked(even_j, re_by, ro_by, at),
            [in_by[t] for t in range(at, 10, 2)],
            turn,
            turn,
            lane < 64,
        )
        for f in range(5):
            for s in range(4):
                one = pltpu.roll(low[f], (128 - 16 * s) % 128, 1)
                two = pltpu.roll(low[f], 80 - 16 * s, 1)
                d[s, f, at, 0] += jnp.where(lane < 16, one, jnp.where(lane < 32, two, 0.0))
                one = pltpu.roll(high[f], 96 - 16 * s, 1)
                two = pltpu.roll(high[f], 48 - 16 * s, 1)
                d[s, f, at, 1] += jnp.where(lane >= 112, two, jnp.where(lane >= 96, one, 0.0))

    for r, ref in enumerate((send_a, send_b)):
        slot = slots[r, i, j]
        ref[0] = u[slot]
        ref[1] = d[slot]


def content(slots, i, j, slot):
    sw = lambda m, r: slots[r, i, j ^ m]
    second = slot == sw(0, 1)
    through = sw(2, 1) == sw(2, 0)
    first = slot == sw(0, 0)
    mask = jnp.where(second, jnp.where(through, 3, 2), jnp.where(first, 1, 0))
    index = jnp.where(
        second,
        jnp.where(through, sw(3, 0), sw(2, 1)),
        jnp.where(first, sw(1, 0), slot),
    )
    return mask, index


def relay_kernel(slots, u, d, got1, got2, got3, send):
    i, j = lax.axis_index("bx"), lax.axis_index("by")
    mask, index = content(slots, i, j, slots[2, i, j])

    @pl.when(mask == 0)
    def _():
        send[0] = u[index]
        send[1] = d[index]

    for m, ref in enumerate((got1, got2, got3), 1):

        @pl.when(mask == m)
        def _():
            send[...] = ref[...]


def tail_kernel(
    slots, counts, u, d, top, got1, got2, got3, got4, out, stage, energy, factor, tick
):
    i, j = lax.axis_index("bx"), lax.axis_index("by")
    speed = jnp.max(jnp.max(jnp.max(top[...], axis=0), axis=0, keepdims=True), axis=1, keepdims=True)
    step = COURANT_FACTOR / jnp.broadcast_to(speed, TILE)

    def count_of(slot):
        is_last = slots[2, i, j] == slot
        column = jnp.where(is_last, j ^ 4, j)
        mask, index = content(slots, i, column, jnp.where(is_last, slots[2, i, j ^ 4], slot))
        return jnp.where(is_last, 4, mask), index, counts[i, index, column ^ mask]

    def load(slot, _):
        mask, index, count = count_of(slot)

        @pl.when(mask == 0)
        def _():
            stage[0] = u[index]
            stage[1] = d[index]

        for m, ref in enumerate((got1, got2, got3, got4), 1):

            @pl.when(mask == m)
            def _():
                stage[...] = ref[...]

        chill = step / count.astype(F32)
        for at in range(2):
            for h in range(2):
                new = [stage[0, f, at, h] - step * stage[1, f, at, h] for f in range(5)]
                inverse = invert(new[0])
                squares = new[1] * new[1] + new[2] * new[2] + new[3] * new[3]
                kinetic = 0.5 * squares * inverse
                energy[slot, at, h] = new[4] - kinetic
                factor[slot, at, h] = (HEAT_RATIO - 1.0) * inverse
                tick[slot, at, h] = chill * new[0] * EMISSION_RATE
                new[4] = kinetic
                for f in range(5):
                    out[slot, f, pl.ds(8 * at, 8), pl.ds(128 * h, 128)] = new[f]
        return 0

    lax.fori_loop(0, 4, load, 0)
    limits = [count_of(slot)[2] for slot in range(4)]
    most = jnp.maximum(jnp.maximum(limits[0], limits[1]), jnp.maximum(limits[2], limits[3]))

    def advance(k, _):
        for slot in range(4):
            for at in range(2):
                for h in range(2):
                    now = energy[slot, at, h]
                    heat = now * factor[slot, at, h]
                    loss = tick[slot, at, h] * root(jnp.minimum(1.0 + heat * heat, BIG))
                    new = now * invert(jnp.minimum(1.0 + loss, BIG))
                    energy[slot, at, h] = jnp.where(k < limits[slot], new, now)
        return 0

    lax.fori_loop(0, most, advance, 0)
    for slot in range(4):
        for at in range(2):
            for h in range(2):
                place = (slot, 4, pl.ds(8 * at, 8), pl.ds(128 * h, 128))
                out[place] = out[place] + energy[slot, at, h]


def pair_even(count):
    return [(k, k ^ 1) for k in range(count)]


def pair_odd(count):
    return [(k, (k + 1) % count if k % 2 else (k - 1) % count) for k in range(count)]


def call(kernel, inputs, outputs, scratch=(), smem=0):
    return pl.pallas_call(
        kernel,
        in_specs=[SMEM] * smem + [VMEM] * (len(inputs) - smem),
        out_specs=[VMEM] * len(outputs),
        out_shape=[shape(*dims) for dims in outputs],
        scratch_shapes=[pltpu.VMEM(dims, F32) for dims in scratch],
        compiler_params=PARAMS,
    )(*inputs)


def on_device(conserved, cool_steps, swap_slot):
    rows, columns = lax.axis_size("bx"), lax.axis_size("by")
    slots = swap_slot.transpose(2, 0, 1)
    counts = cool_steps.transpose(0, 2, 1)
    slab = (11,) + TILE
    face = (10,) + TILE
    u, w, *slabs = call(
        prep_kernel,
        [conserved.reshape(5, 256, 64)],
        [BLOCKS] * 2 + [face] * 2 + [slab] * 2 + [face] * 2 + [TILE],
    )
    e_bx, o_bx, e_by, o_by = slabs[:4]
    got_slabs = [
        lax.ppermute(e_bx, "bx", pair_even(rows)),
        lax.ppermute(o_bx, "bx", pair_odd(rows)),
        lax.ppermute(e_by, "by", pair_even(columns)),
        lax.ppermute(o_by, "by", pair_odd(columns)),
        lax.ppermute(slabs[-1], "by", [(k, k ^ 2) for k in range(columns)]),
    ]
    (d,) = call(inner_kernel, [w], [BLOCKS], [BLOCKS] * 3)
    groups = [
        [i * columns + j for i in range(rows) for j in range(x, columns, 4)] for x in range(4)
    ]
    size = len(groups[0])
    d, send_a, send_b, top = call(
        edge_kernel,
        [slots, u, d, *slabs, *got_slabs],
        [BLOCKS] + [TRAVEL] * 2 + [(size // 2,) + TILE],
        smem=1,
    )
    sends = {1: send_a, 2: send_b, 3: send_a}
    trade = lambda m, block: lax.ppermute(block, "by", [(k, k ^ m) for k in range(columns)])
    got = [trade(m, block) for m, block in sends.items()]
    top = top.reshape(size, 4, 128)
    top = lax.all_to_all(top, ("bx", "by"), 0, 0, axis_index_groups=groups)
    top = top.reshape((size // 2,) + TILE)
    (send_c,) = call(relay_kernel, [slots, u, d, *got], [TRAVEL], smem=1)
    got.append(trade(4, send_c))
    (result,) = call(
        tail_kernel,
        [slots, counts, u, d, top, *got],
        [(4, 5, 16, 256)],
        [TRAVEL] + [(4, 2, 2) + TILE] * 3,
        smem=2,
    )
    return result.reshape((1, 1) + result.shape)


def solution(mesh):
    in_specs = (P(None, "bx", "by", None), P(), P())
    out_specs = P("bx", "by", None, None, None, None)
    return jax.shard_map(
        on_device, mesh=mesh, in_specs=in_specs, out_specs=out_specs, check_vma=False
    )
```

```python
import jax
import jax.numpy as jnp
from jax import lax
from jax.experimental import pallas as pl
from jax.experimental.pallas import tpu as pltpu
from jax.sharding import PartitionSpec as P

HEAT_RATIO = 5.0 / 3.0
COURANT_FACTOR = 0.4
EMISSION_RATE = 100.0
F32 = jnp.float32
TILE = (8, 128)
BLOCKS = (4, 5, 2, 2) + TILE
TRAVEL = (2, 5, 2, 2) + TILE
VMEM = pl.BlockSpec(memory_space=pltpu.VMEM)
ANY = pl.BlockSpec(memory_space=pl.ANY)
PARAMS = pltpu.CompilerParams(vmem_limit_bytes=16 * 1024 * 1024)
PLAN = jax.ShapeDtypeStruct((16, 128), jnp.int32)
BIG = 3e38
SMALL = 1e-37


def shape(*dims):
    return jax.ShapeDtypeStruct(dims, F32)


def iota(axis):
    return lax.broadcasted_iota(jnp.int32, TILE, axis)


def invert(x):
    return pl.reciprocal(x, approx=True)


def root(x):
    return x * lax.rsqrt(jnp.maximum(x, SMALL))


def half_minmod(a, b):
    return 0.5 * jnp.maximum(jnp.minimum(a, b), jnp.minimum(jnp.maximum(a, b), 0.0))


def primitive(u):
    inverse = invert(u[0])
    v1, v2, v3 = u[1] * inverse, u[2] * inverse, u[3] * inverse
    p = (HEAT_RATIO - 1.0) * (u[4] - 0.5 * u[0] * (v1 * v1 + v2 * v2 + v3 * v3))
    return [u[0], v1, v2, v3, p], inverse


def hllc(left, right, n):
    rl, ul, pl_ = left[0], left[n], left[4]
    rr, ur, pr = right[0], right[n], right[4]
    cl = root(HEAT_RATIO * pl_ * invert(rl))
    cr = root(HEAT_RATIO * pr * invert(rr))
    sl = jnp.minimum(ul - cl, ur - cr)
    sr = jnp.maximum(ul + cl, ur + cr)
    ml = rl * (sl - ul)
    mr = rr * (sr - ur)
    mid = (pr - pl_ + ml * ul - mr * ur) * invert(ml - mr)
    use_left = jnp.maximum(sl, mid) >= 0.0
    rho, v1, v2, v3, p = [jnp.where(use_left, a, b) for a, b in zip(left, right)]
    edge = jnp.where(use_left, sl, sr)
    clip = jnp.where(use_left, jnp.minimum(sl, 0.0), jnp.maximum(sr, 0.0))
    u = (None, v1, v2, v3)[n]
    energy = p * (1.0 / (HEAT_RATIO - 1.0)) + 0.5 * rho * (v1 * v1 + v2 * v2 + v3 * v3)
    gap = invert(jnp.where(clip == 0.0, 1.0, edge - mid))
    ratio = (edge - u) * gap
    star_rho = rho * ratio
    star_energy = ratio * energy + (mid - u) * (star_rho * mid + p * gap)
    mass = rho * u
    f_rho = mass + clip * (star_rho - rho)
    out = [f_rho, f_rho * v1, f_rho * v2, f_rho * v3, None]
    out[n] = mass * u + p + clip * (star_rho * mid - mass)
    out[4] = (energy + p) * u + clip * (star_energy - energy)
    return out


def prep_kernel(
    cons, u_out, w_out, e_bx, o_bx, e_by, o_by, in_bx, in_by, top_out
):
    even_i = lax.axis_index("bx") % 2 == 0
    even_j = lax.axis_index("by") % 2 == 0
    lane = iota(1)
    bit0 = (lane // 16) % 2 == 0
    bit1 = (lane // 32) % 2 == 0
    row = iota(0)
    top = jnp.zeros(TILE, F32)
    for at in range(2):
        low, high, inner = [], [], []
        for h in range(2):
            tiles = []
            for f in range(5):
                x = [cons[f, pl.ds(at * 128 + h * 8 + b, 8, stride=16), :] for b in range(8)]
                if h == 0:
                    low.append(jnp.concatenate([x[0], x[1]], axis=1))
                    inner.append(x[2])
                else:
                    high.append(jnp.concatenate([x[6], x[7]], axis=1))
                    inner[f] = jnp.concatenate([x[5], inner[f]], axis=1)
                y = [jnp.concatenate([x[k], x[k + 4]], axis=1) for k in range(4)]
                z = [None] * 4
                for k in range(2):
                    z[k] = jnp.where(bit1, y[k], pltpu.roll(y[k + 2], 32, 1))
                    z[k + 2] = jnp.where(bit1, pltpu.roll(y[k], 96, 1), y[k + 2])
                t = [None] * 4
                for k in (0, 2):
                    t[k] = jnp.where(bit0, z[k], pltpu.roll(z[k + 1], 16, 1))
                    t[k + 1] = jnp.where(bit0, pltpu.roll(z[k], 112, 1), z[k + 1])
                tiles.append(t)
                for s in range(4):
                    u_out[s, f, at, h] = t[s]
            for s in range(4):
                w, inverse = primitive([tiles[f][s] for f in range(5)])
                speed = (
                    jnp.abs(w[1])
                    + jnp.abs(w[2])
                    + jnp.abs(w[3])
                    + 3.0 * root(HEAT_RATIO * w[4] * inverse)
                )
                top = jnp.maximum(top, speed)
                for f in range(5):
                    w_out[s, f, at, h] = w[f]
        low, _ = primitive(low)
        high, _ = primitive(high)
        inner, _ = primitive(inner)
        for f in range(5):
            e_by[f * 2 + at] = jnp.where(even_j, high[f], low[f])
            o_by[f * 2 + at] = jnp.where(even_j, low[f], high[f])
            in_by[f * 2 + at] = inner[f]
    for f in range(5):
        for h in range(2):
            low = jnp.zeros(TILE, F32)
            high = jnp.zeros(TILE, F32)
            inner = jnp.zeros(TILE, F32)
            for s in range(4):
                here = row // 2 == s
                a, b = w_out[s, f, 0, h], w_out[s, f, 1, h]
                low = jnp.where(here, pltpu.roll(a, 2 * s, 0), low)
                high = jnp.where(here, pltpu.roll(b, (2 * s + 2) % 8, 0), high)
                inner = jnp.where(row == 2 * s, pltpu.roll(b, (2 * s + 3) % 8, 0), inner)
                inner = jnp.where(row == 2 * s + 1, pltpu.roll(a, (2 * s + 7) % 8, 0), inner)
            e_bx[f * 2 + h] = jnp.where(even_i, high, low)
            o_bx[f * 2 + h] = jnp.where(even_i, low, high)
            in_bx[f * 2 + h] = inner
    for ref in (e_by, o_by):
        ref[10] = top
    top_out[...] = top


def make_plan(slots, counts, plan):
    i, j = lax.axis_index("bx"), lax.axis_index("by")
    row = iota(0)
    here = lax.broadcasted_iota(jnp.int32, (8, 32), 1) == jnp.bitwise_xor(
        lax.broadcasted_iota(jnp.int32, (8, 32), 0), j
    )

    def columns(line):
        line = jnp.broadcast_to(line.astype(F32), (8, 32))
        value = jnp.sum(jnp.where(here, line, 0.0), axis=1, keepdims=True)
        return jnp.broadcast_to(value, TILE)

    def across(a, mask):
        for bit in (1, 2, 4):
            if mask & bit:
                a = jnp.where(row & bit == 0, pltpu.roll(a, 8 - bit, 0), pltpu.roll(a, bit, 0))
        return a

    give = [columns(slots[r, pl.ds(i, 1), :]) for r in range(3)]
    loads = [columns(counts[i, pl.ds(k, 1), :]) for k in range(4)]
    through = across(give[1], 2) == across(give[0], 2)
    from_one, from_two, from_three = across(give[0], 1), across(give[1], 2), across(give[0], 3)

    def content(slot):
        second, first = slot == give[1], slot == give[0]
        mask = jnp.where(second, jnp.where(through, 3.0, 2.0), jnp.where(first, 1.0, 0.0))
        index = jnp.where(
            second,
            jnp.where(through, from_three, from_two),
            jnp.where(first, from_one, slot),
        )
        return mask, index

    relay_mask, relay_index = content(give[2])
    entries = [give[0], give[1], relay_mask, relay_index]
    far_mask, far_index = across(relay_mask, 4) + 4.0, across(relay_index, 4)
    for slot in range(4):
        is_last = give[2] == float(slot)
        mask, index = content(jnp.full(TILE, slot, F32))
        source = jnp.where(is_last, far_mask, mask)
        index = jnp.where(is_last, far_index, index)
        source0 = jnp.broadcast_to(source[0:1], TILE)
        index0 = jnp.broadcast_to(index[0:1], TILE)
        count = jnp.zeros(TILE, F32)
        for k in range(4):
            hit = (row.astype(F32) == source0) & (index0 == float(k))
            count += jnp.where(hit, loads[k], 0.0)
        count = jnp.sum(count, axis=0, keepdims=True)
        entries += [jnp.where(is_last, 4.0, mask), index, count]
    for e, value in enumerate(entries):
        plan[pl.ds(e, 1), :] = value[0:1].astype(jnp.int32)


def entry(plan, e):
    return plan[pl.ds(e, 1), :][0, 0]


def inner_kernel(slots, counts, w, d, plan, lefts, rights, fluxes):
    make_plan(slots, counts, plan)
    row, lane = iota(0), iota(1)

    def sweep(n, load, down, up, first, last, no_first, no_last):
        left, right = [[], []], [[], []]
        for f in range(5):
            a, b = load(f)
            da, ub = down(a), up(b)
            a_prev, b_prev = da, jnp.where(first, da, down(b))
            a_next, b_next = jnp.where(last, ub, up(a)), ub
            ha = half_minmod(a - a_prev, a_next - a)
            hb = half_minmod(b - b_prev, b_next - b)
            ra, rb = up(a - ha), up(b - hb)
            left[0].append(a + ha)
            left[1].append(b + hb)
            right[0].append(jnp.where(last, rb, ra))
            right[1].append(rb)
        fa = hllc(left[0], right[0], n)
        fb = hllc(left[1], right[1], n)
        out = []
        for f in range(5):
            a = jnp.where(no_first, 0.0, fa[f])
            b = jnp.where(no_last, 0.0, fb[f])
            da = down(a)
            out.append((a - jnp.where(first, 0.0, da), b - jnp.where(first, da, down(b))))
        return out

    def along_first(k, _):
        s, h = k // 2, k % 2
        out = sweep(
            1,
            lambda f: (w[s, f, 0, h], w[s, f, 1, h]),
            lambda a: pltpu.roll(a, 1, 0),
            lambda a: pltpu.roll(a, 7, 0),
            row == 0,
            row == 7,
            row == 0,
            row >= 6,
        )
        for f in range(5):
            d[s, f, 0, h], d[s, f, 1, h] = out[f]
        return 0

    def along_second(k, _):
        s, at = k // 2, k % 2
        out = sweep(
            2,
            lambda f: (w[s, f, at, 0], w[s, f, at, 1]),
            lambda a: pltpu.roll(a, 16, 1),
            lambda a: pltpu.roll(a, 112, 1),
            lane < 16,
            lane >= 112,
            lane < 16,
            lane >= 96,
        )
        for f in range(5):
            d[s, f, at, 0] += out[f][0]
            d[s, f, at, 1] += out[f][1]
        return 0

    first_c, last_c = lane % 16 == 0, lane % 16 == 15

    def previous(here, before):
        return jnp.where(first_c, pltpu.roll(before, 113, 1), pltpu.roll(here, 1, 1))

    def following(here, after):
        return jnp.where(last_c, pltpu.roll(after, 15, 1), pltpu.roll(here, 127, 1))

    def third_states(k, _):
        s, at = k // 2, k % 2
        before, after = (s + 3) % 4, (s + 1) % 4
        for h in range(2):
            for f in range(5):
                a = w[s, f, at, h]
                slope = half_minmod(
                    a - previous(a, w[before, f, at, h]), following(a, w[after, f, at, h]) - a
                )
                lefts[s, f, at, h] = a + slope
                rights[s, f, at, h] = a - slope
        return 0

    def third_fluxes(k, _):
        s, at = k // 2, k % 2
        after = (s + 1) % 4
        for h in range(2):
            out = hllc(
                [lefts[s, f, at, h] for f in range(5)],
                [following(rights[s, f, at, h], rights[after, f, at, h]) for f in range(5)],
                3,
            )
            for f in range(5):
                fluxes[s, f, at, h] = out[f]
        return 0

    def third_change(k, _):
        s, at = k // 2, k % 2
        before = (s + 3) % 4
        for h in range(2):
            for f in range(5):
                a = fluxes[s, f, at, h]
                d[s, f, at, h] += a - previous(a, fluxes[before, f, at, h])
        return 0

    for body in (along_first, along_second, third_states, third_fluxes, third_change):
        lax.fori_loop(0, 8, body, 0, unroll=4)


def edge_kernel(
    plan, u, d_in, se_bx, so_bx, se_by, so_by, in_bx, in_by, top, re_bx, ro_bx, re_by, ro_by, top2,
    d, send_a, send_b, top_out, spread, sent,
):
    i, j = lax.axis_index("bx"), lax.axis_index("by")
    even_i, even_j = i % 2 == 0, j % 2 == 0
    row, lane = iota(0), iota(1)

    top = jnp.maximum(jnp.maximum(top[...], top2[...]), jnp.maximum(re_by[10], ro_by[10]))
    top = jnp.broadcast_to(jnp.max(top, axis=0, keepdims=True), TILE)
    for k in range(spread.shape[0]):
        spread[k] = top
    copy = pltpu.make_async_copy(spread, top_out, sent)
    copy.start()

    def faces(n, own_low, own_high, low, high, inner, back, ahead, zero):
        left, right, left2, right2 = [], [], [], []
        for o, q, a, b, w in zip(own_low, own_high, low, high, inner):
            c = jnp.where(zero, ahead(a), back(o))
            left.append(c + half_minmod(c - a, o - c))
            right.append(o - half_minmod(o - c, jnp.where(zero, ahead(o), w) - o))
            e = jnp.where(zero, ahead(q), back(b))
            left2.append(q + half_minmod(q - jnp.where(zero, w, back(q)), e - q))
            right2.append(e - half_minmod(e - q, b - e))
        low_flux = hllc(left, right, n)
        high_flux = hllc(left2, right2, n)
        return (
            [jnp.where(zero, ahead(f) - f, -f) for f in low_flux],
            [jnp.where(zero, f, f - back(f)) for f in high_flux],
        )

    def picked(flag, a, b, index):
        return [jnp.where(flag, a[t], b[t]) for t in range(index, 10, 2)]

    d[...] = d_in[...]
    for h in range(2):
        low, high = faces(
            1,
            picked(even_i, so_bx, se_bx, h),
            picked(even_i, se_bx, so_bx, h),
            picked(even_i, ro_bx, re_bx, h),
            picked(even_i, re_bx, ro_bx, h),
            [in_bx[t] for t in range(h, 10, 2)],
            lambda a: pltpu.roll(a, 1, 0),
            lambda a: pltpu.roll(a, 7, 0),
            row % 2 == 0,
        )
        for f in range(5):
            for s in range(4):
                d[s, f, 0, h] += jnp.where(row < 2, pltpu.roll(low[f], (8 - 2 * s) % 8, 0), 0.0)
                d[s, f, 1, h] += jnp.where(row >= 6, pltpu.roll(high[f], 6 - 2 * s, 0), 0.0)
    for at in range(2):
        turn = lambda a: pltpu.roll(a, 64, 1)
        low, high = faces(
            2,
            picked(even_j, so_by, se_by, at),
            picked(even_j, se_by, so_by, at),
            picked(even_j, ro_by, re_by, at),
            picked(even_j, re_by, ro_by, at),
            [in_by[t] for t in range(at, 10, 2)],
            turn,
            turn,
            lane < 64,
        )
        for f in range(5):
            for s in range(4):
                one = pltpu.roll(low[f], (128 - 16 * s) % 128, 1)
                two = pltpu.roll(low[f], 80 - 16 * s, 1)
                d[s, f, at, 0] += jnp.where(lane < 16, one, jnp.where(lane < 32, two, 0.0))
                one = pltpu.roll(high[f], 96 - 16 * s, 1)
                two = pltpu.roll(high[f], 48 - 16 * s, 1)
                d[s, f, at, 1] += jnp.where(lane >= 112, two, jnp.where(lane >= 96, one, 0.0))

    for r, ref in enumerate((send_a, send_b)):
        slot = entry(plan, r)
        ref[0] = u[slot]
        ref[1] = d[slot]
    copy.wait()


def relay_kernel(plan, u, d, got1, got2, got3, send):
    mask, index = entry(plan, 2), entry(plan, 3)

    @pl.when(mask == 0)
    def _():
        send[0] = u[index]
        send[1] = d[index]

    for m, ref in enumerate((got1, got2, got3), 1):

        @pl.when(mask == m)
        def _():
            send[...] = ref[...]


def tail_kernel(
    plan, u, d, top, got1, got2, got3, got4, result, out, energy, factor, tick, sent, last
):
    speed = jnp.max(jnp.max(top[...], axis=0), axis=0, keepdims=True)
    speed = jnp.max(speed, axis=1, keepdims=True)
    step = COURANT_FACTOR / jnp.broadcast_to(speed, TILE)
    tiles = [(at, h) for at in range(2) for h in range(2)]

    def load(slot, _):
        mask, index, count = [entry(plan, 4 + 3 * slot + k) for k in range(3)]
        chill = step / count.astype(F32)

        def update(u_of, d_of):
            for at, h in tiles:
                new = [u_of(f, at, h) - step * d_of(f, at, h) for f in range(5)]
                inverse = invert(new[0])
                squares = new[1] * new[1] + new[2] * new[2] + new[3] * new[3]
                kinetic = 0.5 * squares * inverse
                energy[slot, at, h] = new[4] - kinetic
                factor[slot, at, h] = (HEAT_RATIO - 1.0) * inverse
                tick[slot, at, h] = chill * new[0] * EMISSION_RATE
                new[4] = kinetic
                for f in range(5):
                    out[slot, f, pl.ds(8 * at, 8), pl.ds(128 * h, 128)] = new[f]

        @pl.when(mask == 0)
        def _():
            update(lambda f, at, h: u[index, f, at, h], lambda f, at, h: d[index, f, at, h])

        for m, ref in enumerate((got1, got2, got3, got4), 1):

            @pl.when(mask == m)
            def _():
                update(lambda f, at, h: ref[0, f, at, h], lambda f, at, h: ref[1, f, at, h])

        place = (slot, pl.ds(0, 4))
        pltpu.make_async_copy(out.at[place], result.at[place], sent.at[slot]).start()
        return 0

    lax.fori_loop(0, 4, load, 0)
    limits = [entry(plan, 6 + 3 * slot) for slot in range(4)]
    most = jnp.maximum(jnp.maximum(limits[0], limits[1]), jnp.maximum(limits[2], limits[3]))
    places = [(slot, at, h) for slot in range(4) for at, h in tiles]

    def advance(k, state):
        after = []
        for now, place in zip(state, places):
            heat = now * factor[place]
            loss = tick[place] * root(jnp.minimum(1.0 + heat * heat, BIG))
            new = now * invert(jnp.minimum(1.0 + loss, BIG))
            after.append(jnp.where(k < limits[place[0]], new, now))
        return tuple(after)

    state = lax.fori_loop(0, most, advance, tuple(energy[place] for place in places))
    for left, (slot, at, h) in zip(state, places):
        place = (slot, 4, pl.ds(8 * at, 8), pl.ds(128 * h, 128))
        out[place] = out[place] + left
    copies = []
    for slot in range(4):
        place = (slot, pl.ds(4, 1))
        copies.append(pltpu.make_async_copy(out.at[place], result.at[place], last.at[slot]))
        copies[-1].start()
    for slot in range(4):
        place = (slot, pl.ds(0, 4))
        pltpu.make_async_copy(out.at[place], result.at[place], sent.at[slot]).wait()
        copies[slot].wait()


def pair_even(count):
    return [(k, k ^ 1) for k in range(count)]


def pair_odd(count):
    return [(k, (k + 1) % count if k % 2 else (k - 1) % count) for k in range(count)]


def call(kernel, inputs, outputs, scratch=(), hbm_out=0, plan=0):
    return pl.pallas_call(
        kernel,
        in_specs=[VMEM] * len(inputs),
        out_specs=[VMEM] * (len(outputs) - hbm_out) + [ANY] * hbm_out + [VMEM] * plan,
        out_shape=[shape(*dims) for dims in outputs] + [PLAN] * plan,
        scratch_shapes=[pltpu.VMEM(x, F32) if isinstance(x, tuple) else x for x in scratch],
        compiler_params=PARAMS,
    )(*inputs)


def on_device(conserved, cool_steps, swap_slot):
    rows, columns = lax.axis_size("bx"), lax.axis_size("by")
    slots = swap_slot.transpose(2, 0, 1)
    counts = cool_steps.transpose(0, 2, 1)
    slab = (11,) + TILE
    face = (10,) + TILE
    u, w, *slabs = call(
        prep_kernel,
        [conserved.reshape(5, 256, 64)],
        [BLOCKS] * 2 + [face] * 2 + [slab] * 2 + [face] * 2 + [TILE],
    )
    e_bx, o_bx, e_by, o_by = slabs[:4]
    got_slabs = [
        lax.ppermute(e_bx, "bx", pair_even(rows)),
        lax.ppermute(o_bx, "bx", pair_odd(rows)),
        lax.ppermute(e_by, "by", pair_even(columns)),
        lax.ppermute(o_by, "by", pair_odd(columns)),
        lax.ppermute(slabs[-1], "by", [(k, k ^ 2) for k in range(columns)]),
    ]
    d, plan = call(inner_kernel, [slots, counts, w], [BLOCKS], [BLOCKS] * 3, plan=1)
    groups = [
        [i * columns + j for i in range(rows) for j in range(x, columns, 4)] for x in range(4)
    ]
    size = len(groups[0])
    d, send_a, send_b, top = call(
        edge_kernel,
        [plan, u, d, *slabs, *got_slabs],
        [BLOCKS] + [TRAVEL] * 2 + [(size // 2,) + TILE],
        [(size // 2,) + TILE, pltpu.SemaphoreType.DMA],
        hbm_out=1,
    )
    sends = {1: send_a, 2: send_b, 3: send_a}
    trade = lambda m, block: lax.ppermute(block, "by", [(k, k ^ m) for k in range(columns)])
    got = [trade(m, block) for m, block in sends.items()]
    top = top.reshape(size, 4, 128)
    top = lax.all_to_all(top, ("bx", "by"), 0, 0, axis_index_groups=groups)
    top = top.reshape((size // 2,) + TILE)
    (send_c,) = call(relay_kernel, [plan, u, d, *got], [TRAVEL])
    got.append(trade(4, send_c))
    (result,) = call(
        tail_kernel,
        [plan, u, d, top, *got],
        [(4, 5, 16, 256)],
        [(4, 5, 16, 256)] + [(4, 2, 2) + TILE] * 3 + [pltpu.SemaphoreType.DMA((4,))] * 2,
        hbm_out=1,
    )
    return result.reshape((1, 1) + result.shape)


def solution(mesh):
    in_specs = (P(None, "bx", "by", None), P(), P())
    out_specs = P("bx", "by", None, None, None, None)
    return jax.shard_map(
        on_device, mesh=mesh, in_specs=in_specs, out_specs=out_specs, check_vma=False
    )
```

```python
import functools

import jax
import jax.numpy as jnp
from jax import lax
from jax.experimental import pallas as pl
from jax.experimental.pallas import tpu as pltpu
from jax.sharding import PartitionSpec as P

HEAT_RATIO = 5.0 / 3.0
COURANT_FACTOR = 0.4
EMISSION_RATE = 100.0
F32 = jnp.float32
TILE = (8, 128)
BLOCKS = (4, 5, 2, 2) + TILE
TRAVEL = (2, 5, 2, 2) + TILE
VMEM = pl.BlockSpec(memory_space=pltpu.VMEM)
ANY = pl.BlockSpec(memory_space=pl.ANY)
PARAMS = pltpu.CompilerParams(vmem_limit_bytes=16 * 1024 * 1024)
PLAN = jax.ShapeDtypeStruct((24, 128), jnp.int32)
BIG = 3e38
SMALL = 1e-37


def shape(*dims):
    return jax.ShapeDtypeStruct(dims, F32)


def iota(axis):
    return lax.broadcasted_iota(jnp.int32, TILE, axis)


def invert(x):
    return pl.reciprocal(x, approx=True)


def root(x):
    return x * lax.rsqrt(jnp.maximum(x, SMALL))


def half_minmod(a, b):
    return 0.5 * jnp.maximum(jnp.minimum(a, b), jnp.minimum(jnp.maximum(a, b), 0.0))


def primitive(u):
    inverse = invert(u[0])
    v1, v2, v3 = u[1] * inverse, u[2] * inverse, u[3] * inverse
    p = (HEAT_RATIO - 1.0) * (u[4] - 0.5 * u[0] * (v1 * v1 + v2 * v2 + v3 * v3))
    return [u[0], v1, v2, v3, p], inverse


def hllc(left, right, n):
    rl, ul, pl_ = left[0], left[n], left[4]
    rr, ur, pr = right[0], right[n], right[4]
    cl = root(HEAT_RATIO * pl_ * invert(rl))
    cr = root(HEAT_RATIO * pr * invert(rr))
    sl = jnp.minimum(ul - cl, ur - cr)
    sr = jnp.maximum(ul + cl, ur + cr)
    ml = rl * (sl - ul)
    mr = rr * (sr - ur)
    mid = (pr - pl_ + ml * ul - mr * ur) * invert(ml - mr)
    use_left = jnp.maximum(sl, mid) >= 0.0
    rho, v1, v2, v3, p = [jnp.where(use_left, a, b) for a, b in zip(left, right)]
    edge = jnp.where(use_left, sl, sr)
    clip = jnp.where(use_left, jnp.minimum(sl, 0.0), jnp.maximum(sr, 0.0))
    u = (None, v1, v2, v3)[n]
    energy = p * (1.0 / (HEAT_RATIO - 1.0)) + 0.5 * rho * (v1 * v1 + v2 * v2 + v3 * v3)
    gap = invert(jnp.where(clip == 0.0, 1.0, edge - mid))
    ratio = (edge - u) * gap
    star_rho = rho * ratio
    star_energy = ratio * energy + (mid - u) * (star_rho * mid + p * gap)
    mass = rho * u
    f_rho = mass + clip * (star_rho - rho)
    out = [f_rho, f_rho * v1, f_rho * v2, f_rho * v3, None]
    out[n] = mass * u + p + clip * (star_rho * mid - mass)
    out[4] = (energy + p) * u + clip * (star_energy - energy)
    return out


def prep_kernel(
    cons, u_out, w_out, e_bx, o_bx, e_by, o_by, in_bx, in_by, top_out
):
    even_i = lax.axis_index("bx") % 2 == 0
    even_j = lax.axis_index("by") % 2 == 0
    lane = iota(1)
    bit0 = (lane // 16) % 2 == 0
    bit1 = (lane // 32) % 2 == 0
    row = iota(0)
    top = jnp.zeros(TILE, F32)
    for at in range(2):
        low, high, inner = [], [], []
        for h in range(2):
            tiles = []
            for f in range(5):
                x = [cons[f, pl.ds(at * 128 + h * 8 + b, 8, stride=16), :] for b in range(8)]
                if h == 0:
                    low.append(jnp.concatenate([x[0], x[1]], axis=1))
                    inner.append(x[2])
                else:
                    high.append(jnp.concatenate([x[6], x[7]], axis=1))
                    inner[f] = jnp.concatenate([x[5], inner[f]], axis=1)
                y = [jnp.concatenate([x[k], x[k + 4]], axis=1) for k in range(4)]
                z = [None] * 4
                for k in range(2):
                    z[k] = jnp.where(bit1, y[k], pltpu.roll(y[k + 2], 32, 1))
                    z[k + 2] = jnp.where(bit1, pltpu.roll(y[k], 96, 1), y[k + 2])
                t = [None] * 4
                for k in (0, 2):
                    t[k] = jnp.where(bit0, z[k], pltpu.roll(z[k + 1], 16, 1))
                    t[k + 1] = jnp.where(bit0, pltpu.roll(z[k], 112, 1), z[k + 1])
                tiles.append(t)
                for s in range(4):
                    u_out[s, f, at, h] = t[s]
            for s in range(4):
                w, inverse = primitive([tiles[f][s] for f in range(5)])
                speed = (
                    jnp.abs(w[1])
                    + jnp.abs(w[2])
                    + jnp.abs(w[3])
                    + 3.0 * root(HEAT_RATIO * w[4] * inverse)
                )
                top = jnp.maximum(top, speed)
                for f in range(5):
                    w_out[s, f, at, h] = w[f]
        low, _ = primitive(low)
        high, _ = primitive(high)
        inner, _ = primitive(inner)
        for f in range(5):
            e_by[f * 2 + at] = jnp.where(even_j, high[f], low[f])
            o_by[f * 2 + at] = jnp.where(even_j, low[f], high[f])
            in_by[f * 2 + at] = inner[f]
    for f in range(5):
        for h in range(2):
            low = jnp.zeros(TILE, F32)
            high = jnp.zeros(TILE, F32)
            inner = jnp.zeros(TILE, F32)
            for s in range(4):
                here = row // 2 == s
                a, b = w_out[s, f, 0, h], w_out[s, f, 1, h]
                low = jnp.where(here, pltpu.roll(a, 2 * s, 0), low)
                high = jnp.where(here, pltpu.roll(b, (2 * s + 2) % 8, 0), high)
                inner = jnp.where(row == 2 * s, pltpu.roll(b, (2 * s + 3) % 8, 0), inner)
                inner = jnp.where(row == 2 * s + 1, pltpu.roll(a, (2 * s + 7) % 8, 0), inner)
            e_bx[f * 2 + h] = jnp.where(even_i, high, low)
            o_bx[f * 2 + h] = jnp.where(even_i, low, high)
            in_bx[f * 2 + h] = inner
    for ref in (e_by, o_by):
        ref[10] = top
    top_out[0] = top


def make_plan(slots, counts, plan):
    i, j = lax.axis_index("bx"), lax.axis_index("by")
    row = iota(0)
    here = lax.broadcasted_iota(jnp.int32, (8, 32), 1) == jnp.bitwise_xor(
        lax.broadcasted_iota(jnp.int32, (8, 32), 0), j
    )

    def columns(line):
        line = jnp.broadcast_to(line.astype(F32), (8, 32))
        value = jnp.sum(jnp.where(here, line, 0.0), axis=1, keepdims=True)
        return jnp.broadcast_to(value, TILE)

    def across(a, mask):
        for bit in (1, 2, 4):
            if mask & bit:
                a = jnp.where(row & bit == 0, pltpu.roll(a, 8 - bit, 0), pltpu.roll(a, bit, 0))
        return a

    give = [columns(slots[r, pl.ds(i, 1), :]) for r in range(3)]
    loads = [columns(counts[i, pl.ds(k, 1), :]) for k in range(4)]
    def first_round(slot):
        moved = slot == give[0]
        return jnp.where(moved, 1.0, 0.0), jnp.where(moved, across(give[0], 1), slot)

    one, two = first_round(give[1]), first_round(give[2])
    same = give[2] == give[1]
    entries = [give[0], *one, jnp.where(same, 2.0, two[0]), two[1]]
    by_two = [across(one[0], 2) + 2.0, across(one[1], 2)]
    third = [jnp.where(same, a, b) for a, b in zip(by_two, two)]
    by_four = [across(third[0], 4) + 4.0, across(third[1], 4)]
    for slot in range(4):
        here_now = first_round(jnp.full(TILE, slot, F32))
        is_second, is_last = give[1] == float(slot), give[2] == float(slot)
        source, index = [
            jnp.where(is_last, a, jnp.where(is_second, b, c))
            for a, b, c in zip(by_four, by_two, here_now)
        ]
        code = jnp.where(is_last, 3.0, jnp.where(is_second, 2.0, here_now[0]))
        source0 = jnp.broadcast_to(source[0:1], TILE)
        index0 = jnp.broadcast_to(index[0:1], TILE)
        count = jnp.zeros(TILE, F32)
        for k in range(4):
            hit = (row.astype(F32) == source0) & (index0 == float(k))
            count += jnp.where(hit, loads[k], 0.0)
        count = jnp.sum(count, axis=0, keepdims=True)
        entries += [code, index, count]
    for e, value in enumerate(entries):
        plan[pl.ds(e, 1), :] = value[0:1].astype(jnp.int32)


def entry(plan, e):
    return plan[pl.ds(e, 1), :][0, 0]


def inner_kernel(slots, counts, w, d, plan, lefts, rights, fluxes):
    make_plan(slots, counts, plan)
    row, lane = iota(0), iota(1)

    def sweep(n, load, down, up, first, last, no_first, no_last):
        left, right = [[], []], [[], []]
        for f in range(5):
            a, b = load(f)
            da, ub = down(a), up(b)
            a_prev, b_prev = da, jnp.where(first, da, down(b))
            a_next, b_next = jnp.where(last, ub, up(a)), ub
            ha = half_minmod(a - a_prev, a_next - a)
            hb = half_minmod(b - b_prev, b_next - b)
            ra, rb = up(a - ha), up(b - hb)
            left[0].append(a + ha)
            left[1].append(b + hb)
            right[0].append(jnp.where(last, rb, ra))
            right[1].append(rb)
        fa = hllc(left[0], right[0], n)
        fb = hllc(left[1], right[1], n)
        out = []
        for f in range(5):
            a = jnp.where(no_first, 0.0, fa[f])
            b = jnp.where(no_last, 0.0, fb[f])
            da = down(a)
            out.append((a - jnp.where(first, 0.0, da), b - jnp.where(first, da, down(b))))
        return out

    def along_first(k, _):
        s, h = k // 2, k % 2
        out = sweep(
            1,
            lambda f: (w[s, f, 0, h], w[s, f, 1, h]),
            lambda a: pltpu.roll(a, 1, 0),
            lambda a: pltpu.roll(a, 7, 0),
            row == 0,
            row == 7,
            row == 0,
            row >= 6,
        )
        for f in range(5):
            d[s, f, 0, h], d[s, f, 1, h] = out[f]
        return 0

    def along_second(k, _):
        s, at = k // 2, k % 2
        out = sweep(
            2,
            lambda f: (w[s, f, at, 0], w[s, f, at, 1]),
            lambda a: pltpu.roll(a, 16, 1),
            lambda a: pltpu.roll(a, 112, 1),
            lane < 16,
            lane >= 112,
            lane < 16,
            lane >= 96,
        )
        for f in range(5):
            d[s, f, at, 0] += out[f][0]
            d[s, f, at, 1] += out[f][1]
        return 0

    first_c, last_c = lane % 16 == 0, lane % 16 == 15

    def previous(here, before):
        return jnp.where(first_c, pltpu.roll(before, 113, 1), pltpu.roll(here, 1, 1))

    def following(here, after):
        return jnp.where(last_c, pltpu.roll(after, 15, 1), pltpu.roll(here, 127, 1))

    def third_states(k, _):
        s, at = k // 2, k % 2
        before, after = (s + 3) % 4, (s + 1) % 4
        for h in range(2):
            for f in range(5):
                a = w[s, f, at, h]
                slope = half_minmod(
                    a - previous(a, w[before, f, at, h]), following(a, w[after, f, at, h]) - a
                )
                lefts[s, f, at, h] = a + slope
                rights[s, f, at, h] = a - slope
        return 0

    def third_fluxes(k, _):
        s, at = k // 2, k % 2
        after = (s + 1) % 4
        for h in range(2):
            out = hllc(
                [lefts[s, f, at, h] for f in range(5)],
                [following(rights[s, f, at, h], rights[after, f, at, h]) for f in range(5)],
                3,
            )
            for f in range(5):
                fluxes[s, f, at, h] = out[f]
        return 0

    def third_change(k, _):
        s, at = k // 2, k % 2
        before = (s + 3) % 4
        for h in range(2):
            for f in range(5):
                a = fluxes[s, f, at, h]
                d[s, f, at, h] += a - previous(a, fluxes[before, f, at, h])
        return 0

    for body in (along_first, along_second, third_states, third_fluxes, third_change):
        lax.fori_loop(0, 8, body, 0, unroll=4)


def edge_kernel(
    plan, u, d_in, se_bx, so_bx, se_by, so_by, in_bx, in_by, top, re_bx, ro_bx, re_by, ro_by, top2,
    d, send, top_out, spread, sent,
):
    i, j = lax.axis_index("bx"), lax.axis_index("by")
    even_i, even_j = i % 2 == 0, j % 2 == 0
    row, lane = iota(0), iota(1)

    top = jnp.maximum(jnp.maximum(top[0], top2[0]), jnp.maximum(re_by[10], ro_by[10]))
    top = jnp.broadcast_to(jnp.max(top, axis=0, keepdims=True), TILE)
    for k in range(spread.shape[0]):
        spread[k] = top[:6]
    copy = pltpu.make_async_copy(spread, top_out, sent)
    copy.start()

    def faces(n, own_low, own_high, low, high, inner, back, ahead, zero):
        left, right, left2, right2 = [], [], [], []
        for o, q, a, b, w in zip(own_low, own_high, low, high, inner):
            c = jnp.where(zero, ahead(a), back(o))
            left.append(c + half_minmod(c - a, o - c))
            right.append(o - half_minmod(o - c, jnp.where(zero, ahead(o), w) - o))
            e = jnp.where(zero, ahead(q), back(b))
            left2.append(q + half_minmod(q - jnp.where(zero, w, back(q)), e - q))
            right2.append(e - half_minmod(e - q, b - e))
        low_flux = hllc(left, right, n)
        high_flux = hllc(left2, right2, n)
        return (
            [jnp.where(zero, ahead(f) - f, -f) for f in low_flux],
            [jnp.where(zero, f, f - back(f)) for f in high_flux],
        )

    def picked(flag, a, b, index):
        return [jnp.where(flag, a[t], b[t]) for t in range(index, 10, 2)]

    d[...] = d_in[...]
    for h in range(2):
        low, high = faces(
            1,
            picked(even_i, so_bx, se_bx, h),
            picked(even_i, se_bx, so_bx, h),
            picked(even_i, ro_bx, re_bx, h),
            picked(even_i, re_bx, ro_bx, h),
            [in_bx[t] for t in range(h, 10, 2)],
            lambda a: pltpu.roll(a, 1, 0),
            lambda a: pltpu.roll(a, 7, 0),
            row % 2 == 0,
        )
        for f in range(5):
            for s in range(4):
                d[s, f, 0, h] += jnp.where(row < 2, pltpu.roll(low[f], (8 - 2 * s) % 8, 0), 0.0)
                d[s, f, 1, h] += jnp.where(row >= 6, pltpu.roll(high[f], 6 - 2 * s, 0), 0.0)
    for at in range(2):
        turn = lambda a: pltpu.roll(a, 64, 1)
        low, high = faces(
            2,
            picked(even_j, so_by, se_by, at),
            picked(even_j, se_by, so_by, at),
            picked(even_j, ro_by, re_by, at),
            picked(even_j, re_by, ro_by, at),
            [in_by[t] for t in range(at, 10, 2)],
            turn,
            turn,
            lane < 64,
        )
        for f in range(5):
            for s in range(4):
                one = pltpu.roll(low[f], (128 - 16 * s) % 128, 1)
                two = pltpu.roll(low[f], 80 - 16 * s, 1)
                d[s, f, at, 0] += jnp.where(lane < 16, one, jnp.where(lane < 32, two, 0.0))
                one = pltpu.roll(high[f], 96 - 16 * s, 1)
                two = pltpu.roll(high[f], 48 - 16 * s, 1)
                d[s, f, at, 1] += jnp.where(lane >= 112, two, jnp.where(lane >= 96, one, 0.0))

    slot = entry(plan, 0)
    send[0] = u[slot]
    send[1] = d[slot]
    copy.wait()


def relay_kernel(first, plan, u, d, *refs):
    *got, send = refs
    code, index = entry(plan, first), entry(plan, first + 1)

    @pl.when(code == 0)
    def _():
        send[0] = u[index]
        send[1] = d[index]

    for m, ref in enumerate(got, 1):

        @pl.when(code == m)
        def _():
            send[...] = ref[...]


def tail_kernel(
    plan, u, d, top, got1, got2, got4, result, out, energy, factor, tick, sent, last
):
    speed = jnp.max(jnp.max(top[...], axis=0), axis=0, keepdims=True)
    speed = jnp.max(speed, axis=1, keepdims=True)
    step = COURANT_FACTOR / jnp.broadcast_to(speed, TILE)
    tiles = [(at, h) for at in range(2) for h in range(2)]

    def load(slot, _):
        mask, index, count = [entry(plan, 5 + 3 * slot + k) for k in range(3)]
        chill = step / count.astype(F32)

        def update(u_of, d_of):
            for at, h in tiles:
                new = [u_of(f, at, h) - step * d_of(f, at, h) for f in range(5)]
                inverse = invert(new[0])
                squares = new[1] * new[1] + new[2] * new[2] + new[3] * new[3]
                kinetic = 0.5 * squares * inverse
                energy[slot, at, h] = new[4] - kinetic
                factor[slot, at, h] = (HEAT_RATIO - 1.0) * inverse
                tick[slot, at, h] = chill * new[0] * EMISSION_RATE
                new[4] = kinetic
                for f in range(5):
                    out[slot, f, pl.ds(8 * at, 8), pl.ds(128 * h, 128)] = new[f]

        @pl.when(mask == 0)
        def _():
            update(lambda f, at, h: u[index, f, at, h], lambda f, at, h: d[index, f, at, h])

        for m, ref in enumerate((got1, got2, got4), 1):

            @pl.when(mask == m)
            def _():
                update(lambda f, at, h: ref[0, f, at, h], lambda f, at, h: ref[1, f, at, h])

        place = (slot, pl.ds(0, 4))
        pltpu.make_async_copy(out.at[place], result.at[place], sent.at[slot]).start()
        return 0

    lax.fori_loop(0, 4, load, 0)
    limits = [entry(plan, 7 + 3 * slot) for slot in range(4)]
    most = jnp.maximum(jnp.maximum(limits[0], limits[1]), jnp.maximum(limits[2], limits[3]))
    places = [(slot, at, h) for slot in range(4) for at, h in tiles]

    def advance(k, state):
        after = []
        for now, place in zip(state, places):
            heat = now * factor[place]
            loss = tick[place] * root(jnp.minimum(1.0 + heat * heat, BIG))
            new = now * invert(jnp.minimum(1.0 + loss, BIG))
            after.append(jnp.where(k < limits[place[0]], new, now))
        return tuple(after)

    state = lax.fori_loop(0, most, advance, tuple(energy[place] for place in places))
    for left, (slot, at, h) in zip(state, places):
        place = (slot, 4, pl.ds(8 * at, 8), pl.ds(128 * h, 128))
        out[place] = out[place] + left
    copies = []
    for slot in range(4):
        place = (slot, pl.ds(4, 1))
        copies.append(pltpu.make_async_copy(out.at[place], result.at[place], last.at[slot]))
        copies[-1].start()
    for slot in range(4):
        place = (slot, pl.ds(0, 4))
        pltpu.make_async_copy(out.at[place], result.at[place], sent.at[slot]).wait()
        copies[slot].wait()


def pair_even(count):
    return [(k, k ^ 1) for k in range(count)]


def pair_odd(count):
    return [(k, (k + 1) % count if k % 2 else (k - 1) % count) for k in range(count)]


def call(kernel, inputs, outputs, scratch=(), hbm_out=0, plan=0):
    return pl.pallas_call(
        kernel,
        in_specs=[VMEM] * len(inputs),
        out_specs=[VMEM] * (len(outputs) - hbm_out) + [ANY] * hbm_out + [VMEM] * plan,
        out_shape=[shape(*dims) for dims in outputs] + [PLAN] * plan,
        scratch_shapes=[pltpu.VMEM(x, F32) if isinstance(x, tuple) else x for x in scratch],
        compiler_params=PARAMS,
    )(*inputs)


def on_device(conserved, cool_steps, swap_slot):
    rows, columns = lax.axis_size("bx"), lax.axis_size("by")
    slots = swap_slot.transpose(2, 0, 1)
    counts = cool_steps.transpose(0, 2, 1)
    face = (10,) + TILE
    u, w, *slabs = call(
        prep_kernel,
        [conserved.reshape(5, 256, 64)],
        [BLOCKS] * 2
        + [(10,) + TILE, (12,) + TILE, (11,) + TILE, (14,) + TILE]
        + [face] * 2
        + [(13,) + TILE],
    )
    e_bx, o_bx, e_by, o_by = slabs[:4]
    got_slabs = [
        lax.ppermute(e_bx, "bx", pair_even(rows)),
        lax.ppermute(o_bx, "bx", pair_odd(rows)),
        lax.ppermute(e_by, "by", pair_even(columns)),
        lax.ppermute(o_by, "by", pair_odd(columns)),
        lax.ppermute(slabs[-1], "by", [(k, k ^ 2) for k in range(columns)]),
    ]
    d, plan = call(inner_kernel, [slots, counts, w], [BLOCKS], [BLOCKS] * 3, plan=1)
    groups = [
        [i * columns + j for i in range(rows) for j in range(x, columns, 4)] for x in range(4)
    ]
    size = len(groups[0])
    d, send, top = call(
        edge_kernel,
        [plan, u, d, *slabs, *got_slabs],
        [BLOCKS, TRAVEL, (size, 6, 128)],
        [(size, 6, 128), pltpu.SemaphoreType.DMA],
        hbm_out=1,
    )
    trade = lambda m, block: lax.ppermute(block, "by", [(k, k ^ m) for k in range(columns)])
    got = [trade(1, send)]
    top = lax.all_to_all(top, ("bx", "by"), 0, 0, axis_index_groups=groups)
    for first, mask in ((1, 2), (3, 4)):
        kernel = functools.partial(relay_kernel, first)
        (send,) = call(kernel, [plan, u, d, *got], [TRAVEL])
        got.append(trade(mask, send))
    (result,) = call(
        tail_kernel,
        [plan, u, d, top, *got],
        [(4, 5, 16, 256)],
        [(4, 5, 16, 256)] + [(4, 2, 2) + TILE] * 3 + [pltpu.SemaphoreType.DMA((4,))] * 2,
        hbm_out=1,
    )
    return result.reshape((1, 1) + result.shape)


def solution(mesh):
    in_specs = (P(None, "bx", "by", None), P(), P())
    out_specs = P("bx", "by", None, None, None, None)
    return jax.shard_map(
        on_device, mesh=mesh, in_specs=in_specs, out_specs=out_specs, check_vma=False
    )
```

```python
import functools

import jax
import jax.numpy as jnp
from jax import lax
from jax.experimental import pallas as pl
from jax.experimental.pallas import tpu as pltpu
from jax.sharding import PartitionSpec as P

HEAT_RATIO = 5.0 / 3.0
COURANT_FACTOR = 0.4
EMISSION_RATE = 100.0
F32 = jnp.float32
TILE = (8, 128)
BLOCKS = (4, 5, 2, 2) + TILE
TRAVEL = (2, 5, 2, 2) + TILE
VMEM = pl.BlockSpec(memory_space=pltpu.VMEM)
ANY = pl.BlockSpec(memory_space=pl.ANY)
PARAMS = pltpu.CompilerParams(vmem_limit_bytes=16 * 1024 * 1024)
PLAN = jax.ShapeDtypeStruct((24, 128), jnp.int32)
BIG = 3e38
SMALL = 1e-37


def shape(*dims):
    return jax.ShapeDtypeStruct(dims, F32)


def iota(axis):
    return lax.broadcasted_iota(jnp.int32, TILE, axis)


def invert(x):
    return pl.reciprocal(x, approx=True)


def root(x):
    return x * lax.rsqrt(jnp.maximum(x, SMALL))


def half_minmod(a, b):
    return 0.5 * jnp.maximum(jnp.minimum(a, b), jnp.minimum(jnp.maximum(a, b), 0.0))


def primitive(u):
    inverse = invert(u[0])
    v1, v2, v3 = u[1] * inverse, u[2] * inverse, u[3] * inverse
    p = (HEAT_RATIO - 1.0) * (u[4] - 0.5 * u[0] * (v1 * v1 + v2 * v2 + v3 * v3))
    return [u[0], v1, v2, v3, p], inverse


def hllc(left, right, n):
    rl, ul, pl_ = left[0], left[n], left[4]
    rr, ur, pr = right[0], right[n], right[4]
    cl = root(HEAT_RATIO * pl_ * invert(rl))
    cr = root(HEAT_RATIO * pr * invert(rr))
    sl = jnp.minimum(ul - cl, ur - cr)
    sr = jnp.maximum(ul + cl, ur + cr)
    ml = rl * (sl - ul)
    mr = rr * (sr - ur)
    mid = (pr - pl_ + ml * ul - mr * ur) * invert(ml - mr)
    use_left = jnp.maximum(sl, mid) >= 0.0
    rho, v1, v2, v3, p = [jnp.where(use_left, a, b) for a, b in zip(left, right)]
    edge = jnp.where(use_left, sl, sr)
    clip = jnp.where(use_left, jnp.minimum(sl, 0.0), jnp.maximum(sr, 0.0))
    u = (None, v1, v2, v3)[n]
    energy = p * (1.0 / (HEAT_RATIO - 1.0)) + 0.5 * rho * (v1 * v1 + v2 * v2 + v3 * v3)
    gap = invert(jnp.where(clip == 0.0, 1.0, edge - mid))
    ratio = (edge - u) * gap
    star_rho = rho * ratio
    star_energy = ratio * energy + (mid - u) * (star_rho * mid + p * gap)
    mass = rho * u
    f_rho = mass + clip * (star_rho - rho)
    out = [f_rho, f_rho * v1, f_rho * v2, f_rho * v3, None]
    out[n] = mass * u + p + clip * (star_rho * mid - mass)
    out[4] = (energy + p) * u + clip * (star_energy - energy)
    return out


def prep_kernel(
    cons, u_out, w_out, e_bx, o_bx, e_by, o_by, in_bx, in_by, top_out
):
    even_i = lax.axis_index("bx") % 2 == 0
    even_j = lax.axis_index("by") % 2 == 0
    lane = iota(1)
    bit0 = (lane // 16) % 2 == 0
    bit1 = (lane // 32) % 2 == 0
    row = iota(0)
    top = jnp.zeros(TILE, F32)
    for at in range(2):
        low, high, inner = [], [], []
        for h in range(2):
            tiles = []
            for f in range(5):
                x = [cons[f, pl.ds(at * 128 + h * 8 + b, 8, stride=16), :] for b in range(8)]
                if h == 0:
                    low.append(jnp.concatenate([x[0], x[1]], axis=1))
                    inner.append(x[2])
                else:
                    high.append(jnp.concatenate([x[6], x[7]], axis=1))
                    inner[f] = jnp.concatenate([x[5], inner[f]], axis=1)
                y = [jnp.concatenate([x[k], x[k + 4]], axis=1) for k in range(4)]
                z = [None] * 4
                for k in range(2):
                    z[k] = jnp.where(bit1, y[k], pltpu.roll(y[k + 2], 32, 1))
                    z[k + 2] = jnp.where(bit1, pltpu.roll(y[k], 96, 1), y[k + 2])
                t = [None] * 4
                for k in (0, 2):
                    t[k] = jnp.where(bit0, z[k], pltpu.roll(z[k + 1], 16, 1))
                    t[k + 1] = jnp.where(bit0, pltpu.roll(z[k], 112, 1), z[k + 1])
                tiles.append(t)
                for s in range(4):
                    u_out[s, f, at, h] = t[s]
            for s in range(4):
                w, inverse = primitive([tiles[f][s] for f in range(5)])
                speed = (
                    jnp.abs(w[1])
                    + jnp.abs(w[2])
                    + jnp.abs(w[3])
                    + 3.0 * root(HEAT_RATIO * w[4] * inverse)
                )
                top = jnp.maximum(top, speed)
                for f in range(5):
                    w_out[s, f, at, h] = w[f]
        low, _ = primitive(low)
        high, _ = primitive(high)
        inner, _ = primitive(inner)
        for f in range(5):
            e_by[f * 2 + at] = jnp.where(even_j, high[f], low[f])
            o_by[f * 2 + at] = jnp.where(even_j, low[f], high[f])
            in_by[f * 2 + at] = inner[f]
    for f in range(5):
        for h in range(2):
            low = jnp.zeros(TILE, F32)
            high = jnp.zeros(TILE, F32)
            inner = jnp.zeros(TILE, F32)
            for s in range(4):
                here = row // 2 == s
                a, b = w_out[s, f, 0, h], w_out[s, f, 1, h]
                low = jnp.where(here, pltpu.roll(a, 2 * s, 0), low)
                high = jnp.where(here, pltpu.roll(b, (2 * s + 2) % 8, 0), high)
                inner = jnp.where(row == 2 * s, pltpu.roll(b, (2 * s + 3) % 8, 0), inner)
                inner = jnp.where(row == 2 * s + 1, pltpu.roll(a, (2 * s + 7) % 8, 0), inner)
            e_bx[f * 2 + h] = jnp.where(even_i, high, low)
            o_bx[f * 2 + h] = jnp.where(even_i, low, high)
            in_bx[f * 2 + h] = inner
    for ref in (e_by, o_by):
        ref[10] = top
    top_out[0] = top


def make_plan(slots, counts, plan):
    i, j = lax.axis_index("bx"), lax.axis_index("by")
    row = iota(0)
    here = lax.broadcasted_iota(jnp.int32, (8, 32), 1) == jnp.bitwise_xor(
        lax.broadcasted_iota(jnp.int32, (8, 32), 0), j
    )

    def columns(line):
        line = jnp.broadcast_to(line.astype(F32), (8, 32))
        value = jnp.sum(jnp.where(here, line, 0.0), axis=1, keepdims=True)
        return jnp.broadcast_to(value, TILE)

    def across(a, mask):
        for bit in (1, 2, 4):
            if mask & bit:
                a = jnp.where(row & bit == 0, pltpu.roll(a, 8 - bit, 0), pltpu.roll(a, bit, 0))
        return a

    give = [columns(slots[r, pl.ds(i, 1), :]) for r in range(3)]
    loads = [columns(counts[i, pl.ds(k, 1), :]) for k in range(4)]
    def first_round(slot):
        moved = slot == give[0]
        return jnp.where(moved, 1.0, 0.0), jnp.where(moved, across(give[0], 1), slot)

    one, two = first_round(give[1]), first_round(give[2])
    same = give[2] == give[1]
    entries = [give[0], *one, jnp.where(same, 2.0, two[0]), two[1]]
    by_two = [across(one[0], 2) + 2.0, across(one[1], 2)]
    third = [jnp.where(same, a, b) for a, b in zip(by_two, two)]
    by_four = [across(third[0], 4) + 4.0, across(third[1], 4)]
    for slot in range(4):
        here_now = first_round(jnp.full(TILE, slot, F32))
        is_second, is_last = give[1] == float(slot), give[2] == float(slot)
        source, index = [
            jnp.where(is_last, a, jnp.where(is_second, b, c))
            for a, b, c in zip(by_four, by_two, here_now)
        ]
        code = jnp.where(is_last, 3.0, jnp.where(is_second, 2.0, here_now[0]))
        source0 = jnp.broadcast_to(source[0:1], TILE)
        index0 = jnp.broadcast_to(index[0:1], TILE)
        count = jnp.zeros(TILE, F32)
        for k in range(4):
            hit = (row.astype(F32) == source0) & (index0 == float(k))
            count += jnp.where(hit, loads[k], 0.0)
        count = jnp.sum(count, axis=0, keepdims=True)
        entries += [code, index, count]
    entries.append(give[2])
    for e, value in enumerate(entries):
        plan[pl.ds(e, 1), :] = value[0:1].astype(jnp.int32)


def entry(plan, e):
    return plan[pl.ds(e, 1), :][0, 0]


def inner_kernel(slots, counts, w, d, plan, lefts, rights, fluxes):
    make_plan(slots, counts, plan)
    row, lane = iota(0), iota(1)

    def sweep(n, load, down, up, first, last, no_first, no_last):
        left, right = [[], []], [[], []]
        for f in range(5):
            a, b = load(f)
            da, ub = down(a), up(b)
            a_prev, b_prev = da, jnp.where(first, da, down(b))
            a_next, b_next = jnp.where(last, ub, up(a)), ub
            ha = half_minmod(a - a_prev, a_next - a)
            hb = half_minmod(b - b_prev, b_next - b)
            ra, rb = up(a - ha), up(b - hb)
            left[0].append(a + ha)
            left[1].append(b + hb)
            right[0].append(jnp.where(last, rb, ra))
            right[1].append(rb)
        fa = hllc(left[0], right[0], n)
        fb = hllc(left[1], right[1], n)
        out = []
        for f in range(5):
            a = jnp.where(no_first, 0.0, fa[f])
            b = jnp.where(no_last, 0.0, fb[f])
            da = down(a)
            out.append((a - jnp.where(first, 0.0, da), b - jnp.where(first, da, down(b))))
        return out

    def along_first(k, _):
        s, h = k // 2, k % 2
        out = sweep(
            1,
            lambda f: (w[s, f, 0, h], w[s, f, 1, h]),
            lambda a: pltpu.roll(a, 1, 0),
            lambda a: pltpu.roll(a, 7, 0),
            row == 0,
            row == 7,
            row == 0,
            row >= 6,
        )
        for f in range(5):
            d[s, f, 0, h], d[s, f, 1, h] = out[f]
        return 0

    def along_second(k, _):
        s, at = k // 2, k % 2
        out = sweep(
            2,
            lambda f: (w[s, f, at, 0], w[s, f, at, 1]),
            lambda a: pltpu.roll(a, 16, 1),
            lambda a: pltpu.roll(a, 112, 1),
            lane < 16,
            lane >= 112,
            lane < 16,
            lane >= 96,
        )
        for f in range(5):
            d[s, f, at, 0] += out[f][0]
            d[s, f, at, 1] += out[f][1]
        return 0

    first_c, last_c = lane % 16 == 0, lane % 16 == 15

    def previous(here, before):
        return jnp.where(first_c, pltpu.roll(before, 113, 1), pltpu.roll(here, 1, 1))

    def following(here, after):
        return jnp.where(last_c, pltpu.roll(after, 15, 1), pltpu.roll(here, 127, 1))

    def third_states(k, _):
        s, at = k // 2, k % 2
        before, after = (s + 3) % 4, (s + 1) % 4
        for h in range(2):
            for f in range(5):
                a = w[s, f, at, h]
                slope = half_minmod(
                    a - previous(a, w[before, f, at, h]), following(a, w[after, f, at, h]) - a
                )
                lefts[s, f, at, h] = a + slope
                rights[s, f, at, h] = a - slope
        return 0

    def third_fluxes(k, _):
        s, at = k // 2, k % 2
        after = (s + 1) % 4
        for h in range(2):
            out = hllc(
                [lefts[s, f, at, h] for f in range(5)],
                [following(rights[s, f, at, h], rights[after, f, at, h]) for f in range(5)],
                3,
            )
            for f in range(5):
                fluxes[s, f, at, h] = out[f]
        return 0

    def third_change(k, _):
        s, at = k // 2, k % 2
        before = (s + 3) % 4
        for h in range(2):
            for f in range(5):
                a = fluxes[s, f, at, h]
                d[s, f, at, h] += a - previous(a, fluxes[before, f, at, h])
        return 0

    for body in (along_first, along_second, third_states, third_fluxes, third_change):
        lax.fori_loop(0, 8, body, 0, unroll=4)


def edge_kernel(
    plan, u, d_in, se_bx, so_bx, se_by, so_by, in_bx, in_by, top, re_bx, ro_bx, re_by, ro_by, top2,
    d, send, top_out, spread, sent,
):
    i, j = lax.axis_index("bx"), lax.axis_index("by")
    even_i, even_j = i % 2 == 0, j % 2 == 0
    row, lane = iota(0), iota(1)

    top = jnp.maximum(jnp.maximum(top[0], top2[0]), jnp.maximum(re_by[10], ro_by[10]))
    top = jnp.broadcast_to(jnp.max(top, axis=0, keepdims=True), TILE)
    for k in range(spread.shape[0]):
        spread[k] = top
    copy = pltpu.make_async_copy(spread, top_out, sent)
    copy.start()

    def faces(n, own_low, own_high, low, high, inner, back, ahead, zero):
        left, right, left2, right2 = [], [], [], []
        for o, q, a, b, w in zip(own_low, own_high, low, high, inner):
            c = jnp.where(zero, ahead(a), back(o))
            left.append(c + half_minmod(c - a, o - c))
            right.append(o - half_minmod(o - c, jnp.where(zero, ahead(o), w) - o))
            e = jnp.where(zero, ahead(q), back(b))
            left2.append(q + half_minmod(q - jnp.where(zero, w, back(q)), e - q))
            right2.append(e - half_minmod(e - q, b - e))
        low_flux = hllc(left, right, n)
        high_flux = hllc(left2, right2, n)
        return (
            [jnp.where(zero, ahead(f) - f, -f) for f in low_flux],
            [jnp.where(zero, f, f - back(f)) for f in high_flux],
        )

    def picked(flag, a, b, index):
        return [jnp.where(flag, a[t], b[t]) for t in range(index, 10, 2)]

    d[...] = d_in[...]
    for h in range(2):
        low, high = faces(
            1,
            picked(even_i, so_bx, se_bx, h),
            picked(even_i, se_bx, so_bx, h),
            picked(even_i, ro_bx, re_bx, h),
            picked(even_i, re_bx, ro_bx, h),
            [in_bx[t] for t in range(h, 10, 2)],
            lambda a: pltpu.roll(a, 1, 0),
            lambda a: pltpu.roll(a, 7, 0),
            row % 2 == 0,
        )
        for f in range(5):
            for s in range(4):
                d[s, f, 0, h] += jnp.where(row < 2, pltpu.roll(low[f], (8 - 2 * s) % 8, 0), 0.0)
                d[s, f, 1, h] += jnp.where(row >= 6, pltpu.roll(high[f], 6 - 2 * s, 0), 0.0)
    for at in range(2):
        turn = lambda a: pltpu.roll(a, 64, 1)
        low, high = faces(
            2,
            picked(even_j, so_by, se_by, at),
            picked(even_j, se_by, so_by, at),
            picked(even_j, ro_by, re_by, at),
            picked(even_j, re_by, ro_by, at),
            [in_by[t] for t in range(at, 10, 2)],
            turn,
            turn,
            lane < 64,
        )
        for f in range(5):
            for s in range(4):
                one = pltpu.roll(low[f], (128 - 16 * s) % 128, 1)
                two = pltpu.roll(low[f], 80 - 16 * s, 1)
                d[s, f, at, 0] += jnp.where(lane < 16, one, jnp.where(lane < 32, two, 0.0))
                one = pltpu.roll(high[f], 96 - 16 * s, 1)
                two = pltpu.roll(high[f], 48 - 16 * s, 1)
                d[s, f, at, 1] += jnp.where(lane >= 112, two, jnp.where(lane >= 96, one, 0.0))

    slot = entry(plan, 0)
    send[0] = u[slot]
    send[1] = d[slot]
    copy.wait()


def relay_kernel(first, plan, u, d, *refs):
    *got, send = refs
    code, index = entry(plan, first), entry(plan, first + 1)

    @pl.when(code == 0)
    def _():
        send[0] = u[index]
        send[1] = d[index]

    for m, ref in enumerate(got, 1):

        @pl.when(code == m)
        def _():
            send[...] = ref[...]


def block_tiles():
    return [(at, h) for at in range(2) for h in range(2)]


def update(out, energy, factor, tick, slot, step, count, u_of, d_of):
    chill = step / count.astype(F32)
    for at, h in block_tiles():
        new = [u_of(f, at, h) - step * d_of(f, at, h) for f in range(5)]
        inverse = invert(new[0])
        squares = new[1] * new[1] + new[2] * new[2] + new[3] * new[3]
        kinetic = 0.5 * squares * inverse
        energy[slot, at, h] = new[4] - kinetic
        factor[slot, at, h] = (HEAT_RATIO - 1.0) * inverse
        tick[slot, at, h] = chill * new[0] * EMISSION_RATE
        new[4] = kinetic
        for f in range(5):
            out[slot, f, pl.ds(8 * at, 8), pl.ds(128 * h, 128)] = new[f]


def cool(out, energy, factor, tick, limits):
    places = [(slot, at, h) for slot in range(len(limits)) for at, h in block_tiles()]
    most = limits[0]
    for limit in limits[1:]:
        most = jnp.maximum(most, limit)

    def advance(k, state):
        after = []
        for now, place in zip(state, places):
            heat = now * factor[place]
            loss = tick[place] * root(jnp.minimum(1.0 + heat * heat, BIG))
            new = now * invert(jnp.minimum(1.0 + loss, BIG))
            after.append(jnp.where(k < limits[place[0]], new, now))
        return tuple(after)

    state = lax.fori_loop(0, most, advance, tuple(energy[place] for place in places))
    for left, (slot, at, h) in zip(state, places):
        place = (slot, 4, pl.ds(8 * at, 8), pl.ds(128 * h, 128))
        out[place] = out[place] + left


def near_kernel(
    plan, u, d, top, got1, got2, step_out, result, out, energy, factor, tick, sent, last
):
    speed = jnp.max(jnp.max(top[...], axis=0), axis=0, keepdims=True)
    speed = jnp.max(speed, axis=1, keepdims=True)
    step = COURANT_FACTOR / jnp.broadcast_to(speed, TILE)
    step_out[...] = step
    skipped = entry(plan, 17)
    target = lambda k: k + jnp.where(k >= skipped, 1, 0)

    def load(k, _):
        code, index, count = [entry(plan, 5 + 3 * target(k) + e) for e in range(3)]
        store = lambda *parts: update(out, energy, factor, tick, k, step, count, *parts)

        @pl.when(code == 0)
        def _():
            store(lambda f, at, h: u[index, f, at, h], lambda f, at, h: d[index, f, at, h])

        for m, ref in enumerate((got1, got2), 1):

            @pl.when(code == m)
            def _():
                store(lambda f, at, h: ref[0, f, at, h], lambda f, at, h: ref[1, f, at, h])

        rows = pl.ds(0, 4)
        pltpu.make_async_copy(
            out.at[k, rows], result.at[target(k), rows], sent.at[k]
        ).start()
        return 0

    lax.fori_loop(0, 3, load, 0)
    cool(out, energy, factor, tick, [entry(plan, 7 + 3 * target(k)) for k in range(3)])
    copies = []
    for k in range(3):
        row = pl.ds(4, 1)
        copies.append(
            pltpu.make_async_copy(out.at[k, row], result.at[target(k), row], last.at[k])
        )
        copies[-1].start()
    for k in range(3):
        rows = pl.ds(0, 4)
        pltpu.make_async_copy(out.at[k, rows], result.at[target(k), rows], sent.at[k]).wait()
        copies[k].wait()


def far_kernel(plan, step, got, given, result, out, energy, factor, tick, sent, last):
    slot = entry(plan, 17)
    count = entry(plan, 7 + 3 * slot)
    u_of, d_of = [lambda f, at, h, k=k: got[k, f, at, h] for k in range(2)]
    update(out, energy, factor, tick, 0, step[...], count, u_of, d_of)
    first = pltpu.make_async_copy(
        out.at[0, pl.ds(0, 4)], result.at[slot, pl.ds(0, 4)], sent
    )
    first.start()
    cool(out, energy, factor, tick, [count])
    second = pltpu.make_async_copy(
        out.at[0, pl.ds(4, 1)], result.at[slot, pl.ds(4, 1)], last
    )
    second.start()
    first.wait()
    second.wait()


def pair_even(count):
    return [(k, k ^ 1) for k in range(count)]


def pair_odd(count):
    return [(k, (k + 1) % count if k % 2 else (k - 1) % count) for k in range(count)]


def call(kernel, inputs, outputs, scratch=(), hbm_in=0, hbm_out=0, plan=0, aliases=None):
    return pl.pallas_call(
        kernel,
        in_specs=[VMEM] * (len(inputs) - hbm_in) + [ANY] * hbm_in,
        out_specs=[VMEM] * (len(outputs) - hbm_out) + [ANY] * hbm_out + [VMEM] * plan,
        out_shape=[shape(*dims) for dims in outputs] + [PLAN] * plan,
        scratch_shapes=[pltpu.VMEM(x, F32) if isinstance(x, tuple) else x for x in scratch],
        compiler_params=PARAMS,
        input_output_aliases=aliases or {},
    )(*inputs)


def on_device(conserved, cool_steps, swap_slot):
    rows, columns = lax.axis_size("bx"), lax.axis_size("by")
    slots = swap_slot.transpose(2, 0, 1)
    counts = cool_steps.transpose(0, 2, 1)
    face = (10,) + TILE
    u, w, *slabs = call(
        prep_kernel,
        [conserved.reshape(5, 256, 64)],
        [BLOCKS] * 2
        + [(10,) + TILE, (12,) + TILE, (11,) + TILE, (14,) + TILE]
        + [face] * 2
        + [(13,) + TILE],
    )
    e_bx, o_bx, e_by, o_by = slabs[:4]
    got_slabs = [
        lax.ppermute(e_bx, "bx", pair_even(rows)),
        lax.ppermute(o_bx, "bx", pair_odd(rows)),
        lax.ppermute(e_by, "by", pair_even(columns)),
        lax.ppermute(o_by, "by", pair_odd(columns)),
        lax.ppermute(slabs[-1], "by", [(k, k ^ 2) for k in range(columns)]),
    ]
    d, plan = call(inner_kernel, [slots, counts, w], [BLOCKS], [BLOCKS] * 3, plan=1)
    groups = [
        [i * columns + j for i in range(rows) for j in range(x, columns, 4)] for x in range(4)
    ]
    size = len(groups[0])
    chunks = (size * 6 // 8,) + TILE
    d, send, top = call(
        edge_kernel,
        [plan, u, d, *slabs, *got_slabs],
        [BLOCKS, TRAVEL, chunks],
        [chunks, pltpu.SemaphoreType.DMA],
        hbm_out=1,
    )
    trade = lambda m, block: lax.ppermute(block, "by", [(k, k ^ m) for k in range(columns)])
    got = [trade(1, send)]
    top = top.reshape(size, 6, 1, 128)
    top = lax.all_to_all(top, ("bx", "by"), 0, 0, axis_index_groups=groups)
    top = top.reshape(chunks)
    for first, mask in ((1, 2), (3, 4)):
        kernel = functools.partial(relay_kernel, first)
        (send,) = call(kernel, [plan, u, d, *got], [TRAVEL])
        got.append(trade(mask, send))
    block = (5, 16, 256)
    state = (2, 2) + TILE
    step, result = call(
        near_kernel,
        [plan, u, d, top, *got[:2]],
        [TILE, (4,) + block],
        [(3,) + block] + [(3,) + state] * 3 + [pltpu.SemaphoreType.DMA((3,))] * 2,
        hbm_out=1,
    )
    (result,) = call(
        far_kernel,
        [plan, step, got[2], result],
        [(4,) + block],
        [(1,) + block] + [(1,) + state] * 3 + [pltpu.SemaphoreType.DMA] * 2,
        hbm_in=1,
        hbm_out=1,
        aliases={3: 0},
    )
    return result.reshape((1, 1) + result.shape)


def solution(mesh):
    in_specs = (P(None, "bx", "by", None), P(), P())
    out_specs = P("bx", "by", None, None, None, None)
    return jax.shard_map(
        on_device, mesh=mesh, in_specs=in_specs, out_specs=out_specs, check_vma=False
    )
```

```python
import functools

import jax
import jax.numpy as jnp
from jax import lax
from jax.experimental import pallas as pl
from jax.experimental.pallas import tpu as pltpu
from jax.sharding import PartitionSpec as P

HEAT_RATIO = 5.0 / 3.0
COURANT_FACTOR = 0.4
EMISSION_RATE = 100.0
F32 = jnp.float32
TILE = (8, 128)
BLOCKS = (4, 5, 2, 2) + TILE
TRAVEL = (2, 5, 2, 2) + TILE
HALF = (5, 2, 2) + TILE
VMEM = pl.BlockSpec(memory_space=pltpu.VMEM)
ANY = pl.BlockSpec(memory_space=pl.ANY)
PARAMS = pltpu.CompilerParams(vmem_limit_bytes=16 * 1024 * 1024)
PLAN = jax.ShapeDtypeStruct((24, 128), jnp.int32)
BIG = 3e38
SMALL = 1e-37


def shape(*dims):
    return jax.ShapeDtypeStruct(dims, F32)


def iota(axis):
    return lax.broadcasted_iota(jnp.int32, TILE, axis)


def invert(x):
    return pl.reciprocal(x, approx=True)


def root(x):
    return x * lax.rsqrt(jnp.maximum(x, SMALL))


def half_minmod(a, b):
    return 0.5 * jnp.maximum(jnp.minimum(a, b), jnp.minimum(jnp.maximum(a, b), 0.0))


def primitive(u):
    inverse = invert(u[0])
    v1, v2, v3 = u[1] * inverse, u[2] * inverse, u[3] * inverse
    p = (HEAT_RATIO - 1.0) * (u[4] - 0.5 * u[0] * (v1 * v1 + v2 * v2 + v3 * v3))
    return [u[0], v1, v2, v3, p], inverse


def hllc(left, right, n):
    rl, ul, pl_ = left[0], left[n], left[4]
    rr, ur, pr = right[0], right[n], right[4]
    cl = root(HEAT_RATIO * pl_ * invert(rl))
    cr = root(HEAT_RATIO * pr * invert(rr))
    sl = jnp.minimum(ul - cl, ur - cr)
    sr = jnp.maximum(ul + cl, ur + cr)
    ml = rl * (sl - ul)
    mr = rr * (sr - ur)
    mid = (pr - pl_ + ml * ul - mr * ur) * invert(ml - mr)
    use_left = jnp.maximum(sl, mid) >= 0.0
    rho, v1, v2, v3, p = [jnp.where(use_left, a, b) for a, b in zip(left, right)]
    edge = jnp.where(use_left, sl, sr)
    clip = jnp.where(use_left, jnp.minimum(sl, 0.0), jnp.maximum(sr, 0.0))
    u = (None, v1, v2, v3)[n]
    energy = p * (1.0 / (HEAT_RATIO - 1.0)) + 0.5 * rho * (v1 * v1 + v2 * v2 + v3 * v3)
    gap = invert(jnp.where(clip == 0.0, 1.0, edge - mid))
    ratio = (edge - u) * gap
    star_rho = rho * ratio
    star_energy = ratio * energy + (mid - u) * (star_rho * mid + p * gap)
    mass = rho * u
    f_rho = mass + clip * (star_rho - rho)
    out = [f_rho, f_rho * v1, f_rho * v2, f_rho * v3, None]
    out[n] = mass * u + p + clip * (star_rho * mid - mass)
    out[4] = (energy + p) * u + clip * (star_energy - energy)
    return out


def prep_kernel(
    cons, u_out, w_out, e_bx, o_bx, e_by, o_by, in_bx, in_by, top_out
):
    even_i = lax.axis_index("bx") % 2 == 0
    even_j = lax.axis_index("by") % 2 == 0
    lane = iota(1)
    bit0 = (lane // 16) % 2 == 0
    bit1 = (lane // 32) % 2 == 0
    row = iota(0)
    top = jnp.zeros(TILE, F32)
    for at in range(2):
        low, high, inner = [], [], []
        for h in range(2):
            tiles = []
            for f in range(5):
                x = [cons[f, pl.ds(at * 128 + h * 8 + b, 8, stride=16), :] for b in range(8)]
                if h == 0:
                    low.append(jnp.concatenate([x[0], x[1]], axis=1))
                    inner.append(x[2])
                else:
                    high.append(jnp.concatenate([x[6], x[7]], axis=1))
                    inner[f] = jnp.concatenate([x[5], inner[f]], axis=1)
                y = [jnp.concatenate([x[k], x[k + 4]], axis=1) for k in range(4)]
                z = [None] * 4
                for k in range(2):
                    z[k] = jnp.where(bit1, y[k], pltpu.roll(y[k + 2], 32, 1))
                    z[k + 2] = jnp.where(bit1, pltpu.roll(y[k], 96, 1), y[k + 2])
                t = [None] * 4
                for k in (0, 2):
                    t[k] = jnp.where(bit0, z[k], pltpu.roll(z[k + 1], 16, 1))
                    t[k + 1] = jnp.where(bit0, pltpu.roll(z[k], 112, 1), z[k + 1])
                tiles.append(t)
                for s in range(4):
                    u_out[s, f, at, h] = t[s]
            for s in range(4):
                w, inverse = primitive([tiles[f][s] for f in range(5)])
                speed = (
                    jnp.abs(w[1])
                    + jnp.abs(w[2])
                    + jnp.abs(w[3])
                    + 3.0 * root(HEAT_RATIO * w[4] * inverse)
                )
                top = jnp.maximum(top, speed)
                for f in range(5):
                    w_out[s, f, at, h] = w[f]
        low, _ = primitive(low)
        high, _ = primitive(high)
        inner, _ = primitive(inner)
        for f in range(5):
            e_by[f * 2 + at] = jnp.where(even_j, high[f], low[f])
            o_by[f * 2 + at] = jnp.where(even_j, low[f], high[f])
            in_by[f * 2 + at] = inner[f]
    for f in range(5):
        for h in range(2):
            low = jnp.zeros(TILE, F32)
            high = jnp.zeros(TILE, F32)
            inner = jnp.zeros(TILE, F32)
            for s in range(4):
                here = row // 2 == s
                a, b = w_out[s, f, 0, h], w_out[s, f, 1, h]
                low = jnp.where(here, pltpu.roll(a, 2 * s, 0), low)
                high = jnp.where(here, pltpu.roll(b, (2 * s + 2) % 8, 0), high)
                inner = jnp.where(row == 2 * s, pltpu.roll(b, (2 * s + 3) % 8, 0), inner)
                inner = jnp.where(row == 2 * s + 1, pltpu.roll(a, (2 * s + 7) % 8, 0), inner)
            e_bx[f * 2 + h] = jnp.where(even_i, high, low)
            o_bx[f * 2 + h] = jnp.where(even_i, low, high)
            in_bx[f * 2 + h] = inner
    for ref in (e_by, o_by):
        ref[10] = top
    top_out[0] = top


def make_plan(slots, counts, plan):
    i, j = lax.axis_index("bx"), lax.axis_index("by")
    row = iota(0)
    here = lax.broadcasted_iota(jnp.int32, (8, 32), 1) == jnp.bitwise_xor(
        lax.broadcasted_iota(jnp.int32, (8, 32), 0), j
    )

    def columns(line):
        line = jnp.broadcast_to(line.astype(F32), (8, 32))
        value = jnp.sum(jnp.where(here, line, 0.0), axis=1, keepdims=True)
        return jnp.broadcast_to(value, TILE)

    def across(a, mask):
        for bit in (1, 2, 4):
            if mask & bit:
                a = jnp.where(row & bit == 0, pltpu.roll(a, 8 - bit, 0), pltpu.roll(a, bit, 0))
        return a

    give = [columns(slots[r, pl.ds(i, 1), :]) for r in range(3)]
    loads = [columns(counts[i, pl.ds(k, 1), :]) for k in range(4)]
    def first_round(slot):
        moved = slot == give[0]
        return jnp.where(moved, 1.0, 0.0), jnp.where(moved, across(give[0], 1), slot)

    one, two = first_round(give[1]), first_round(give[2])
    same = give[2] == give[1]
    entries = [give[0], *one, jnp.where(same, 2.0, two[0]), two[1]]
    by_two = [across(one[0], 2) + 2.0, across(one[1], 2)]
    third = [jnp.where(same, a, b) for a, b in zip(by_two, two)]
    by_four = [across(third[0], 4) + 4.0, across(third[1], 4)]
    for slot in range(4):
        here_now = first_round(jnp.full(TILE, slot, F32))
        is_second, is_last = give[1] == float(slot), give[2] == float(slot)
        source, index = [
            jnp.where(is_last, a, jnp.where(is_second, b, c))
            for a, b, c in zip(by_four, by_two, here_now)
        ]
        code = jnp.where(is_last, 3.0, jnp.where(is_second, 2.0, here_now[0]))
        source0 = jnp.broadcast_to(source[0:1], TILE)
        index0 = jnp.broadcast_to(index[0:1], TILE)
        count = jnp.zeros(TILE, F32)
        for k in range(4):
            hit = (row.astype(F32) == source0) & (index0 == float(k))
            count += jnp.where(hit, loads[k], 0.0)
        count = jnp.sum(count, axis=0, keepdims=True)
        entries += [code, index, count]
    entries.append(give[2])
    for e, value in enumerate(entries):
        plan[pl.ds(e, 1), :] = value[0:1].astype(jnp.int32)


def entry(plan, e):
    return plan[pl.ds(e, 1), :][0, 0]


def inner_kernel(slots, counts, w, d, plan, lefts, rights, fluxes):
    make_plan(slots, counts, plan)
    row, lane = iota(0), iota(1)

    def sweep(n, load, down, up, first, last, no_first, no_last):
        left, right = [[], []], [[], []]
        for f in range(5):
            a, b = load(f)
            da, ub = down(a), up(b)
            a_prev, b_prev = da, jnp.where(first, da, down(b))
            a_next, b_next = jnp.where(last, ub, up(a)), ub
            ha = half_minmod(a - a_prev, a_next - a)
            hb = half_minmod(b - b_prev, b_next - b)
            ra, rb = up(a - ha), up(b - hb)
            left[0].append(a + ha)
            left[1].append(b + hb)
            right[0].append(jnp.where(last, rb, ra))
            right[1].append(rb)
        fa = hllc(left[0], right[0], n)
        fb = hllc(left[1], right[1], n)
        out = []
        for f in range(5):
            a = jnp.where(no_first, 0.0, fa[f])
            b = jnp.where(no_last, 0.0, fb[f])
            da = down(a)
            out.append((a - jnp.where(first, 0.0, da), b - jnp.where(first, da, down(b))))
        return out

    def along_first(k, _):
        s, h = k // 2, k % 2
        out = sweep(
            1,
            lambda f: (w[s, f, 0, h], w[s, f, 1, h]),
            lambda a: pltpu.roll(a, 1, 0),
            lambda a: pltpu.roll(a, 7, 0),
            row == 0,
            row == 7,
            row == 0,
            row >= 6,
        )
        for f in range(5):
            d[s, f, 0, h], d[s, f, 1, h] = out[f]
        return 0

    def along_second(k, _):
        s, at = k // 2, k % 2
        out = sweep(
            2,
            lambda f: (w[s, f, at, 0], w[s, f, at, 1]),
            lambda a: pltpu.roll(a, 16, 1),
            lambda a: pltpu.roll(a, 112, 1),
            lane < 16,
            lane >= 112,
            lane < 16,
            lane >= 96,
        )
        for f in range(5):
            d[s, f, at, 0] += out[f][0]
            d[s, f, at, 1] += out[f][1]
        return 0

    first_c, last_c = lane % 16 == 0, lane % 16 == 15

    def previous(here, before):
        return jnp.where(first_c, pltpu.roll(before, 113, 1), pltpu.roll(here, 1, 1))

    def following(here, after):
        return jnp.where(last_c, pltpu.roll(after, 15, 1), pltpu.roll(here, 127, 1))

    def third_states(k, _):
        s, at = k // 2, k % 2
        before, after = (s + 3) % 4, (s + 1) % 4
        for h in range(2):
            for f in range(5):
                a = w[s, f, at, h]
                slope = half_minmod(
                    a - previous(a, w[before, f, at, h]), following(a, w[after, f, at, h]) - a
                )
                lefts[s, f, at, h] = a + slope
                rights[s, f, at, h] = a - slope
        return 0

    def third_fluxes(k, _):
        s, at = k // 2, k % 2
        after = (s + 1) % 4
        for h in range(2):
            out = hllc(
                [lefts[s, f, at, h] for f in range(5)],
                [following(rights[s, f, at, h], rights[after, f, at, h]) for f in range(5)],
                3,
            )
            for f in range(5):
                fluxes[s, f, at, h] = out[f]
        return 0

    def third_change(k, _):
        s, at = k // 2, k % 2
        before = (s + 3) % 4
        for h in range(2):
            for f in range(5):
                a = fluxes[s, f, at, h]
                d[s, f, at, h] += a - previous(a, fluxes[before, f, at, h])
        return 0

    for body in (along_first, along_second, third_states, third_fluxes, third_change):
        unroll = 8 if body in (third_states, third_change) else 4
        lax.fori_loop(0, 8, body, 0, unroll=unroll)


def edge_kernel(
    plan, u, d_in, se_bx, so_bx, se_by, so_by, in_bx, in_by, top, re_bx, ro_bx, re_by, ro_by, top2,
    d, send, top_out, spread, sent,
):
    i, j = lax.axis_index("bx"), lax.axis_index("by")
    even_i, even_j = i % 2 == 0, j % 2 == 0
    row, lane = iota(0), iota(1)

    top = jnp.maximum(jnp.maximum(top[0], top2[0]), jnp.maximum(re_by[10], ro_by[10]))
    top = jnp.broadcast_to(jnp.max(top, axis=0, keepdims=True), TILE)
    for k in range(spread.shape[0]):
        spread[k] = top
    copy = pltpu.make_async_copy(spread, top_out, sent)
    copy.start()

    def faces(n, own_low, own_high, low, high, inner, back, ahead, zero):
        left, right, left2, right2 = [], [], [], []
        for o, q, a, b, w in zip(own_low, own_high, low, high, inner):
            c = jnp.where(zero, ahead(a), back(o))
            left.append(c + half_minmod(c - a, o - c))
            right.append(o - half_minmod(o - c, jnp.where(zero, ahead(o), w) - o))
            e = jnp.where(zero, ahead(q), back(b))
            left2.append(q + half_minmod(q - jnp.where(zero, w, back(q)), e - q))
            right2.append(e - half_minmod(e - q, b - e))
        low_flux = hllc(left, right, n)
        high_flux = hllc(left2, right2, n)
        return (
            [jnp.where(zero, ahead(f) - f, -f) for f in low_flux],
            [jnp.where(zero, f, f - back(f)) for f in high_flux],
        )

    def picked(flag, a, b, index):
        return [jnp.where(flag, a[t], b[t]) for t in range(index, 10, 2)]

    d[...] = d_in[...]
    for h in range(2):
        low, high = faces(
            1,
            picked(even_i, so_bx, se_bx, h),
            picked(even_i, se_bx, so_bx, h),
            picked(even_i, ro_bx, re_bx, h),
            picked(even_i, re_bx, ro_bx, h),
            [in_bx[t] for t in range(h, 10, 2)],
            lambda a: pltpu.roll(a, 1, 0),
            lambda a: pltpu.roll(a, 7, 0),
            row % 2 == 0,
        )
        for f in range(5):
            for s in range(4):
                d[s, f, 0, h] += jnp.where(row < 2, pltpu.roll(low[f], (8 - 2 * s) % 8, 0), 0.0)
                d[s, f, 1, h] += jnp.where(row >= 6, pltpu.roll(high[f], 6 - 2 * s, 0), 0.0)
    for at in range(2):
        turn = lambda a: pltpu.roll(a, 64, 1)
        low, high = faces(
            2,
            picked(even_j, so_by, se_by, at),
            picked(even_j, se_by, so_by, at),
            picked(even_j, ro_by, re_by, at),
            picked(even_j, re_by, ro_by, at),
            [in_by[t] for t in range(at, 10, 2)],
            turn,
            turn,
            lane < 64,
        )
        for f in range(5):
            for s in range(4):
                one = pltpu.roll(low[f], (128 - 16 * s) % 128, 1)
                two = pltpu.roll(low[f], 80 - 16 * s, 1)
                d[s, f, at, 0] += jnp.where(lane < 16, one, jnp.where(lane < 32, two, 0.0))
                one = pltpu.roll(high[f], 96 - 16 * s, 1)
                two = pltpu.roll(high[f], 48 - 16 * s, 1)
                d[s, f, at, 1] += jnp.where(lane >= 112, two, jnp.where(lane >= 96, one, 0.0))

    slot = entry(plan, 0)
    send[0] = u[slot]
    send[1] = d[slot]
    copy.wait()


def relay_kernel(plan, u, d, got1, send_u, send_d):
    code, index = entry(plan, 1), entry(plan, 2)

    @pl.when(code == 0)
    def _():
        send_u[...] = u[index]
        send_d[...] = d[index]

    @pl.when(code == 1)
    def _():
        send_u[...] = got1[0]
        send_d[...] = got1[1]


def pass_kernel(part, plan, own, got1, got2, send):
    code, index = entry(plan, 3), entry(plan, 4)

    @pl.when(code == 0)
    def _():
        send[...] = own[index]

    @pl.when(code == 1)
    def _():
        send[...] = got1[part]

    @pl.when(code == 2)
    def _():
        send[...] = got2[...]


def block_tiles():
    return [(at, h) for at in range(2) for h in range(2)]


def update(out, energy, factor, tick, slot, step, count, u_of, d_of):
    chill = step / count.astype(F32)
    for at, h in block_tiles():
        new = [u_of(f, at, h) - step * d_of(f, at, h) for f in range(5)]
        inverse = invert(new[0])
        squares = new[1] * new[1] + new[2] * new[2] + new[3] * new[3]
        kinetic = 0.5 * squares * inverse
        energy[slot, at, h] = new[4] - kinetic
        factor[slot, at, h] = (HEAT_RATIO - 1.0) * inverse
        tick[slot, at, h] = chill * new[0] * EMISSION_RATE
        new[4] = kinetic
        for f in range(5):
            out[slot, f, pl.ds(8 * at, 8), pl.ds(128 * h, 128)] = new[f]


def cool(out, energy, factor, tick, limits):
    places = [(slot, at, h) for slot in range(len(limits)) for at, h in block_tiles()]
    most = limits[0]
    for limit in limits[1:]:
        most = jnp.maximum(most, limit)

    def advance(k, state):
        after = []
        for now, place in zip(state, places):
            heat = now * factor[place]
            loss = tick[place] * root(jnp.minimum(1.0 + heat * heat, BIG))
            new = now * invert(jnp.minimum(1.0 + loss, BIG))
            after.append(jnp.where(k < limits[place[0]], new, now))
        return tuple(after)

    state = lax.fori_loop(0, most, advance, tuple(energy[place] for place in places))
    for left, (slot, at, h) in zip(state, places):
        place = (slot, 4, pl.ds(8 * at, 8), pl.ds(128 * h, 128))
        out[place] = out[place] + left


def near_kernel(
    plan, u, d, top, got1, got_u, got_d, step_out, result, out, energy, factor, tick, sent, last
):
    speed = jnp.max(jnp.max(top[...], axis=0), axis=0, keepdims=True)
    speed = jnp.max(speed, axis=1, keepdims=True)
    step = COURANT_FACTOR / jnp.broadcast_to(speed, TILE)
    step_out[...] = step
    skipped = entry(plan, 17)
    target = lambda k: k + jnp.where(k >= skipped, 1, 0)

    def load(k, _):
        code, index, count = [entry(plan, 5 + 3 * target(k) + e) for e in range(3)]
        store = lambda *parts: update(out, energy, factor, tick, k, step, count, *parts)

        @pl.when(code == 0)
        def _():
            store(lambda f, at, h: u[index, f, at, h], lambda f, at, h: d[index, f, at, h])

        @pl.when(code == 1)
        def _():
            store(lambda f, at, h: got1[0, f, at, h], lambda f, at, h: got1[1, f, at, h])

        @pl.when(code == 2)
        def _():
            store(lambda f, at, h: got_u[f, at, h], lambda f, at, h: got_d[f, at, h])

        rows = pl.ds(0, 4)
        pltpu.make_async_copy(
            out.at[k, rows], result.at[target(k), rows], sent.at[k]
        ).start()
        return 0

    lax.fori_loop(0, 3, load, 0)
    cool(out, energy, factor, tick, [entry(plan, 7 + 3 * target(k)) for k in range(3)])
    copies = []
    for k in range(3):
        row = pl.ds(4, 1)
        copies.append(
            pltpu.make_async_copy(out.at[k, row], result.at[target(k), row], last.at[k])
        )
        copies[-1].start()
    for k in range(3):
        rows = pl.ds(0, 4)
        pltpu.make_async_copy(out.at[k, rows], result.at[target(k), rows], sent.at[k]).wait()
        copies[k].wait()


def far_kernel(plan, step, got_u, got_d, given, result, out, energy, factor, tick, sent, last):
    slot = entry(plan, 17)
    count = entry(plan, 7 + 3 * slot)
    u_of, d_of = [lambda f, at, h, ref=ref: ref[f, at, h] for ref in (got_u, got_d)]
    update(out, energy, factor, tick, 0, step[...], count, u_of, d_of)
    first = pltpu.make_async_copy(
        out.at[0, pl.ds(0, 4)], result.at[slot, pl.ds(0, 4)], sent
    )
    first.start()
    cool(out, energy, factor, tick, [count])
    second = pltpu.make_async_copy(
        out.at[0, pl.ds(4, 1)], result.at[slot, pl.ds(4, 1)], last
    )
    second.start()
    first.wait()
    second.wait()


def pair_even(count):
    return [(k, k ^ 1) for k in range(count)]


def pair_odd(count):
    return [(k, (k + 1) % count if k % 2 else (k - 1) % count) for k in range(count)]


def call(kernel, inputs, outputs, scratch=(), hbm_in=0, hbm_out=0, plan=0, aliases=None):
    return pl.pallas_call(
        kernel,
        in_specs=[VMEM] * (len(inputs) - hbm_in) + [ANY] * hbm_in,
        out_specs=[VMEM] * (len(outputs) - hbm_out) + [ANY] * hbm_out + [VMEM] * plan,
        out_shape=[shape(*dims) for dims in outputs] + [PLAN] * plan,
        scratch_shapes=[pltpu.VMEM(x, F32) if isinstance(x, tuple) else x for x in scratch],
        compiler_params=PARAMS,
        input_output_aliases=aliases or {},
    )(*inputs)


def on_device(conserved, cool_steps, swap_slot):
    rows, columns = lax.axis_size("bx"), lax.axis_size("by")
    slots = swap_slot.transpose(2, 0, 1)
    counts = cool_steps.transpose(0, 2, 1)
    face = (10,) + TILE
    u, w, *slabs = call(
        prep_kernel,
        [conserved.reshape(5, 256, 64)],
        [BLOCKS] * 2
        + [(10,) + TILE, (12,) + TILE, (11,) + TILE, (14,) + TILE]
        + [face] * 2
        + [(13,) + TILE],
    )
    e_bx, o_bx, e_by, o_by = slabs[:4]
    got_slabs = [
        lax.ppermute(e_bx, "bx", pair_even(rows)),
        lax.ppermute(o_bx, "bx", pair_odd(rows)),
        lax.ppermute(e_by, "by", pair_even(columns)),
        lax.ppermute(o_by, "by", pair_odd(columns)),
        lax.ppermute(slabs[-1], "by", [(k, k ^ 2) for k in range(columns)]),
    ]
    d, plan = call(inner_kernel, [slots, counts, w], [BLOCKS], [BLOCKS] * 3, plan=1)
    groups = [
        [i * columns + j for i in range(rows) for j in range(x, columns, 4)] for x in range(4)
    ]
    size = len(groups[0])
    chunks = (size * 3 // 8,) + TILE
    d, send, top = call(
        edge_kernel,
        [plan, u, d, *slabs, *got_slabs],
        [BLOCKS, TRAVEL, chunks],
        [chunks, pltpu.SemaphoreType.DMA],
        hbm_out=1,
    )
    trade = lambda m, block: lax.ppermute(block, "by", [(k, k ^ m) for k in range(columns)])
    got1 = trade(1, send)
    top = top.reshape(size, 3, 1, 128)
    top = lax.all_to_all(top, ("bx", "by"), 0, 0, axis_index_groups=groups)
    top = top.reshape(chunks)
    sends = call(relay_kernel, [plan, u, d, got1], [HALF] * 2)
    got2 = [trade(2, send) for send in sends]
    got4 = []
    for part, own in enumerate((u, d)):
        kernel = functools.partial(pass_kernel, part)
        (send,) = call(kernel, [plan, own, got1, got2[part]], [HALF])
        got4.append(trade(4, send))
    block = (5, 16, 256)
    state = (2, 2) + TILE
    step, result = call(
        near_kernel,
        [plan, u, d, top, got1, *got2],
        [TILE, (4,) + block],
        [(3,) + block] + [(3,) + state] * 3 + [pltpu.SemaphoreType.DMA((3,))] * 2,
        hbm_out=1,
    )
    (result,) = call(
        far_kernel,
        [plan, step, *got4, result],
        [(4,) + block],
        [(1,) + block] + [(1,) + state] * 3 + [pltpu.SemaphoreType.DMA] * 2,
        hbm_in=1,
        hbm_out=1,
        aliases={4: 0},
    )
    return result.reshape((1, 1) + result.shape)


def solution(mesh):
    in_specs = (P(None, "bx", "by", None), P(), P())
    out_specs = P("bx", "by", None, None, None, None)
    return jax.shard_map(
        on_device, mesh=mesh, in_specs=in_specs, out_specs=out_specs, check_vma=False
    )
```

```python
import functools

import jax
import jax.numpy as jnp
from jax import lax
from jax.experimental import pallas as pl
from jax.experimental.pallas import tpu as pltpu
from jax.sharding import PartitionSpec as P

HEAT_RATIO = 5.0 / 3.0
COURANT_FACTOR = 0.4
EMISSION_RATE = 100.0
F32 = jnp.float32
TILE = (8, 128)
BLOCKS = (4, 5, 2, 2) + TILE
TRAVEL = (2, 5, 2, 2) + TILE
HALF = (5, 2, 2) + TILE
VMEM = pl.BlockSpec(memory_space=pltpu.VMEM)
ANY = pl.BlockSpec(memory_space=pl.ANY)
PARAMS = pltpu.CompilerParams(vmem_limit_bytes=16 * 1024 * 1024)
PLAN = jax.ShapeDtypeStruct((24, 128), jnp.int32)
BIG = 3e38
SMALL = 1e-37


def shape(*dims):
    return jax.ShapeDtypeStruct(dims, F32)


def iota(axis):
    return lax.broadcasted_iota(jnp.int32, TILE, axis)


def invert(x):
    return pl.reciprocal(x, approx=True)


def root(x):
    x = jnp.maximum(x, SMALL)
    return x * lax.rsqrt(x)


def half_minmod(a, b):
    return 0.5 * jnp.maximum(jnp.minimum(a, b), jnp.minimum(jnp.maximum(a, b), 0.0))


def primitive(u):
    inverse = invert(u[0])
    v1, v2, v3 = u[1] * inverse, u[2] * inverse, u[3] * inverse
    p = (HEAT_RATIO - 1.0) * (u[4] - 0.5 * u[0] * (v1 * v1 + v2 * v2 + v3 * v3))
    return [u[0], v1, v2, v3, p], inverse


def hllc(left, right, n):
    rl, ul, pl_ = left[0], left[n], left[4]
    rr, ur, pr = right[0], right[n], right[4]
    cl = root(HEAT_RATIO * pl_ * invert(rl))
    cr = root(HEAT_RATIO * pr * invert(rr))
    sl = jnp.minimum(ul - cl, ur - cr)
    sr = jnp.maximum(ul + cl, ur + cr)
    ml = rl * (sl - ul)
    mr = rr * (sr - ur)
    mid = (pr - pl_ + ml * ul - mr * ur) * invert(ml - mr)
    use_left = jnp.maximum(sl, mid) >= 0.0
    rho, v1, v2, v3, p = [jnp.where(use_left, a, b) for a, b in zip(left, right)]
    edge = jnp.where(use_left, sl, sr)
    clip = jnp.where(use_left, jnp.minimum(sl, 0.0), jnp.maximum(sr, 0.0))
    u = (None, v1, v2, v3)[n]
    energy = p * (1.0 / (HEAT_RATIO - 1.0)) + 0.5 * rho * (v1 * v1 + v2 * v2 + v3 * v3)
    gap = invert(jnp.where(clip == 0.0, 1.0, edge - mid))
    ratio = (edge - u) * gap
    star_rho = rho * ratio
    star_energy = ratio * energy + (mid - u) * (star_rho * mid + p * gap)
    mass = rho * u
    f_rho = mass + clip * (star_rho - rho)
    out = [f_rho, f_rho * v1, f_rho * v2, f_rho * v3, None]
    out[n] = mass * u + p + clip * (star_rho * mid - mass)
    out[4] = (energy + p) * u + clip * (star_energy - energy)
    return out


def prep_kernel(
    cons, u_out, w_out, e_bx, o_bx, e_by, o_by, in_bx, in_by, top_out
):
    even_i = lax.axis_index("bx") % 2 == 0
    even_j = lax.axis_index("by") % 2 == 0
    lane = iota(1)
    bit0 = (lane // 16) % 2 == 0
    bit1 = (lane // 32) % 2 == 0
    row = iota(0)
    top = jnp.zeros(TILE, F32)
    for at in range(2):
        low, high, inner = [], [], []
        for h in range(2):
            tiles = []
            for f in range(5):
                x = [cons[f, pl.ds(at * 128 + h * 8 + b, 8, stride=16), :] for b in range(8)]
                if h == 0:
                    low.append(jnp.concatenate([x[0], x[1]], axis=1))
                    inner.append(x[2])
                else:
                    high.append(jnp.concatenate([x[6], x[7]], axis=1))
                    inner[f] = jnp.concatenate([x[5], inner[f]], axis=1)
                y = [jnp.concatenate([x[k], x[k + 4]], axis=1) for k in range(4)]
                z = [None] * 4
                for k in range(2):
                    z[k] = jnp.where(bit1, y[k], pltpu.roll(y[k + 2], 32, 1))
                    z[k + 2] = jnp.where(bit1, pltpu.roll(y[k], 96, 1), y[k + 2])
                t = [None] * 4
                for k in (0, 2):
                    t[k] = jnp.where(bit0, z[k], pltpu.roll(z[k + 1], 16, 1))
                    t[k + 1] = jnp.where(bit0, pltpu.roll(z[k], 112, 1), z[k + 1])
                tiles.append(t)
                for s in range(4):
                    u_out[s, f, at, h] = t[s]
            for s in range(4):
                w, inverse = primitive([tiles[f][s] for f in range(5)])
                speed = (
                    jnp.abs(w[1])
                    + jnp.abs(w[2])
                    + jnp.abs(w[3])
                    + 3.0 * root(HEAT_RATIO * w[4] * inverse)
                )
                top = jnp.maximum(top, speed)
                for f in range(5):
                    w_out[s, f, at, h] = w[f]
        low, _ = primitive(low)
        high, _ = primitive(high)
        inner, _ = primitive(inner)
        for f in range(5):
            e_by[f * 2 + at] = jnp.where(even_j, high[f], low[f])
            o_by[f * 2 + at] = jnp.where(even_j, low[f], high[f])
            in_by[f * 2 + at] = inner[f]
    for f in range(5):
        for h in range(2):
            low = jnp.zeros(TILE, F32)
            high = jnp.zeros(TILE, F32)
            inner = jnp.zeros(TILE, F32)
            for s in range(4):
                here = row // 2 == s
                a, b = w_out[s, f, 0, h], w_out[s, f, 1, h]
                low = jnp.where(here, pltpu.roll(a, 2 * s, 0), low)
                high = jnp.where(here, pltpu.roll(b, (2 * s + 2) % 8, 0), high)
                inner = jnp.where(row == 2 * s, pltpu.roll(b, (2 * s + 3) % 8, 0), inner)
                inner = jnp.where(row == 2 * s + 1, pltpu.roll(a, (2 * s + 7) % 8, 0), inner)
            e_bx[f * 2 + h] = jnp.where(even_i, high, low)
            o_bx[f * 2 + h] = jnp.where(even_i, low, high)
            in_bx[f * 2 + h] = inner
    for ref in (e_by, o_by):
        ref[10] = top
    top_out[0] = top


def make_plan(slots, counts, plan):
    i, j = lax.axis_index("bx"), lax.axis_index("by")
    row = iota(0)
    here = lax.broadcasted_iota(jnp.int32, (8, 32), 1) == jnp.bitwise_xor(
        lax.broadcasted_iota(jnp.int32, (8, 32), 0), j
    )

    def columns(line):
        line = jnp.broadcast_to(line.astype(F32), (8, 32))
        value = jnp.sum(jnp.where(here, line, 0.0), axis=1, keepdims=True)
        return jnp.broadcast_to(value, TILE)

    def across(a, mask):
        for bit in (1, 2, 4):
            if mask & bit:
                a = jnp.where(row & bit == 0, pltpu.roll(a, 8 - bit, 0), pltpu.roll(a, bit, 0))
        return a

    give = [columns(slots[r, pl.ds(i, 1), :]) for r in range(3)]
    loads = [columns(counts[i, pl.ds(k, 1), :]) for k in range(4)]
    def first_round(slot):
        moved = slot == give[0]
        return jnp.where(moved, 1.0, 0.0), jnp.where(moved, across(give[0], 1), slot)

    one, two = first_round(give[1]), first_round(give[2])
    same = give[2] == give[1]
    entries = [give[0], *one, jnp.where(same, 2.0, two[0]), two[1]]
    by_two = [across(one[0], 2) + 2.0, across(one[1], 2)]
    third = [jnp.where(same, a, b) for a, b in zip(by_two, two)]
    by_four = [across(third[0], 4) + 4.0, across(third[1], 4)]
    for slot in range(4):
        here_now = first_round(jnp.full(TILE, slot, F32))
        is_second, is_last = give[1] == float(slot), give[2] == float(slot)
        source, index = [
            jnp.where(is_last, a, jnp.where(is_second, b, c))
            for a, b, c in zip(by_four, by_two, here_now)
        ]
        code = jnp.where(is_last, 3.0, jnp.where(is_second, 2.0, here_now[0]))
        source0 = jnp.broadcast_to(source[0:1], TILE)
        index0 = jnp.broadcast_to(index[0:1], TILE)
        count = jnp.zeros(TILE, F32)
        for k in range(4):
            hit = (row.astype(F32) == source0) & (index0 == float(k))
            count += jnp.where(hit, loads[k], 0.0)
        count = jnp.sum(count, axis=0, keepdims=True)
        entries += [code, index, count]
    entries.append(give[2])
    for e, value in enumerate(entries):
        plan[pl.ds(e, 1), :] = value[0:1].astype(jnp.int32)


def entry(plan, e):
    return plan[pl.ds(e, 1), :][0, 0]


def inner_kernel(slots, counts, w, d, plan, lefts, rights, fluxes):
    make_plan(slots, counts, plan)
    row, lane = iota(0), iota(1)

    def sweep(n, load, down, up, first, last, no_first, no_last):
        left, right = [[], []], [[], []]
        for f in range(5):
            a, b = load(f)
            da, ub = down(a), up(b)
            a_prev, b_prev = da, jnp.where(first, da, down(b))
            a_next, b_next = jnp.where(last, ub, up(a)), ub
            ha = half_minmod(a - a_prev, a_next - a)
            hb = half_minmod(b - b_prev, b_next - b)
            ra, rb = up(a - ha), up(b - hb)
            left[0].append(a + ha)
            left[1].append(b + hb)
            right[0].append(jnp.where(last, rb, ra))
            right[1].append(rb)
        fa = hllc(left[0], right[0], n)
        fb = hllc(left[1], right[1], n)
        out = []
        for f in range(5):
            a = jnp.where(no_first, 0.0, fa[f])
            b = jnp.where(no_last, 0.0, fb[f])
            da = down(a)
            out.append((a - jnp.where(first, 0.0, da), b - jnp.where(first, da, down(b))))
        return out

    def along_first(k, _):
        s, h = k // 2, k % 2
        out = sweep(
            1,
            lambda f: (w[s, f, 0, h], w[s, f, 1, h]),
            lambda a: pltpu.roll(a, 1, 0),
            lambda a: pltpu.roll(a, 7, 0),
            row == 0,
            row == 7,
            row == 0,
            row >= 6,
        )
        for f in range(5):
            d[s, f, 0, h], d[s, f, 1, h] = out[f]
        return 0

    def along_second(k, _):
        s, at = k // 2, k % 2
        out = sweep(
            2,
            lambda f: (w[s, f, at, 0], w[s, f, at, 1]),
            lambda a: pltpu.roll(a, 16, 1),
            lambda a: pltpu.roll(a, 112, 1),
            lane < 16,
            lane >= 112,
            lane < 16,
            lane >= 96,
        )
        for f in range(5):
            d[s, f, at, 0] += out[f][0]
            d[s, f, at, 1] += out[f][1]
        return 0

    first_c, last_c = lane % 16 == 0, lane % 16 == 15

    def previous(here, before):
        return jnp.where(first_c, pltpu.roll(before, 113, 1), pltpu.roll(here, 1, 1))

    def following(here, after):
        return jnp.where(last_c, pltpu.roll(after, 15, 1), pltpu.roll(here, 127, 1))

    def third_states(k, _):
        s, at = k // 2, k % 2
        before, after = (s + 3) % 4, (s + 1) % 4
        for h in range(2):
            for f in range(5):
                a = w[s, f, at, h]
                slope = half_minmod(
                    a - previous(a, w[before, f, at, h]), following(a, w[after, f, at, h]) - a
                )
                lefts[s, f, at, h] = a + slope
                rights[s, f, at, h] = a - slope
        return 0

    def third_fluxes(k, _):
        s, at = k // 2, k % 2
        after = (s + 1) % 4
        for h in range(2):
            out = hllc(
                [lefts[s, f, at, h] for f in range(5)],
                [following(rights[s, f, at, h], rights[after, f, at, h]) for f in range(5)],
                3,
            )
            for f in range(5):
                fluxes[s, f, at, h] = out[f]
        return 0

    def third_change(k, _):
        s, at = k // 2, k % 2
        before = (s + 3) % 4
        for h in range(2):
            for f in range(5):
                a = fluxes[s, f, at, h]
                d[s, f, at, h] += a - previous(a, fluxes[before, f, at, h])
        return 0

    for body in (along_first, along_second, third_states, third_fluxes, third_change):
        unroll = 8 if body in (third_states, third_change) else 4
        lax.fori_loop(0, 8, body, 0, unroll=unroll)


def edge_kernel(
    plan, u, d_in, se_bx, so_bx, se_by, so_by, in_bx, in_by, top, re_bx, ro_bx, re_by, ro_by, top2,
    d, send, top_out, spread, sent,
):
    i, j = lax.axis_index("bx"), lax.axis_index("by")
    even_i, even_j = i % 2 == 0, j % 2 == 0
    row, lane = iota(0), iota(1)

    top = jnp.maximum(jnp.maximum(top[0], top2[0]), jnp.maximum(re_by[10], ro_by[10]))
    top = jnp.broadcast_to(jnp.max(top, axis=0, keepdims=True), TILE)
    for k in range(spread.shape[0]):
        spread[k] = top
    copy = pltpu.make_async_copy(spread, top_out, sent)
    copy.start()

    def faces(n, own_low, own_high, low, high, inner, back, ahead, zero):
        left, right, left2, right2 = [], [], [], []
        for o, q, a, b, w in zip(own_low, own_high, low, high, inner):
            c = jnp.where(zero, ahead(a), back(o))
            left.append(c + half_minmod(c - a, o - c))
            right.append(o - half_minmod(o - c, jnp.where(zero, ahead(o), w) - o))
            e = jnp.where(zero, ahead(q), back(b))
            left2.append(q + half_minmod(q - jnp.where(zero, w, back(q)), e - q))
            right2.append(e - half_minmod(e - q, b - e))
        low_flux = hllc(left, right, n)
        high_flux = hllc(left2, right2, n)
        return (
            [jnp.where(zero, ahead(f) - f, -f) for f in low_flux],
            [jnp.where(zero, f, f - back(f)) for f in high_flux],
        )

    def picked(flag, a, b, index):
        return [jnp.where(flag, a[t], b[t]) for t in range(index, 10, 2)]

    d[...] = d_in[...]
    for h in range(2):
        low, high = faces(
            1,
            picked(even_i, so_bx, se_bx, h),
            picked(even_i, se_bx, so_bx, h),
            picked(even_i, ro_bx, re_bx, h),
            picked(even_i, re_bx, ro_bx, h),
            [in_bx[t] for t in range(h, 10, 2)],
            lambda a: pltpu.roll(a, 1, 0),
            lambda a: pltpu.roll(a, 7, 0),
            row % 2 == 0,
        )
        for f in range(5):
            for s in range(4):
                d[s, f, 0, h] += jnp.where(row < 2, pltpu.roll(low[f], (8 - 2 * s) % 8, 0), 0.0)
                d[s, f, 1, h] += jnp.where(row >= 6, pltpu.roll(high[f], 6 - 2 * s, 0), 0.0)
    for at in range(2):
        turn = lambda a: pltpu.roll(a, 64, 1)
        low, high = faces(
            2,
            picked(even_j, so_by, se_by, at),
            picked(even_j, se_by, so_by, at),
            picked(even_j, ro_by, re_by, at),
            picked(even_j, re_by, ro_by, at),
            [in_by[t] for t in range(at, 10, 2)],
            turn,
            turn,
            lane < 64,
        )
        for f in range(5):
            for s in range(4):
                one = pltpu.roll(low[f], (128 - 16 * s) % 128, 1)
                two = pltpu.roll(low[f], 80 - 16 * s, 1)
                d[s, f, at, 0] += jnp.where(lane < 16, one, jnp.where(lane < 32, two, 0.0))
                one = pltpu.roll(high[f], 96 - 16 * s, 1)
                two = pltpu.roll(high[f], 48 - 16 * s, 1)
                d[s, f, at, 1] += jnp.where(lane >= 112, two, jnp.where(lane >= 96, one, 0.0))

    slot = entry(plan, 0)
    send[0] = u[slot]
    send[1] = d[slot]
    copy.wait()


def relay_kernel(plan, u, d, got1, send_u, send_d):
    code, index = entry(plan, 1), entry(plan, 2)

    @pl.when(code == 0)
    def _():
        send_u[...] = u[index]
        send_d[...] = d[index]

    @pl.when(code == 1)
    def _():
        send_u[...] = got1[0]
        send_d[...] = got1[1]


def pass_kernel(part, plan, own, got1, got2, send):
    code, index = entry(plan, 3), entry(plan, 4)

    @pl.when(code == 0)
    def _():
        send[...] = own[index]

    @pl.when(code == 1)
    def _():
        send[...] = got1[part]

    @pl.when(code == 2)
    def _():
        send[...] = got2[...]


def block_tiles():
    return [(at, h) for at in range(2) for h in range(2)]


def update(out, energy, factor, tick, slot, step, count, u_of, d_of):
    chill = step / count.astype(F32)
    for at, h in block_tiles():
        new = [u_of(f, at, h) - step * d_of(f, at, h) for f in range(5)]
        inverse = invert(new[0])
        squares = new[1] * new[1] + new[2] * new[2] + new[3] * new[3]
        kinetic = 0.5 * squares * inverse
        energy[slot, at, h] = new[4] - kinetic
        factor[slot, at, h] = (HEAT_RATIO - 1.0) * inverse
        tick[slot, at, h] = chill * new[0] * EMISSION_RATE
        new[4] = kinetic
        for f in range(5):
            out[slot, f, pl.ds(8 * at, 8), pl.ds(128 * h, 128)] = new[f]


def cool(out, energy, factor, tick, limits):
    places = [(slot, at, h) for slot in range(len(limits)) for at, h in block_tiles()]
    most = limits[0]
    for limit in limits[1:]:
        most = jnp.maximum(most, limit)

    def advance(k, state):
        after = []
        for now, place in zip(state, places):
            heat = now * factor[place]
            loss = tick[place] * root(jnp.minimum(1.0 + heat * heat, BIG))
            new = now * invert(jnp.minimum(1.0 + loss, BIG))
            after.append(jnp.where(k < limits[place[0]], new, now))
        return tuple(after)

    state = lax.fori_loop(0, most, advance, tuple(energy[place] for place in places))
    for left, (slot, at, h) in zip(state, places):
        place = (slot, 4, pl.ds(8 * at, 8), pl.ds(128 * h, 128))
        out[place] = out[place] + left


def near_kernel(
    plan, u, d, top, got1, got_u, got_d, step_out, result, out, energy, factor, tick, sent, last
):
    speed = jnp.max(jnp.max(top[...], axis=0), axis=0, keepdims=True)
    speed = jnp.max(speed, axis=1, keepdims=True)
    step = COURANT_FACTOR / jnp.broadcast_to(speed, TILE)
    step_out[...] = step
    skipped = entry(plan, 17)
    target = lambda k: k + jnp.where(k >= skipped, 1, 0)

    def load(k, _):
        code, index, count = [entry(plan, 5 + 3 * target(k) + e) for e in range(3)]
        store = lambda *parts: update(out, energy, factor, tick, k, step, count, *parts)

        @pl.when(code == 0)
        def _():
            store(lambda f, at, h: u[index, f, at, h], lambda f, at, h: d[index, f, at, h])

        @pl.when(code == 1)
        def _():
            store(lambda f, at, h: got1[0, f, at, h], lambda f, at, h: got1[1, f, at, h])

        @pl.when(code == 2)
        def _():
            store(lambda f, at, h: got_u[f, at, h], lambda f, at, h: got_d[f, at, h])

        rows = pl.ds(0, 4)
        pltpu.make_async_copy(
            out.at[k, rows], result.at[target(k), rows], sent.at[k]
        ).start()
        return 0

    lax.fori_loop(0, 3, load, 0)
    cool(out, energy, factor, tick, [entry(plan, 7 + 3 * target(k)) for k in range(3)])
    copies = []
    for k in range(3):
        row = pl.ds(4, 1)
        copies.append(
            pltpu.make_async_copy(out.at[k, row], result.at[target(k), row], last.at[k])
        )
        copies[-1].start()
    for k in range(3):
        rows = pl.ds(0, 4)
        pltpu.make_async_copy(out.at[k, rows], result.at[target(k), rows], sent.at[k]).wait()
        copies[k].wait()


def far_kernel(plan, step, got_u, got_d, given, result, out, energy, factor, tick, sent, last):
    slot = entry(plan, 17)
    count = entry(plan, 7 + 3 * slot)
    u_of, d_of = [lambda f, at, h, ref=ref: ref[f, at, h] for ref in (got_u, got_d)]
    update(out, energy, factor, tick, 0, step[...], count, u_of, d_of)
    first = pltpu.make_async_copy(
        out.at[0, pl.ds(0, 4)], result.at[slot, pl.ds(0, 4)], sent
    )
    first.start()
    cool(out, energy, factor, tick, [count])
    second = pltpu.make_async_copy(
        out.at[0, pl.ds(4, 1)], result.at[slot, pl.ds(4, 1)], last
    )
    second.start()
    first.wait()
    second.wait()


def pair_even(count):
    return [(k, k ^ 1) for k in range(count)]


def pair_odd(count):
    return [(k, (k + 1) % count if k % 2 else (k - 1) % count) for k in range(count)]


def call(kernel, inputs, outputs, scratch=(), hbm_in=0, hbm_out=0, plan=0, aliases=None):
    return pl.pallas_call(
        kernel,
        in_specs=[VMEM] * (len(inputs) - hbm_in) + [ANY] * hbm_in,
        out_specs=[VMEM] * (len(outputs) - hbm_out) + [ANY] * hbm_out + [VMEM] * plan,
        out_shape=[shape(*dims) for dims in outputs] + [PLAN] * plan,
        scratch_shapes=[pltpu.VMEM(x, F32) if isinstance(x, tuple) else x for x in scratch],
        compiler_params=PARAMS,
        input_output_aliases=aliases or {},
    )(*inputs)


def on_device(conserved, cool_steps, swap_slot):
    rows, columns = lax.axis_size("bx"), lax.axis_size("by")
    slots = swap_slot.transpose(2, 0, 1)
    counts = cool_steps.transpose(0, 2, 1)
    face = (10,) + TILE
    u, w, *slabs = call(
        prep_kernel,
        [conserved.reshape(5, 256, 64)],
        [BLOCKS] * 2
        + [(10,) + TILE, (13,) + TILE, (11,) + TILE, (14,) + TILE]
        + [face] * 2
        + [(12,) + TILE],
    )
    e_bx, o_bx, e_by, o_by = slabs[:4]
    got_slabs = [
        lax.ppermute(e_bx, "bx", pair_even(rows)),
        lax.ppermute(o_bx, "bx", pair_odd(rows)),
        lax.ppermute(e_by, "by", pair_even(columns)),
        lax.ppermute(o_by, "by", pair_odd(columns)),
        lax.ppermute(slabs[-1], "by", [(k, k ^ 2) for k in range(columns)]),
    ]
    d, plan = call(inner_kernel, [slots, counts, w], [BLOCKS], [BLOCKS] * 3, plan=1)
    groups = [
        [i * columns + j for i in range(rows) for j in range(x, columns, 4)] for x in range(4)
    ]
    size = len(groups[0])
    chunks = (size * 3 // 8,) + TILE
    d, send, top = call(
        edge_kernel,
        [plan, u, d, *slabs, *got_slabs],
        [BLOCKS, TRAVEL, chunks],
        [chunks, pltpu.SemaphoreType.DMA],
        hbm_out=1,
    )
    trade = lambda m, block: lax.ppermute(block, "by", [(k, k ^ m) for k in range(columns)])
    got1 = trade(1, send)
    top = top.reshape(size, 3, 1, 128)
    top = lax.all_to_all(top, ("bx", "by"), 0, 0, axis_index_groups=groups)
    top = top.reshape(chunks)
    sends = call(relay_kernel, [plan, u, d, got1], [HALF] * 2)
    got2 = [trade(2, send) for send in sends]
    got4 = []
    for part, own in enumerate((u, d)):
        kernel = functools.partial(pass_kernel, part)
        (send,) = call(kernel, [plan, own, got1, got2[part]], [HALF])
        got4.append(trade(4, send))
    block = (5, 16, 256)
    state = (2, 2) + TILE
    step, result = call(
        near_kernel,
        [plan, u, d, top, got1, *got2],
        [TILE, (4,) + block],
        [(3,) + block] + [(3,) + state] * 3 + [pltpu.SemaphoreType.DMA((3,))] * 2,
        hbm_out=1,
    )
    (result,) = call(
        far_kernel,
        [plan, step, *got4, result],
        [(4,) + block],
        [(1,) + block] + [(1,) + state] * 3 + [pltpu.SemaphoreType.DMA] * 2,
        hbm_in=1,
        hbm_out=1,
        aliases={4: 0},
    )
    return result.reshape((1, 1) + result.shape)


def solution(mesh):
    in_specs = (P(None, "bx", "by", None), P(), P())
    out_specs = P("bx", "by", None, None, None, None)
    return jax.shard_map(
        on_device, mesh=mesh, in_specs=in_specs, out_specs=out_specs, check_vma=False
    )
```

```python
import functools

import jax
import jax.numpy as jnp
from jax import lax
from jax.experimental import pallas as pl
from jax.experimental.pallas import tpu as pltpu
from jax.sharding import PartitionSpec as P

HEAT_RATIO = 5.0 / 3.0
COURANT_FACTOR = 0.4
EMISSION_RATE = 100.0
F32 = jnp.float32
TILE = (8, 128)
BLOCKS = (4, 5, 2, 2) + TILE
TRAVEL = (2, 5, 2, 2) + TILE
HALF = (5, 2, 2) + TILE
VMEM = pl.BlockSpec(memory_space=pltpu.VMEM)
ANY = pl.BlockSpec(memory_space=pl.ANY)
PLAN = jax.ShapeDtypeStruct((24, 128), jnp.int32)
BIG = 3e38
SMALL = 1e-37


def shape(*dims):
    return jax.ShapeDtypeStruct(dims, F32)


def iota(axis):
    return lax.broadcasted_iota(jnp.int32, TILE, axis)


def invert(x):
    return pl.reciprocal(x, approx=True)


def root(x):
    x = jnp.maximum(x, SMALL)
    return x * lax.rsqrt(x)


def half_minmod(a, b):
    return 0.5 * jnp.maximum(jnp.minimum(a, b), jnp.minimum(jnp.maximum(a, b), 0.0))


def primitive(u):
    inverse = invert(u[0])
    v1, v2, v3 = u[1] * inverse, u[2] * inverse, u[3] * inverse
    p = (HEAT_RATIO - 1.0) * (u[4] - 0.5 * u[0] * (v1 * v1 + v2 * v2 + v3 * v3))
    return [u[0], v1, v2, v3, p], inverse


def hllc(left, right, n):
    rl, ul, pl_ = left[0], left[n], left[4]
    rr, ur, pr = right[0], right[n], right[4]
    cl = root(HEAT_RATIO * pl_ * invert(rl))
    cr = root(HEAT_RATIO * pr * invert(rr))
    sl = jnp.minimum(ul - cl, ur - cr)
    sr = jnp.maximum(ul + cl, ur + cr)
    ml = rl * (sl - ul)
    mr = rr * (sr - ur)
    mid = (pr - pl_ + ml * ul - mr * ur) * invert(ml - mr)
    use_left = jnp.maximum(sl, mid) >= 0.0
    rho, v1, v2, v3, p = [jnp.where(use_left, a, b) for a, b in zip(left, right)]
    edge = jnp.where(use_left, sl, sr)
    clip = jnp.where(use_left, jnp.minimum(sl, 0.0), jnp.maximum(sr, 0.0))
    u = (None, v1, v2, v3)[n]
    energy = p * (1.0 / (HEAT_RATIO - 1.0)) + 0.5 * rho * (v1 * v1 + v2 * v2 + v3 * v3)
    gap = invert(jnp.where(clip == 0.0, 1.0, edge - mid))
    ratio = (edge - u) * gap
    star_rho = rho * ratio
    star_energy = ratio * energy + (mid - u) * (star_rho * mid + p * gap)
    mass = rho * u
    f_rho = mass + clip * (star_rho - rho)
    out = [f_rho, f_rho * v1, f_rho * v2, f_rho * v3, None]
    out[n] = mass * u + p + clip * (star_rho * mid - mass)
    out[4] = (energy + p) * u + clip * (star_energy - energy)
    return out


def prep_kernel(
    source, u_out, w_out, e_bx, o_bx, e_by, o_by, in_bx, in_by, top_out, cons, arrived
):
    copies = []
    for at in range(2):
        for f in range(5):
            place = (f, pl.ds(at * 128, 128))
            copies.append(
                pltpu.make_async_copy(source.at[place], cons.at[place], arrived.at[at, f])
            )
            copies[-1].start()
    even_i = lax.axis_index("bx") % 2 == 0
    even_j = lax.axis_index("by") % 2 == 0
    lane = iota(1)
    bit0 = (lane // 16) % 2 == 0
    bit1 = (lane // 32) % 2 == 0
    row = iota(0)
    top = jnp.zeros(TILE, F32)
    for at in range(2):
        for copy in copies[at * 5 : at * 5 + 5]:
            copy.wait()
        low, high, inner = [], [], []
        for h in range(2):
            tiles = []
            for f in range(5):
                x = [cons[f, pl.ds(at * 128 + h * 8 + b, 8, stride=16), :] for b in range(8)]
                if h == 0:
                    low.append(jnp.concatenate([x[0], x[1]], axis=1))
                    inner.append(x[2])
                else:
                    high.append(jnp.concatenate([x[6], x[7]], axis=1))
                    inner[f] = jnp.concatenate([x[5], inner[f]], axis=1)
                y = [jnp.concatenate([x[k], x[k + 4]], axis=1) for k in range(4)]
                z = [None] * 4
                for k in range(2):
                    z[k] = jnp.where(bit1, y[k], pltpu.roll(y[k + 2], 32, 1))
                    z[k + 2] = jnp.where(bit1, pltpu.roll(y[k], 96, 1), y[k + 2])
                t = [None] * 4
                for k in (0, 2):
                    t[k] = jnp.where(bit0, z[k], pltpu.roll(z[k + 1], 16, 1))
                    t[k + 1] = jnp.where(bit0, pltpu.roll(z[k], 112, 1), z[k + 1])
                tiles.append(t)
                for s in range(4):
                    u_out[s, f, at, h] = t[s]
            for s in range(4):
                w, inverse = primitive([tiles[f][s] for f in range(5)])
                speed = (
                    jnp.abs(w[1])
                    + jnp.abs(w[2])
                    + jnp.abs(w[3])
                    + 3.0 * root(HEAT_RATIO * w[4] * inverse)
                )
                top = jnp.maximum(top, speed)
                for f in range(5):
                    w_out[s, f, at, h] = w[f]
        low, _ = primitive(low)
        high, _ = primitive(high)
        inner, _ = primitive(inner)
        for f in range(5):
            e_by[f * 2 + at] = jnp.where(even_j, high[f], low[f])
            o_by[f * 2 + at] = jnp.where(even_j, low[f], high[f])
            in_by[f * 2 + at] = inner[f]
    for f in range(5):
        for h in range(2):
            low = jnp.zeros(TILE, F32)
            high = jnp.zeros(TILE, F32)
            inner = jnp.zeros(TILE, F32)
            for s in range(4):
                here = row // 2 == s
                a, b = w_out[s, f, 0, h], w_out[s, f, 1, h]
                low = jnp.where(here, pltpu.roll(a, 2 * s, 0), low)
                high = jnp.where(here, pltpu.roll(b, (2 * s + 2) % 8, 0), high)
                inner = jnp.where(row == 2 * s, pltpu.roll(b, (2 * s + 3) % 8, 0), inner)
                inner = jnp.where(row == 2 * s + 1, pltpu.roll(a, (2 * s + 7) % 8, 0), inner)
            e_bx[f * 2 + h] = jnp.where(even_i, high, low)
            o_bx[f * 2 + h] = jnp.where(even_i, low, high)
            in_bx[f * 2 + h] = inner
    for ref in (e_by, o_by):
        ref[10] = top
    top_out[0] = top


def make_plan(slots, counts, plan):
    i, j = lax.axis_index("bx"), lax.axis_index("by")
    row = iota(0)
    here = lax.broadcasted_iota(jnp.int32, (8, 32), 1) == jnp.bitwise_xor(
        lax.broadcasted_iota(jnp.int32, (8, 32), 0), j
    )

    def columns(line):
        line = jnp.broadcast_to(line.astype(F32), (8, 32))
        value = jnp.sum(jnp.where(here, line, 0.0), axis=1, keepdims=True)
        return jnp.broadcast_to(value, TILE)

    def across(a, mask):
        for bit in (1, 2, 4):
            if mask & bit:
                a = jnp.where(row & bit == 0, pltpu.roll(a, 8 - bit, 0), pltpu.roll(a, bit, 0))
        return a

    give = [columns(slots[r, pl.ds(i, 1), :]) for r in range(3)]
    loads = [columns(counts[i, pl.ds(k, 1), :]) for k in range(4)]
    def first_round(slot):
        moved = slot == give[0]
        return jnp.where(moved, 1.0, 0.0), jnp.where(moved, across(give[0], 1), slot)

    one, two = first_round(give[1]), first_round(give[2])
    same = give[2] == give[1]
    entries = [give[0], *one, jnp.where(same, 2.0, two[0]), two[1]]
    by_two = [across(one[0], 2) + 2.0, across(one[1], 2)]
    third = [jnp.where(same, a, b) for a, b in zip(by_two, two)]
    by_four = [across(third[0], 4) + 4.0, across(third[1], 4)]
    for slot in range(4):
        here_now = first_round(jnp.full(TILE, slot, F32))
        is_second, is_last = give[1] == float(slot), give[2] == float(slot)
        source, index = [
            jnp.where(is_last, a, jnp.where(is_second, b, c))
            for a, b, c in zip(by_four, by_two, here_now)
        ]
        code = jnp.where(is_last, 3.0, jnp.where(is_second, 2.0, here_now[0]))
        source0 = jnp.broadcast_to(source[0:1], TILE)
        index0 = jnp.broadcast_to(index[0:1], TILE)
        count = jnp.zeros(TILE, F32)
        for k in range(4):
            hit = (row.astype(F32) == source0) & (index0 == float(k))
            count += jnp.where(hit, loads[k], 0.0)
        count = jnp.sum(count, axis=0, keepdims=True)
        entries += [code, index, count]
    entries.append(give[2])
    for e, value in enumerate(entries):
        plan[pl.ds(e, 1), :] = value[0:1].astype(jnp.int32)


def entry(plan, e):
    return plan[pl.ds(e, 1), :][0, 0]


def inner_kernel(slots, counts, w, d, plan, lefts, rights, fluxes):
    make_plan(slots, counts, plan)
    row, lane = iota(0), iota(1)

    def sweep(n, load, down, up, first, last, no_first, no_last):
        left, right = [[], []], [[], []]
        for f in range(5):
            a, b = load(f)
            da, ub = down(a), up(b)
            a_prev, b_prev = da, jnp.where(first, da, down(b))
            a_next, b_next = jnp.where(last, ub, up(a)), ub
            ha = half_minmod(a - a_prev, a_next - a)
            hb = half_minmod(b - b_prev, b_next - b)
            ra, rb = up(a - ha), up(b - hb)
            left[0].append(a + ha)
            left[1].append(b + hb)
            right[0].append(jnp.where(last, rb, ra))
            right[1].append(rb)
        fa = hllc(left[0], right[0], n)
        fb = hllc(left[1], right[1], n)
        out = []
        for f in range(5):
            a = jnp.where(no_first, 0.0, fa[f])
            b = jnp.where(no_last, 0.0, fb[f])
            da = down(a)
            out.append((a - jnp.where(first, 0.0, da), b - jnp.where(first, da, down(b))))
        return out

    def along_first(k, _):
        s, h = k // 2, k % 2
        out = sweep(
            1,
            lambda f: (w[s, f, 0, h], w[s, f, 1, h]),
            lambda a: pltpu.roll(a, 1, 0),
            lambda a: pltpu.roll(a, 7, 0),
            row == 0,
            row == 7,
            row == 0,
            row >= 6,
        )
        for f in range(5):
            d[s, f, 0, h], d[s, f, 1, h] = out[f]
        return 0

    def along_second(k, _):
        s, at = k // 2, k % 2
        out = sweep(
            2,
            lambda f: (w[s, f, at, 0], w[s, f, at, 1]),
            lambda a: pltpu.roll(a, 16, 1),
            lambda a: pltpu.roll(a, 112, 1),
            lane < 16,
            lane >= 112,
            lane < 16,
            lane >= 96,
        )
        for f in range(5):
            d[s, f, at, 0] += out[f][0]
            d[s, f, at, 1] += out[f][1]
        return 0

    first_c, last_c = lane % 16 == 0, lane % 16 == 15

    def previous(here, before):
        return jnp.where(first_c, pltpu.roll(before, 113, 1), pltpu.roll(here, 1, 1))

    def following(here, after):
        return jnp.where(last_c, pltpu.roll(after, 15, 1), pltpu.roll(here, 127, 1))

    def third_states(k, _):
        s, at = k // 2, k % 2
        before, after = (s + 3) % 4, (s + 1) % 4
        for h in range(2):
            for f in range(5):
                a = w[s, f, at, h]
                slope = half_minmod(
                    a - previous(a, w[before, f, at, h]), following(a, w[after, f, at, h]) - a
                )
                lefts[s, f, at, h] = a + slope
                rights[s, f, at, h] = a - slope
        return 0

    def third_fluxes(k, _):
        s, at = k // 2, k % 2
        after = (s + 1) % 4
        for h in range(2):
            out = hllc(
                [lefts[s, f, at, h] for f in range(5)],
                [following(rights[s, f, at, h], rights[after, f, at, h]) for f in range(5)],
                3,
            )
            for f in range(5):
                fluxes[s, f, at, h] = out[f]
        return 0

    def third_change(k, _):
        s, at = k // 2, k % 2
        before = (s + 3) % 4
        for h in range(2):
            for f in range(5):
                a = fluxes[s, f, at, h]
                d[s, f, at, h] += a - previous(a, fluxes[before, f, at, h])
        return 0

    for body in (along_first, along_second, third_states, third_fluxes, third_change):
        unroll = 8 if body in (third_states, third_change) else 4
        lax.fori_loop(0, 8, body, 0, unroll=unroll)


def edge_kernel(
    plan, u, d_in, se_bx, so_bx, se_by, so_by, in_bx, in_by, top, re_bx, ro_bx, re_by, ro_by, top2,
    d, send, top_out, spread, sent,
):
    i, j = lax.axis_index("bx"), lax.axis_index("by")
    even_i, even_j = i % 2 == 0, j % 2 == 0
    row, lane = iota(0), iota(1)

    top = jnp.maximum(jnp.maximum(top[0], top2[0]), jnp.maximum(re_by[10], ro_by[10]))
    top = jnp.broadcast_to(jnp.max(top, axis=0, keepdims=True), TILE)
    for k in range(spread.shape[0]):
        spread[k] = top
    copy = pltpu.make_async_copy(spread, top_out, sent)
    copy.start()

    def faces(n, own_low, own_high, low, high, inner, back, ahead, zero):
        left, right, left2, right2 = [], [], [], []
        for o, q, a, b, w in zip(own_low, own_high, low, high, inner):
            c = jnp.where(zero, ahead(a), back(o))
            left.append(c + half_minmod(c - a, o - c))
            right.append(o - half_minmod(o - c, jnp.where(zero, ahead(o), w) - o))
            e = jnp.where(zero, ahead(q), back(b))
            left2.append(q + half_minmod(q - jnp.where(zero, w, back(q)), e - q))
            right2.append(e - half_minmod(e - q, b - e))
        low_flux = hllc(left, right, n)
        high_flux = hllc(left2, right2, n)
        return (
            [jnp.where(zero, ahead(f) - f, -f) for f in low_flux],
            [jnp.where(zero, f, f - back(f)) for f in high_flux],
        )

    def picked(flag, a, b, index):
        return [jnp.where(flag, a[t], b[t]) for t in range(index, 10, 2)]

    d[...] = d_in[...]
    for h in range(2):
        low, high = faces(
            1,
            picked(even_i, so_bx, se_bx, h),
            picked(even_i, se_bx, so_bx, h),
            picked(even_i, ro_bx, re_bx, h),
            picked(even_i, re_bx, ro_bx, h),
            [in_bx[t] for t in range(h, 10, 2)],
            lambda a: pltpu.roll(a, 1, 0),
            lambda a: pltpu.roll(a, 7, 0),
            row % 2 == 0,
        )
        for f in range(5):
            for s in range(4):
                d[s, f, 0, h] += jnp.where(row < 2, pltpu.roll(low[f], (8 - 2 * s) % 8, 0), 0.0)
                d[s, f, 1, h] += jnp.where(row >= 6, pltpu.roll(high[f], 6 - 2 * s, 0), 0.0)
    for at in range(2):
        turn = lambda a: pltpu.roll(a, 64, 1)
        low, high = faces(
            2,
            picked(even_j, so_by, se_by, at),
            picked(even_j, se_by, so_by, at),
            picked(even_j, ro_by, re_by, at),
            picked(even_j, re_by, ro_by, at),
            [in_by[t] for t in range(at, 10, 2)],
            turn,
            turn,
            lane < 64,
        )
        for f in range(5):
            for s in range(4):
                one = pltpu.roll(low[f], (128 - 16 * s) % 128, 1)
                two = pltpu.roll(low[f], 80 - 16 * s, 1)
                d[s, f, at, 0] += jnp.where(lane < 16, one, jnp.where(lane < 32, two, 0.0))
                one = pltpu.roll(high[f], 96 - 16 * s, 1)
                two = pltpu.roll(high[f], 48 - 16 * s, 1)
                d[s, f, at, 1] += jnp.where(lane >= 112, two, jnp.where(lane >= 96, one, 0.0))

    slot = entry(plan, 0)
    send[0] = u[slot]
    send[1] = d[slot]
    copy.wait()


def relay_kernel(plan, u, d, got1, send_u, send_d):
    code, index = entry(plan, 1), entry(plan, 2)

    @pl.when(code == 0)
    def _():
        send_u[...] = u[index]
        send_d[...] = d[index]

    @pl.when(code == 1)
    def _():
        send_u[...] = got1[0]
        send_d[...] = got1[1]


def pass_kernel(part, plan, own, got1, got2, send):
    code, index = entry(plan, 3), entry(plan, 4)

    @pl.when(code == 0)
    def _():
        send[...] = own[index]

    @pl.when(code == 1)
    def _():
        send[...] = got1[part]

    @pl.when(code == 2)
    def _():
        send[...] = got2[...]


def block_tiles():
    return [(at, h) for at in range(2) for h in range(2)]


def update(out, energy, factor, tick, slot, step, count, u_of, d_of):
    chill = step / count.astype(F32)
    for at, h in block_tiles():
        new = [u_of(f, at, h) - step * d_of(f, at, h) for f in range(5)]
        inverse = invert(new[0])
        squares = new[1] * new[1] + new[2] * new[2] + new[3] * new[3]
        kinetic = 0.5 * squares * inverse
        energy[slot, at, h] = new[4] - kinetic
        factor[slot, at, h] = (HEAT_RATIO - 1.0) * inverse
        tick[slot, at, h] = chill * new[0] * EMISSION_RATE
        new[4] = kinetic
        for f in range(5):
            out[slot, f, pl.ds(8 * at, 8), pl.ds(128 * h, 128)] = new[f]


def cool(out, energy, factor, tick, limits):
    places = [(slot, at, h) for slot in range(len(limits)) for at, h in block_tiles()]
    most = limits[0]
    for limit in limits[1:]:
        most = jnp.maximum(most, limit)

    def advance(k, state):
        after = []
        for now, place in zip(state, places):
            heat = now * factor[place]
            loss = tick[place] * root(jnp.minimum(1.0 + heat * heat, BIG))
            new = now * invert(jnp.minimum(1.0 + loss, BIG))
            after.append(jnp.where(k < limits[place[0]], new, now))
        return tuple(after)

    state = lax.fori_loop(0, most, advance, tuple(energy[place] for place in places))
    for left, (slot, at, h) in zip(state, places):
        place = (slot, 4, pl.ds(8 * at, 8), pl.ds(128 * h, 128))
        out[place] = out[place] + left


def near_kernel(
    plan, u, d, top, got1, got_u, got_d, step_out, result, out, energy, factor, tick, sent, last
):
    speed = jnp.max(jnp.max(top[...], axis=0), axis=0, keepdims=True)
    speed = jnp.max(speed, axis=1, keepdims=True)
    step = COURANT_FACTOR / jnp.broadcast_to(speed, TILE)
    step_out[...] = step
    skipped = entry(plan, 17)
    target = lambda k: k + jnp.where(k >= skipped, 1, 0)

    def load(k, _):
        code, index, count = [entry(plan, 5 + 3 * target(k) + e) for e in range(3)]
        store = lambda *parts: update(out, energy, factor, tick, k, step, count, *parts)

        @pl.when(code == 0)
        def _():
            store(lambda f, at, h: u[index, f, at, h], lambda f, at, h: d[index, f, at, h])

        @pl.when(code == 1)
        def _():
            store(lambda f, at, h: got1[0, f, at, h], lambda f, at, h: got1[1, f, at, h])

        @pl.when(code == 2)
        def _():
            store(lambda f, at, h: got_u[f, at, h], lambda f, at, h: got_d[f, at, h])

        rows = pl.ds(0, 4)
        pltpu.make_async_copy(
            out.at[k, rows], result.at[target(k), rows], sent.at[k]
        ).start()
        return 0

    lax.fori_loop(0, 3, load, 0)
    cool(out, energy, factor, tick, [entry(plan, 7 + 3 * target(k)) for k in range(3)])
    copies = []
    for k in range(3):
        row = pl.ds(4, 1)
        copies.append(
            pltpu.make_async_copy(out.at[k, row], result.at[target(k), row], last.at[k])
        )
        copies[-1].start()
    for k in range(3):
        rows = pl.ds(0, 4)
        pltpu.make_async_copy(out.at[k, rows], result.at[target(k), rows], sent.at[k]).wait()
        copies[k].wait()


def far_kernel(plan, step, got_u, got_d, given, result, out, energy, factor, tick, sent, last):
    slot = entry(plan, 17)
    count = entry(plan, 7 + 3 * slot)
    u_of, d_of = [lambda f, at, h, ref=ref: ref[f, at, h] for ref in (got_u, got_d)]
    update(out, energy, factor, tick, 0, step[...], count, u_of, d_of)
    first = pltpu.make_async_copy(
        out.at[0, pl.ds(0, 4)], result.at[slot, pl.ds(0, 4)], sent
    )
    first.start()
    cool(out, energy, factor, tick, [count])
    second = pltpu.make_async_copy(
        out.at[0, pl.ds(4, 1)], result.at[slot, pl.ds(4, 1)], last
    )
    second.start()
    first.wait()
    second.wait()


def pair_even(count):
    return [(k, k ^ 1) for k in range(count)]


def pair_odd(count):
    return [(k, (k + 1) % count if k % 2 else (k - 1) % count) for k in range(count)]


def call(kernel, inputs, outputs, scratch=(), hbm_in=0, hbm_out=0, plan=0, aliases=None, room=16):
    return pl.pallas_call(
        kernel,
        in_specs=[VMEM] * (len(inputs) - hbm_in) + [ANY] * hbm_in,
        out_specs=[VMEM] * (len(outputs) - hbm_out) + [ANY] * hbm_out + [VMEM] * plan,
        out_shape=[shape(*dims) for dims in outputs] + [PLAN] * plan,
        scratch_shapes=[pltpu.VMEM(x, F32) if isinstance(x, tuple) else x for x in scratch],
        compiler_params=pltpu.CompilerParams(vmem_limit_bytes=room * 2**20),
        input_output_aliases=aliases or {},
    )(*inputs)


def on_device(conserved, cool_steps, swap_slot):
    rows, columns = lax.axis_size("bx"), lax.axis_size("by")
    slots = swap_slot.transpose(2, 0, 1)
    counts = cool_steps.transpose(0, 2, 1)
    face = (10,) + TILE
    u, w, *slabs = call(
        prep_kernel,
        [conserved.reshape(5, 256, 64)],
        [BLOCKS] * 2
        + [(10,) + TILE, (13,) + TILE, (11,) + TILE, (14,) + TILE]
        + [face] * 2
        + [(12,) + TILE],
        [(5, 256, 64), pltpu.SemaphoreType.DMA((2, 5))],
        hbm_in=1,
        room=53,
    )
    e_bx, o_bx, e_by, o_by = slabs[:4]
    got_slabs = [
        lax.ppermute(e_bx, "bx", pair_even(rows)),
        lax.ppermute(o_bx, "bx", pair_odd(rows)),
        lax.ppermute(e_by, "by", pair_even(columns)),
        lax.ppermute(o_by, "by", pair_odd(columns)),
        lax.ppermute(slabs[-1], "by", [(k, k ^ 2) for k in range(columns)]),
    ]
    d, plan = call(inner_kernel, [slots, counts, w], [BLOCKS], [BLOCKS] * 3, plan=1)
    groups = [
        [i * columns + j for i in range(rows) for j in range(x, columns, 4)] for x in range(4)
    ]
    size = len(groups[0])
    chunks = (size * 3 // 8,) + TILE
    d, send, top = call(
        edge_kernel,
        [plan, u, d, *slabs, *got_slabs],
        [BLOCKS, TRAVEL, chunks],
        [chunks, pltpu.SemaphoreType.DMA],
        hbm_out=1,
    )
    trade = lambda m, block: lax.ppermute(block, "by", [(k, k ^ m) for k in range(columns)])
    got1 = trade(1, send)
    top = top.reshape(size, 3, 1, 128)
    top = lax.all_to_all(top, ("bx", "by"), 0, 0, axis_index_groups=groups)
    top = top.reshape(chunks)
    sends = call(relay_kernel, [plan, u, d, got1], [HALF] * 2)
    got2 = [trade(2, send) for send in sends]
    got4 = []
    for part, own in enumerate((u, d)):
        kernel = functools.partial(pass_kernel, part)
        (send,) = call(kernel, [plan, own, got1, got2[part]], [HALF])
        got4.append(trade(4, send))
    block = (5, 16, 256)
    state = (2, 2) + TILE
    step, result = call(
        near_kernel,
        [plan, u, d, top, got1, *got2],
        [TILE, (4,) + block],
        [(3,) + block] + [(3,) + state] * 3 + [pltpu.SemaphoreType.DMA((3,))] * 2,
        hbm_out=1,
    )
    (result,) = call(
        far_kernel,
        [plan, step, *got4, result],
        [(4,) + block],
        [(1,) + block] + [(1,) + state] * 3 + [pltpu.SemaphoreType.DMA] * 2,
        hbm_in=1,
        hbm_out=1,
        aliases={4: 0},
    )
    return result.reshape((1, 1) + result.shape)


def solution(mesh):
    in_specs = (P(None, "bx", "by", None), P(), P())
    out_specs = P("bx", "by", None, None, None, None)
    return jax.shard_map(
        on_device, mesh=mesh, in_specs=in_specs, out_specs=out_specs, check_vma=False
    )
```

```python
import functools

import jax
import jax.numpy as jnp
from jax import lax
from jax.experimental import pallas as pl
from jax.experimental.pallas import tpu as pltpu
from jax.sharding import PartitionSpec as P

HEAT_RATIO = 5.0 / 3.0
COURANT_FACTOR = 0.4
EMISSION_RATE = 100.0
F32 = jnp.float32
TILE = (8, 128)
BLOCKS = (4, 5, 2, 2) + TILE
TRAVEL = (2, 5, 2, 2) + TILE
HALF = (5, 2, 2) + TILE
VMEM = pl.BlockSpec(memory_space=pltpu.VMEM)
ANY = pl.BlockSpec(memory_space=pl.ANY)
PLAN = jax.ShapeDtypeStruct((24, 128), jnp.int32)
BIG = 3e38
SMALL = 1e-37


def shape(*dims):
    return jax.ShapeDtypeStruct(dims, F32)


def iota(axis):
    return lax.broadcasted_iota(jnp.int32, TILE, axis)


def invert(x):
    return pl.reciprocal(x, approx=True)


def root(x):
    x = jnp.maximum(x, SMALL)
    return x * lax.rsqrt(x)


def half_minmod(a, b):
    return 0.5 * jnp.maximum(jnp.minimum(a, b), jnp.minimum(jnp.maximum(a, b), 0.0))


def primitive(u):
    inverse = invert(u[0])
    v1, v2, v3 = u[1] * inverse, u[2] * inverse, u[3] * inverse
    p = (HEAT_RATIO - 1.0) * (u[4] - 0.5 * u[0] * (v1 * v1 + v2 * v2 + v3 * v3))
    return [u[0], v1, v2, v3, p], inverse


def hllc(left, right, n):
    rl, ul, pl_ = left[0], left[n], left[4]
    rr, ur, pr = right[0], right[n], right[4]
    cl = root(HEAT_RATIO * pl_ * invert(rl))
    cr = root(HEAT_RATIO * pr * invert(rr))
    sl = jnp.minimum(ul - cl, ur - cr)
    sr = jnp.maximum(ul + cl, ur + cr)
    ml = rl * (sl - ul)
    mr = rr * (sr - ur)
    mid = (pr - pl_ + ml * ul - mr * ur) * invert(ml - mr)
    use_left = jnp.maximum(sl, mid) >= 0.0
    rho, v1, v2, v3, p = [jnp.where(use_left, a, b) for a, b in zip(left, right)]
    edge = jnp.where(use_left, sl, sr)
    clip = jnp.where(use_left, jnp.minimum(sl, 0.0), jnp.maximum(sr, 0.0))
    u = (None, v1, v2, v3)[n]
    energy = p * (1.0 / (HEAT_RATIO - 1.0)) + 0.5 * rho * (v1 * v1 + v2 * v2 + v3 * v3)
    gap = invert(jnp.where(clip == 0.0, 1.0, edge - mid))
    ratio = (edge - u) * gap
    star_rho = rho * ratio
    star_energy = ratio * energy + (mid - u) * (star_rho * mid + p * gap)
    mass = rho * u
    f_rho = mass + clip * (star_rho - rho)
    out = [f_rho, f_rho * v1, f_rho * v2, f_rho * v3, None]
    out[n] = mass * u + p + clip * (star_rho * mid - mass)
    out[4] = (energy + p) * u + clip * (star_energy - energy)
    return out


def prep_kernel(
    source, u_out, w_out, e_bx, o_bx, e_by, o_by, in_bx, in_by, top_out, cons, arrived
):
    copies = []
    for at in range(2):
        for f in range(5):
            place = (f, pl.ds(at * 128, 128))
            copies.append(
                pltpu.make_async_copy(source.at[place], cons.at[place], arrived.at[at, f])
            )
            copies[-1].start()
    even_i = lax.axis_index("bx") % 2 == 0
    even_j = lax.axis_index("by") % 2 == 0
    lane = iota(1)
    bit0 = (lane // 16) % 2 == 0
    bit1 = (lane // 32) % 2 == 0
    row = iota(0)
    top = jnp.zeros(TILE, F32)
    for at in range(2):
        for copy in copies[at * 5 : at * 5 + 5]:
            copy.wait()
        low, high, inner = [], [], []
        for h in range(2):
            tiles = []
            for f in range(5):
                x = [cons[f, pl.ds(at * 128 + h * 8 + b, 8, stride=16), :] for b in range(8)]
                if h == 0:
                    low.append(jnp.concatenate([x[0], x[1]], axis=1))
                    inner.append(x[2])
                else:
                    high.append(jnp.concatenate([x[6], x[7]], axis=1))
                    inner[f] = jnp.concatenate([x[5], inner[f]], axis=1)
                y = [jnp.concatenate([x[k], x[k + 4]], axis=1) for k in range(4)]
                z = [None] * 4
                for k in range(2):
                    z[k] = jnp.where(bit1, y[k], pltpu.roll(y[k + 2], 32, 1))
                    z[k + 2] = jnp.where(bit1, pltpu.roll(y[k], 96, 1), y[k + 2])
                t = [None] * 4
                for k in (0, 2):
                    t[k] = jnp.where(bit0, z[k], pltpu.roll(z[k + 1], 16, 1))
                    t[k + 1] = jnp.where(bit0, pltpu.roll(z[k], 112, 1), z[k + 1])
                tiles.append(t)
                for s in range(4):
                    u_out[s, f, at, h] = t[s]
            for s in range(4):
                w, inverse = primitive([tiles[f][s] for f in range(5)])
                speed = (
                    jnp.abs(w[1])
                    + jnp.abs(w[2])
                    + jnp.abs(w[3])
                    + 3.0 * root(HEAT_RATIO * w[4] * inverse)
                )
                top = jnp.maximum(top, speed)
                for f in range(5):
                    w_out[s, f, at, h] = w[f]
        low, _ = primitive(low)
        high, _ = primitive(high)
        inner, _ = primitive(inner)
        for f in range(5):
            e_by[f * 2 + at] = jnp.where(even_j, high[f], low[f])
            o_by[f * 2 + at] = jnp.where(even_j, low[f], high[f])
            in_by[f * 2 + at] = inner[f]
    for f in range(5):
        for h in range(2):
            low = jnp.zeros(TILE, F32)
            high = jnp.zeros(TILE, F32)
            inner = jnp.zeros(TILE, F32)
            for s in range(4):
                here = row // 2 == s
                a, b = w_out[s, f, 0, h], w_out[s, f, 1, h]
                low = jnp.where(here, pltpu.roll(a, 2 * s, 0), low)
                high = jnp.where(here, pltpu.roll(b, (2 * s + 2) % 8, 0), high)
                inner = jnp.where(row == 2 * s, pltpu.roll(b, (2 * s + 3) % 8, 0), inner)
                inner = jnp.where(row == 2 * s + 1, pltpu.roll(a, (2 * s + 7) % 8, 0), inner)
            e_bx[f * 2 + h] = jnp.where(even_i, high, low)
            o_bx[f * 2 + h] = jnp.where(even_i, low, high)
            in_bx[f * 2 + h] = inner
    for ref in (e_by, o_by):
        ref[10] = top
    top_out[0] = top


def make_plan(slots, counts, plan):
    i, j = lax.axis_index("bx"), lax.axis_index("by")
    row = iota(0)
    here = lax.broadcasted_iota(jnp.int32, (8, 32), 1) == jnp.bitwise_xor(
        lax.broadcasted_iota(jnp.int32, (8, 32), 0), j
    )

    def columns(line):
        line = jnp.broadcast_to(line.astype(F32), (8, 32))
        value = jnp.sum(jnp.where(here, line, 0.0), axis=1, keepdims=True)
        return jnp.broadcast_to(value, TILE)

    def across(a, mask):
        for bit in (1, 2, 4):
            if mask & bit:
                a = jnp.where(row & bit == 0, pltpu.roll(a, 8 - bit, 0), pltpu.roll(a, bit, 0))
        return a

    give = [columns(slots[r, pl.ds(i, 1), :]) for r in range(3)]
    loads = [columns(counts[i, pl.ds(k, 1), :]) for k in range(4)]
    def first_round(slot):
        moved = slot == give[0]
        return jnp.where(moved, 1.0, 0.0), jnp.where(moved, across(give[0], 1), slot)

    one, two = first_round(give[1]), first_round(give[2])
    same = give[2] == give[1]
    entries = [give[0], *one, jnp.where(same, 2.0, two[0]), two[1]]
    by_two = [across(one[0], 2) + 2.0, across(one[1], 2)]
    third = [jnp.where(same, a, b) for a, b in zip(by_two, two)]
    by_four = [across(third[0], 4) + 4.0, across(third[1], 4)]
    for slot in range(4):
        here_now = first_round(jnp.full(TILE, slot, F32))
        is_second, is_last = give[1] == float(slot), give[2] == float(slot)
        source, index = [
            jnp.where(is_last, a, jnp.where(is_second, b, c))
            for a, b, c in zip(by_four, by_two, here_now)
        ]
        code = jnp.where(is_last, 3.0, jnp.where(is_second, 2.0, here_now[0]))
        source0 = jnp.broadcast_to(source[0:1], TILE)
        index0 = jnp.broadcast_to(index[0:1], TILE)
        count = jnp.zeros(TILE, F32)
        for k in range(4):
            hit = (row.astype(F32) == source0) & (index0 == float(k))
            count += jnp.where(hit, loads[k], 0.0)
        count = jnp.sum(count, axis=0, keepdims=True)
        entries += [code, index, count]
    entries.append(give[2])
    for e, value in enumerate(entries):
        plan[pl.ds(e, 1), :] = value[0:1].astype(jnp.int32)


def entry(plan, e):
    return plan[pl.ds(e, 1), :][0, 0]


def inner_kernel(slots, counts, w, d, plan, lefts, rights, fluxes):
    make_plan(slots, counts, plan)
    row, lane = iota(0), iota(1)

    def sweep(n, load, down, up, first, last, no_first, no_last):
        left, right = [[], []], [[], []]
        for f in range(5):
            a, b = load(f)
            da, ub = down(a), up(b)
            a_prev, b_prev = da, jnp.where(first, da, down(b))
            a_next, b_next = jnp.where(last, ub, up(a)), ub
            ha = half_minmod(a - a_prev, a_next - a)
            hb = half_minmod(b - b_prev, b_next - b)
            ra, rb = up(a - ha), up(b - hb)
            left[0].append(a + ha)
            left[1].append(b + hb)
            right[0].append(jnp.where(last, rb, ra))
            right[1].append(rb)
        fa = hllc(left[0], right[0], n)
        fb = hllc(left[1], right[1], n)
        out = []
        for f in range(5):
            a = jnp.where(no_first, 0.0, fa[f])
            b = jnp.where(no_last, 0.0, fb[f])
            da = down(a)
            out.append((a - jnp.where(first, 0.0, da), b - jnp.where(first, da, down(b))))
        return out

    def along_first(k, _):
        s, h = k // 2, k % 2
        out = sweep(
            1,
            lambda f: (w[s, f, 0, h], w[s, f, 1, h]),
            lambda a: pltpu.roll(a, 1, 0),
            lambda a: pltpu.roll(a, 7, 0),
            row == 0,
            row == 7,
            row == 0,
            row >= 6,
        )
        for f in range(5):
            d[s, f, 0, h], d[s, f, 1, h] = out[f]
        return 0

    def along_second(k, _):
        s, at = k // 2, k % 2
        out = sweep(
            2,
            lambda f: (w[s, f, at, 0], w[s, f, at, 1]),
            lambda a: pltpu.roll(a, 16, 1),
            lambda a: pltpu.roll(a, 112, 1),
            lane < 16,
            lane >= 112,
            lane < 16,
            lane >= 96,
        )
        for f in range(5):
            d[s, f, at, 0] += out[f][0]
            d[s, f, at, 1] += out[f][1]
        return 0

    first_c, last_c = lane % 16 == 0, lane % 16 == 15

    def previous(here, before):
        return jnp.where(first_c, pltpu.roll(before, 113, 1), pltpu.roll(here, 1, 1))

    def following(here, after):
        return jnp.where(last_c, pltpu.roll(after, 15, 1), pltpu.roll(here, 127, 1))

    def third_states(k, _):
        s, at = k // 2, k % 2
        before, after = (s + 3) % 4, (s + 1) % 4
        for h in range(2):
            for f in range(5):
                a = w[s, f, at, h]
                slope = half_minmod(
                    a - previous(a, w[before, f, at, h]), following(a, w[after, f, at, h]) - a
                )
                lefts[s, f, at, h] = a + slope
                rights[s, f, at, h] = a - slope
        return 0

    def third_fluxes(k, _):
        s, at = k // 2, k % 2
        after = (s + 1) % 4
        for h in range(2):
            out = hllc(
                [lefts[s, f, at, h] for f in range(5)],
                [following(rights[s, f, at, h], rights[after, f, at, h]) for f in range(5)],
                3,
            )
            for f in range(5):
                fluxes[s, f, at, h] = out[f]
        return 0

    def third_change(k, _):
        s, at = k // 2, k % 2
        before = (s + 3) % 4
        for h in range(2):
            for f in range(5):
                a = fluxes[s, f, at, h]
                d[s, f, at, h] += a - previous(a, fluxes[before, f, at, h])
        return 0

    for body in (along_first, along_second, third_states, third_fluxes, third_change):
        unroll = 4 if body in (along_first, along_second) else 8
        lax.fori_loop(0, 8, body, 0, unroll=unroll)


def edge_kernel(
    plan, u, d_in, se_bx, so_bx, se_by, so_by, in_bx, in_by, top, re_bx, ro_bx, re_by, ro_by, top2,
    d, send, top_out, spread, sent,
):
    i, j = lax.axis_index("bx"), lax.axis_index("by")
    even_i, even_j = i % 2 == 0, j % 2 == 0
    row, lane = iota(0), iota(1)

    top = jnp.maximum(jnp.maximum(top[0], top2[0]), jnp.maximum(re_by[10], ro_by[10]))
    top = jnp.broadcast_to(jnp.max(top, axis=0, keepdims=True), TILE)
    for k in range(spread.shape[0]):
        spread[k] = top
    copy = pltpu.make_async_copy(spread, top_out, sent)
    copy.start()

    def faces(n, own_low, own_high, low, high, inner, back, ahead, zero):
        left, right, left2, right2 = [], [], [], []
        for o, q, a, b, w in zip(own_low, own_high, low, high, inner):
            c = jnp.where(zero, ahead(a), back(o))
            left.append(c + half_minmod(c - a, o - c))
            right.append(o - half_minmod(o - c, jnp.where(zero, ahead(o), w) - o))
            e = jnp.where(zero, ahead(q), back(b))
            left2.append(q + half_minmod(q - jnp.where(zero, w, back(q)), e - q))
            right2.append(e - half_minmod(e - q, b - e))
        low_flux = hllc(left, right, n)
        high_flux = hllc(left2, right2, n)
        return (
            [jnp.where(zero, ahead(f) - f, -f) for f in low_flux],
            [jnp.where(zero, f, f - back(f)) for f in high_flux],
        )

    def picked(flag, a, b, index):
        return [jnp.where(flag, a[t], b[t]) for t in range(index, 10, 2)]

    d[...] = d_in[...]
    for h in range(2):
        low, high = faces(
            1,
            picked(even_i, so_bx, se_bx, h),
            picked(even_i, se_bx, so_bx, h),
            picked(even_i, ro_bx, re_bx, h),
            picked(even_i, re_bx, ro_bx, h),
            [in_bx[t] for t in range(h, 10, 2)],
            lambda a: pltpu.roll(a, 1, 0),
            lambda a: pltpu.roll(a, 7, 0),
            row % 2 == 0,
        )
        for f in range(5):
            for s in range(4):
                d[s, f, 0, h] += jnp.where(row < 2, pltpu.roll(low[f], (8 - 2 * s) % 8, 0), 0.0)
                d[s, f, 1, h] += jnp.where(row >= 6, pltpu.roll(high[f], 6 - 2 * s, 0), 0.0)
    for at in range(2):
        turn = lambda a: pltpu.roll(a, 64, 1)
        low, high = faces(
            2,
            picked(even_j, so_by, se_by, at),
            picked(even_j, se_by, so_by, at),
            picked(even_j, ro_by, re_by, at),
            picked(even_j, re_by, ro_by, at),
            [in_by[t] for t in range(at, 10, 2)],
            turn,
            turn,
            lane < 64,
        )
        for f in range(5):
            for s in range(4):
                one = pltpu.roll(low[f], (128 - 16 * s) % 128, 1)
                two = pltpu.roll(low[f], 80 - 16 * s, 1)
                d[s, f, at, 0] += jnp.where(lane < 16, one, jnp.where(lane < 32, two, 0.0))
                one = pltpu.roll(high[f], 96 - 16 * s, 1)
                two = pltpu.roll(high[f], 48 - 16 * s, 1)
                d[s, f, at, 1] += jnp.where(lane >= 112, two, jnp.where(lane >= 96, one, 0.0))

    slot = entry(plan, 0)
    send[0] = u[slot]
    send[1] = d[slot]
    copy.wait()


def relay_kernel(plan, u, d, got1, send_u, send_d):
    code, index = entry(plan, 1), entry(plan, 2)

    @pl.when(code == 0)
    def _():
        send_u[...] = u[index]
        send_d[...] = d[index]

    @pl.when(code == 1)
    def _():
        send_u[...] = got1[0]
        send_d[...] = got1[1]


def pass_kernel(part, plan, own, got1, got2, send):
    code, index = entry(plan, 3), entry(plan, 4)

    @pl.when(code == 0)
    def _():
        send[...] = own[index]

    @pl.when(code == 1)
    def _():
        send[...] = got1[part]

    @pl.when(code == 2)
    def _():
        send[...] = got2[...]


def block_tiles():
    return [(at, h) for at in range(2) for h in range(2)]


def update(out, energy, factor, tick, slot, step, count, u_of, d_of):
    chill = step / count.astype(F32)
    for at, h in block_tiles():
        new = [u_of(f, at, h) - step * d_of(f, at, h) for f in range(5)]
        inverse = invert(new[0])
        squares = new[1] * new[1] + new[2] * new[2] + new[3] * new[3]
        kinetic = 0.5 * squares * inverse
        energy[slot, at, h] = new[4] - kinetic
        factor[slot, at, h] = (HEAT_RATIO - 1.0) * inverse
        tick[slot, at, h] = chill * new[0] * EMISSION_RATE
        new[4] = kinetic
        for f in range(5):
            out[slot, f, pl.ds(8 * at, 8), pl.ds(128 * h, 128)] = new[f]


def cool(out, energy, factor, tick, limits):
    places = [(slot, at, h) for slot in range(len(limits)) for at, h in block_tiles()]
    most = limits[0]
    for limit in limits[1:]:
        most = jnp.maximum(most, limit)

    def advance(k, state):
        after = []
        for now, place in zip(state, places):
            heat = now * factor[place]
            loss = tick[place] * root(jnp.minimum(1.0 + heat * heat, BIG))
            new = now * invert(jnp.minimum(1.0 + loss, BIG))
            after.append(jnp.where(k < limits[place[0]], new, now))
        return tuple(after)

    state = lax.fori_loop(0, most, advance, tuple(energy[place] for place in places))
    for left, (slot, at, h) in zip(state, places):
        place = (slot, 4, pl.ds(8 * at, 8), pl.ds(128 * h, 128))
        out[place] = out[place] + left


def near_kernel(
    plan, u, d, top, got1, got_u, got_d, step_out, result, out, energy, factor, tick, sent, last
):
    speed = jnp.max(jnp.max(top[...], axis=0), axis=0, keepdims=True)
    speed = jnp.max(speed, axis=1, keepdims=True)
    step = COURANT_FACTOR / jnp.broadcast_to(speed, TILE)
    step_out[...] = step
    skipped = entry(plan, 17)
    target = lambda k: k + jnp.where(k >= skipped, 1, 0)

    def load(k, _):
        code, index, count = [entry(plan, 5 + 3 * target(k) + e) for e in range(3)]
        store = lambda *parts: update(out, energy, factor, tick, k, step, count, *parts)

        @pl.when(code == 0)
        def _():
            store(lambda f, at, h: u[index, f, at, h], lambda f, at, h: d[index, f, at, h])

        @pl.when(code == 1)
        def _():
            store(lambda f, at, h: got1[0, f, at, h], lambda f, at, h: got1[1, f, at, h])

        @pl.when(code == 2)
        def _():
            store(lambda f, at, h: got_u[f, at, h], lambda f, at, h: got_d[f, at, h])

        rows = pl.ds(0, 4)
        pltpu.make_async_copy(
            out.at[k, rows], result.at[target(k), rows], sent.at[k]
        ).start()
        return 0

    lax.fori_loop(0, 3, load, 0)
    cool(out, energy, factor, tick, [entry(plan, 7 + 3 * target(k)) for k in range(3)])
    copies = []
    for k in range(3):
        row = pl.ds(4, 1)
        copies.append(
            pltpu.make_async_copy(out.at[k, row], result.at[target(k), row], last.at[k])
        )
        copies[-1].start()
    for k in range(3):
        rows = pl.ds(0, 4)
        pltpu.make_async_copy(out.at[k, rows], result.at[target(k), rows], sent.at[k]).wait()
        copies[k].wait()


def far_kernel(plan, step, got_u, got_d, given, result, out, energy, factor, tick, sent, last):
    slot = entry(plan, 17)
    count = entry(plan, 7 + 3 * slot)
    u_of, d_of = [lambda f, at, h, ref=ref: ref[f, at, h] for ref in (got_u, got_d)]
    update(out, energy, factor, tick, 0, step[...], count, u_of, d_of)
    first = pltpu.make_async_copy(
        out.at[0, pl.ds(0, 4)], result.at[slot, pl.ds(0, 4)], sent
    )
    first.start()
    cool(out, energy, factor, tick, [count])
    second = pltpu.make_async_copy(
        out.at[0, pl.ds(4, 1)], result.at[slot, pl.ds(4, 1)], last
    )
    second.start()
    first.wait()
    second.wait()


def pair_even(count):
    return [(k, k ^ 1) for k in range(count)]


def pair_odd(count):
    return [(k, (k + 1) % count if k % 2 else (k - 1) % count) for k in range(count)]


def call(kernel, inputs, outputs, scratch=(), hbm_in=0, hbm_out=0, plan=0, aliases=None, room=16):
    return pl.pallas_call(
        kernel,
        in_specs=[VMEM] * (len(inputs) - hbm_in) + [ANY] * hbm_in,
        out_specs=[VMEM] * (len(outputs) - hbm_out) + [ANY] * hbm_out + [VMEM] * plan,
        out_shape=[shape(*dims) for dims in outputs] + [PLAN] * plan,
        scratch_shapes=[pltpu.VMEM(x, F32) if isinstance(x, tuple) else x for x in scratch],
        compiler_params=pltpu.CompilerParams(vmem_limit_bytes=room * 2**20),
        input_output_aliases=aliases or {},
    )(*inputs)


def on_device(conserved, cool_steps, swap_slot):
    rows, columns = lax.axis_size("bx"), lax.axis_size("by")
    slots = swap_slot.transpose(2, 0, 1)
    counts = cool_steps.transpose(0, 2, 1)
    face = (10,) + TILE
    u, w, *slabs = call(
        prep_kernel,
        [conserved.reshape(5, 256, 64)],
        [BLOCKS] * 2
        + [(10,) + TILE, (13,) + TILE, (11,) + TILE, (14,) + TILE]
        + [face] * 2
        + [(12,) + TILE],
        [(5, 256, 64), pltpu.SemaphoreType.DMA((2, 5))],
        hbm_in=1,
        room=53,
    )
    e_bx, o_bx, e_by, o_by = slabs[:4]
    got_slabs = [
        lax.ppermute(e_bx, "bx", pair_even(rows)),
        lax.ppermute(o_bx, "bx", pair_odd(rows)),
        lax.ppermute(e_by, "by", pair_even(columns)),
        lax.ppermute(o_by, "by", pair_odd(columns)),
        lax.ppermute(slabs[-1], "by", [(k, k ^ 2) for k in range(columns)]),
    ]
    d, plan = call(inner_kernel, [slots, counts, w], [BLOCKS], [BLOCKS] * 3, plan=1)
    groups = [
        [i * columns + j for i in range(rows) for j in range(x, columns, 4)] for x in range(4)
    ]
    size = len(groups[0])
    chunks = (size * 3 // 8,) + TILE
    d, send, top = call(
        edge_kernel,
        [plan, u, d, *slabs, *got_slabs],
        [BLOCKS, TRAVEL, chunks],
        [chunks, pltpu.SemaphoreType.DMA],
        hbm_out=1,
    )
    trade = lambda m, block: lax.ppermute(block, "by", [(k, k ^ m) for k in range(columns)])
    got1 = trade(1, send)
    top = top.reshape(size, 3, 1, 128)
    top = lax.all_to_all(top, ("bx", "by"), 0, 0, axis_index_groups=groups)
    top = top.reshape(chunks)
    sends = call(relay_kernel, [plan, u, d, got1], [HALF] * 2)
    got2 = [trade(2, send) for send in sends]
    got4 = []
    for part, own in enumerate((u, d)):
        kernel = functools.partial(pass_kernel, part)
        (send,) = call(kernel, [plan, own, got1, got2[part]], [HALF])
        got4.append(trade(4, send))
    block = (5, 16, 256)
    state = (2, 2) + TILE
    step, result = call(
        near_kernel,
        [plan, u, d, top, got1, *got2],
        [TILE, (4,) + block],
        [(3,) + block] + [(3,) + state] * 3 + [pltpu.SemaphoreType.DMA((3,))] * 2,
        hbm_out=1,
    )
    (result,) = call(
        far_kernel,
        [plan, step, *got4, result],
        [(4,) + block],
        [(1,) + block] + [(1,) + state] * 3 + [pltpu.SemaphoreType.DMA] * 2,
        hbm_in=1,
        hbm_out=1,
        aliases={4: 0},
    )
    return result.reshape((1, 1) + result.shape)


def solution(mesh):
    in_specs = (P(None, "bx", "by", None), P(), P())
    out_specs = P("bx", "by", None, None, None, None)
    return jax.shard_map(
        on_device, mesh=mesh, in_specs=in_specs, out_specs=out_specs, check_vma=False
    )
```
